32 devices in a mesh: inner: 4 (over y, x), outer: 8 (over z, core).
Axes of the slice: x: 2, y: 2, z: 4, core: 2. Of those that a mesh axis runs over, the one named last changes fastest.
Arguments:
- query: bfloat16 [8192, 2048], P(('outer', 'inner')), may hold values from -12 to 12
- keys: bfloat16 [8192, 2048], P(('outer', 'inner')), may hold values from -12 to 12
- values: bfloat16 [8192, 2048], P(('outer', 'inner')), may hold values from -6 to 6
- middle_head_shift: int32 [16], replicated, may hold values from 0 to 3
- coarse_head_shift: int32 [16], replicated, may hold values from 0 to 255
Outputs:
- attended: bfloat16 [8192, 2048], P(('outer', 'inner'))
The draws below stay inside these ranges and needn't reach their ends.
All inputs are finite; a program needn't handle non-finite values.
Results may differ from the reference program's by a relative error of at most 0.0045.
Values may be sent and summed in bfloat16 or wider, within the bound.
No kernel may reach another device: no remote copies, remote signals or barrier semaphores. Data moves between devices by JAX's collectives and lax.ppermute only.
A program may use at most 64 MiB of HBM per device.

```python
import jax
import jax.numpy as jnp
from jax import lax

HEAD_COUNT = 16
HEAD_FEATURES = 128
D = 2048
MIDDLE_DILATION = 4
SEG_PAIR = 512
MIDDLE_SEGMENT = 1024
COARSE_DILATION = 256
TOKENS = 8192


def draw_keys(key, part):
    key = jax.random.fold_in(key, 3)
    result = jax.random.truncated_normal(key, -4.0, 4.0, (TOKENS, D), jnp.float32)
    return result.astype(jnp.bfloat16)


def draw_query(key, part):
    key = jax.random.fold_in(key, 7)
    key_extra = jax.random.fold_in(key, 1)
    result = jax.random.truncated_normal(key_extra, -4.0, 4.0, (TOKENS, D), jnp.float32)
    return result.astype(jnp.bfloat16)


def set_ends(values, own_key, smallest, top_value):
    longest = values.shape.index(max(values.shape))
    spots = []
    for shift in (0, 1):
        where = [jax.random.randint(jax.random.fold_in(own_key, axis), (), 0, length) for axis, length in enumerate(values.shape)]
        where[longest] = (where[longest] + shift) % values.shape[longest]
        spots.append(tuple(where))
    return values.at[spots[0]].set(smallest).at[spots[1]].set(top_value)


def shard_levels(own_key, extent, cuts, least, top_value):
    def one(dim, parts):
        steps = jax.random.uniform(jax.random.fold_in(jax.random.fold_in(own_key, 6), dim), (parts,), jnp.float32, least / len(cuts), top_value / len(cuts))
        return jnp.repeat(jnp.exp(steps), extent[dim] // parts).reshape((-1,) + (1,) * (len(extent) - dim - 1))

    loudness = one(*cuts[0])
    for cut in cuts[1:]:
        loudness = loudness * one(*cut)
    return loudness


def gaussian(rng, extent, scale, reach, cuts=(), kind=jnp.bfloat16):
    values = jax.random.normal(rng, extent, jnp.float32) * scale
    if len(cuts) > 0:
        values = shard_levels(rng, extent, cuts, -0.22, 0.18) * values
    return jnp.clip(values, min=-reach, max=reach).astype(kind)


def setup_inputs(seed: int = 0) -> dict:
    streams_of = jax.random.split(jax.random.key(seed), 6)
    return {
        "query": draw_query(jax.random.fold_in(streams_of[5], 71), 0),
        "keys": draw_keys(jax.random.fold_in(streams_of[5], 71), 0),
        "values": gaussian(streams_of[2], (TOKENS, D), 1.0, 6.0, ((0, 32),)),
        "middle_head_shift": set_ends(jax.random.randint(streams_of[3], (HEAD_COUNT,), 0, MIDDLE_DILATION), jax.random.fold_in(streams_of[3], 1), 0, MIDDLE_DILATION - 1).astype(jnp.int32),
        "coarse_head_shift": set_ends(jax.random.randint(streams_of[4], (HEAD_COUNT,), 0, COARSE_DILATION), jax.random.fold_in(streams_of[4], 1), 0, COARSE_DILATION - 1).astype(jnp.int32),
    }


def attend(query_part, key_part, value_part):
    scores = jnp.einsum("qhe,khe->qhk", query_part.astype(jnp.float32), key_part.astype(jnp.float32)) * (HEAD_FEATURES ** -0.5)
    top = jnp.max(scores, axis=-1)
    weights = jnp.exp(scores - top[..., None])
    total = jnp.sum(weights, axis=-1)
    rounded = lax.optimization_barrier(weights.astype(jnp.bfloat16)).astype(jnp.float32)
    summed = jnp.einsum("qhk,khe->qhe", rounded, value_part.astype(jnp.float32))
    return summed / total[..., None], top + jnp.log(total)


def pick_dilated_rows(array, select, group):
    shaped = array.reshape(-1, group, HEAD_COUNT, HEAD_FEATURES)
    kept = jnp.where(select[None, :, :, None], shaped, jnp.zeros_like(shaped))
    return jnp.sum(kept, axis=1).astype(array.dtype)


def reference(query, keys, values, middle_head_shift, coarse_head_shift):
    count = query.shape[0]
    query_per_head = query.reshape(count, HEAD_COUNT, HEAD_FEATURES)
    key_per_head = keys.reshape(count, HEAD_COUNT, HEAD_FEATURES)
    value_per_head = values.reshape(count, HEAD_COUNT, HEAD_FEATURES)

    blocks = (query_per_head.reshape(-1, SEG_PAIR, HEAD_COUNT, HEAD_FEATURES), key_per_head.reshape(-1, SEG_PAIR, HEAD_COUNT, HEAD_FEATURES), value_per_head.reshape(-1, SEG_PAIR, HEAD_COUNT, HEAD_FEATURES))
    out_zero, lse_zero = lax.map(lambda blk: attend(blk[0], blk[1], blk[2]), blocks)
    out_zero = out_zero.reshape(count, HEAD_COUNT, HEAD_FEATURES)
    lse_zero = lse_zero.reshape(count, HEAD_COUNT)

    middle_row_index = jnp.arange(MIDDLE_DILATION)[:, None] == middle_head_shift[None, :]
    rows_per_segment = MIDDLE_SEGMENT // MIDDLE_DILATION
    middle_block_count = tuple(pick_dilated_rows(source_tensor, middle_row_index, MIDDLE_DILATION).reshape(-1, rows_per_segment, HEAD_COUNT, HEAD_FEATURES) for source_tensor in (query_per_head, key_per_head, value_per_head))
    middle_output_sparse, lse_one = lax.map(lambda blk: attend(blk[0], blk[1], blk[2]), middle_block_count)
    middle_output_sparse = middle_output_sparse.reshape(-1, HEAD_COUNT, HEAD_FEATURES)
    lse_one = lse_one.reshape(-1, HEAD_COUNT)
    lse_one_full = jnp.where(middle_row_index[None], lse_one[:, None, :], -jnp.inf).reshape(count, HEAD_COUNT)
    middle_output_dense = jnp.repeat(middle_output_sparse, MIDDLE_DILATION, axis=0)

    coarse_row_index = jnp.arange(COARSE_DILATION)[:, None] == coarse_head_shift[None, :]
    coarse_query_rows = pick_dilated_rows(query_per_head, coarse_row_index, COARSE_DILATION)
    coarse_key_rows = pick_dilated_rows(key_per_head, coarse_row_index, COARSE_DILATION)
    coarse_value_rows = pick_dilated_rows(value_per_head, coarse_row_index, COARSE_DILATION)
    coarse_output_sparse, lse_two = attend(coarse_query_rows, coarse_key_rows, coarse_value_rows)
    lse_two_full = jnp.where(coarse_row_index[None], lse_two[:, None, :], -jnp.inf).reshape(count, HEAD_COUNT)
    coarse_output_dense = jnp.repeat(coarse_output_sparse, COARSE_DILATION, axis=0)

    top = jnp.maximum(jnp.maximum(lse_zero, lse_one_full), lse_two_full)
    weight_zero = jnp.exp(lse_zero - top)
    weight_one = jnp.exp(lse_one_full - top)
    weight_two = jnp.exp(lse_two_full - top)
    mixed = weight_zero[..., None] * out_zero + weight_one[..., None] * middle_output_dense + weight_two[..., None] * coarse_output_dense
    mixed = mixed / (weight_zero + weight_one + weight_two)[..., None]
    return mixed.reshape(count, D).astype(jnp.bfloat16)
```

```python
import functools

import jax
import jax.numpy as jnp
from jax import lax
from jax.experimental import pallas as pl
from jax.experimental.pallas import tpu as pltpu
from jax.sharding import PartitionSpec as P

HEAD_COUNT = 16
HEAD_FEATURES = 128
MIDDLE_DILATION = 4
CHUNKS = (6, 5, 3, 2)
LOG2_E = 1.4426950408889634
MASKED = -1e30


def partner(value, axis, mask):
    pairs = [(source, source ^ mask) for source in range(lax.axis_size(axis))]
    return lax.ppermute(value, axis, pairs)


def member_first(rows, shift):
    members = rows // MIDDLE_DILATION
    row = lax.broadcasted_iota(jnp.int32, (rows, rows), 0)
    token = lax.broadcasted_iota(jnp.int32, (rows, rows), 1)
    slot = row // members
    wanted = MIDDLE_DILATION * (row % members) + (shift + slot) % MIDDLE_DILATION
    return (token == wanted).astype(jnp.float32).astype(jnp.bfloat16)


def fill_orders(order_ref):
    for shift in range(MIDDLE_DILATION):
        order_ref[shift] = member_first(order_ref.shape[1], shift)


def dot(a, b):
    return jnp.dot(a, b, preferred_element_type=jnp.float32)


def head_columns(head):
    return slice(head * HEAD_FEATURES, (head + 1) * HEAD_FEATURES)


def prepare_kernel(chunks, middle_ref, coarse_ref, k_ref, v_ref, members_ref, vm_ref, *rest):
    vr_refs, coarse_out_ref, order_ref = rest[: len(chunks)], rest[-2], rest[-1]
    rows = k_ref.shape[0]
    members = rows // MIDDLE_DILATION
    fill_orders(order_ref)
    head_row = lax.broadcasted_iota(jnp.int32, (HEAD_COUNT, rows), 0)
    token = lax.broadcasted_iota(jnp.int32, (HEAD_COUNT, rows), 1)
    coarse_k = jnp.zeros((HEAD_COUNT, HEAD_FEATURES), jnp.float32)
    coarse_v = jnp.zeros((HEAD_COUNT, HEAD_FEATURES), jnp.float32)
    head = 0
    for chunk, vr_ref in zip(chunks, vr_refs):
        for place in range(chunk):
            columns = head_columns(head)
            order = order_ref[middle_ref[head]]
            k, v = k_ref[:, columns], v_ref[:, columns]
            v_ordered = dot(order, v).astype(jnp.bfloat16)
            k_members = dot(order[:members], k).astype(jnp.bfloat16)
            members_ref[:members, columns] = k_members
            members_ref[members:, columns] = v_ordered[:members]
            vm_ref[:, columns] = v_ordered[:members]
            vr_ref[:, head_columns(place)] = v_ordered[members:]
            chosen = (head_row == head) & (token == coarse_ref[head])
            chosen = chosen.astype(jnp.float32).astype(jnp.bfloat16)
            coarse_k += dot(chosen, k)
            coarse_v += dot(chosen, v)
            head += 1
    coarse_out_ref[0, :HEAD_COUNT] = coarse_k.astype(jnp.bfloat16)
    coarse_out_ref[0, HEAD_COUNT:] = coarse_v.astype(jnp.bfloat16)


def reorder_kernel(middle_ref, k_ref, ordered_ref, members_ref, order_ref):
    members = members_ref.shape[0]
    fill_orders(order_ref)
    for head in range(HEAD_COUNT):
        columns = head_columns(head)
        ordered = dot(order_ref[middle_ref[head]], k_ref[:, columns]).astype(jnp.bfloat16)
        ordered_ref[:, columns] = ordered
        members_ref[:, columns] = ordered[:members]


def attend_kernel(
    first, middle_ref, coarse_ref, q_ref, k_ref, v_ref, kp_ref, vm_ref, vr_ref, cross_ref, diagonal_k_ref,
    diagonal_v_ref, ck_ref, cv_ref, *rest,
):
    out_ref = rest[-1]
    head = first + pl.program_id(0)
    shift, spot = middle_ref[head], coarse_ref[head]
    rows = q_ref.shape[0]
    members = rows // MIDDLE_DILATION
    q = q_ref[...]

    def scores(keys):
        return lax.dot_general(q, keys, (((1,), (1,)), ((), ())), preferred_element_type=jnp.float32)

    row = lax.broadcasted_iota(jnp.int32, (rows, 1), 0)
    row_is_member = row % MIDDLE_DILATION == shift
    own = scores(k_ref[...])
    other = scores(kp_ref[...])
    far_keys = jnp.concatenate([cross_ref[:members], diagonal_k_ref[...]], axis=0)
    far_values = jnp.concatenate([cross_ref[members:], diagonal_v_ref[...]], axis=0)
    far = jnp.where(row_is_member, scores(far_keys), MASKED)
    coarse = jnp.where(row == spot, scores(ck_ref[0]), MASKED)
    top = jnp.max(jnp.maximum(own, other), axis=1, keepdims=True)
    top = jnp.maximum(top, jnp.max(far, axis=1, keepdims=True))
    top = jnp.maximum(top, jnp.max(coarse, axis=1, keepdims=True))
    scale = HEAD_FEATURES ** (-0.5) * LOG2_E

    def weights(part):
        return jnp.exp2((part - top) * scale)

    column = lax.broadcasted_iota(jnp.int32, (1, rows), 1)
    own_twice = row_is_member & (column % MIDDLE_DILATION == shift)
    other_twice = row_is_member & (column < members)
    own, other, far, coarse = weights(own), weights(other), weights(far), weights(coarse)
    own = jnp.where(own_twice, own + own, own)
    other = jnp.where(other_twice, other + other, other)
    total = jnp.sum(own + other, axis=1, keepdims=True)
    total += jnp.sum(far, axis=1, keepdims=True) + jnp.sum(coarse, axis=1, keepdims=True)
    other = other.astype(jnp.bfloat16)
    other_values = jnp.concatenate([vm_ref[...], vr_ref[...]], axis=0)
    summed = dot(own.astype(jnp.bfloat16), v_ref[...])
    summed += dot(other, other_values)
    summed += dot(far.astype(jnp.bfloat16), far_values)
    summed += dot(coarse.astype(jnp.bfloat16), cv_ref[0])
    out_ref[...] = (summed / total).astype(jnp.bfloat16)


def cost(flops, moved, exps=0):
    return pl.CostEstimate(flops=int(flops), bytes_accessed=int(moved), transcendentals=int(exps))


def gather_all(value):
    for axis in ("outer", "inner"):
        size = lax.axis_size(axis)
        if size & (size - 1):
            value = lax.all_gather(value, axis, axis=0, tiled=True)
            continue
        order = [2**j for j in range(size.bit_length() - 1)]
        for mask in order:
            value = jnp.concatenate([value, partner(value, axis, mask)], axis=0)
    return value


def on_device(query, keys, values, middle_head_shift, coarse_head_shift):
    rows, width = query.shape
    members = rows // MIDDLE_DILATION
    bf16 = jnp.bfloat16
    smem = pl.BlockSpec(memory_space=pltpu.SMEM)
    vmem = pl.BlockSpec(memory_space=pltpu.VMEM)
    params = pltpu.CompilerParams(vmem_limit_bytes=32 * 1024 * 1024)
    order_scratch = pltpu.VMEM((MIDDLE_DILATION, rows, rows), bf16)

    other_keys = partner(keys, "inner", 1)
    prepared = pl.pallas_call(
        functools.partial(prepare_kernel, CHUNKS),
        out_shape=[
            jax.ShapeDtypeStruct((2 * members, width), bf16),
            jax.ShapeDtypeStruct((members, width), bf16),
            *[jax.ShapeDtypeStruct((rows - members, c * HEAD_FEATURES), bf16) for c in CHUNKS],
            jax.ShapeDtypeStruct((1, 2 * HEAD_COUNT, HEAD_FEATURES), bf16),
        ],
        in_specs=[smem, smem, vmem, vmem],
        out_specs=[vmem] * (3 + len(CHUNKS)),
        scratch_shapes=[order_scratch],
        compiler_params=params,
        cost_estimate=cost(2 * rows * rows * width * 1.5, 5 * rows * width * 2),
        name="prepare",
    )(middle_head_shift, coarse_head_shift, keys, values)
    own_members, own_vm, own_vr, coarse = prepared[0], prepared[1], prepared[2:-1], prepared[-1]
    coarse = gather_all(coarse)
    devices = coarse.shape[0]
    coarse = jnp.transpose(coarse, (1, 0, 2))
    cross = partner(own_members, "inner", 2)
    other_vm = partner(own_vm, "inner", 1)
    other_vr = [partner(piece, "inner", 1) for piece in own_vr]
    other_ordered, other_km = pl.pallas_call(
        reorder_kernel,
        out_shape=[
            jax.ShapeDtypeStruct((rows, width), bf16),
            jax.ShapeDtypeStruct((members, width), bf16),
        ],
        in_specs=[smem, vmem],
        out_specs=[vmem, vmem],
        scratch_shapes=[order_scratch],
        compiler_params=params,
        cost_estimate=cost(2 * rows * rows * width, 3 * rows * width * 2),
        name="reorder",
    )(middle_head_shift, other_keys)
    diagonal_k = partner(other_km, "inner", 2)
    diagonal_v = partner(other_vm, "inner", 2)

    out = None
    first = 0
    for chunk, vr in zip(CHUNKS, other_vr):

        def column_block(count, first=first):
            return pl.BlockSpec((count, HEAD_FEATURES), lambda i: (0, first + i))

        whole, part = column_block(rows), column_block(members)
        own_chunk = pl.BlockSpec((rows - members, HEAD_FEATURES), lambda i: (0, i))
        coarse_k = pl.BlockSpec((1, devices, HEAD_FEATURES), lambda i, first=first: (first + i, 0, 0))
        coarse_v = pl.BlockSpec((1, devices, HEAD_FEATURES), lambda i, first=first: (HEAD_COUNT + first + i, 0, 0))
        args = [middle_head_shift, coarse_head_shift, query, keys, values, other_ordered, other_vm, vr, cross]
        args += [diagonal_k, diagonal_v, coarse, coarse]
        specs = [smem, smem, whole, whole, whole, whole, part, own_chunk, column_block(2 * members)]
        specs += [part, part, coarse_k, coarse_v]
        aliases = {}
        if out is not None:
            aliases = {len(args): 0}
            args.append(out)
            specs.append(pl.BlockSpec(memory_space=pl.ANY))
        pairs = rows * (2 * rows + 2 * members + devices) * chunk
        out = pl.pallas_call(
            functools.partial(attend_kernel, first),
            out_shape=jax.ShapeDtypeStruct((rows, width), bf16),
            grid=(chunk,),
            in_specs=specs,
            out_specs=whole,
            input_output_aliases=aliases,
            compiler_params=params,
            cost_estimate=cost(4 * pairs * HEAD_FEATURES, 6 * rows * HEAD_FEATURES * 2 * chunk, pairs),
            name="attend",
        )(*args)
        first += chunk
    return out


def solution(mesh):
    placed = (
        P(("outer", "inner"), None),
        P(("outer", "inner"), None),
        P(("outer", "inner"), None),
        P(),
        P(),
    )
    return jax.shard_map(
        on_device,
        mesh=mesh,
        in_specs=placed,
        out_specs=P(("outer", "inner"), None),
        check_vma=False,
    )
```

```python
import functools

import jax
import jax.numpy as jnp
from jax import lax
from jax.experimental import pallas as pl
from jax.experimental.pallas import tpu as pltpu
from jax.sharding import PartitionSpec as P

HEAD_COUNT = 16
HEAD_FEATURES = 128
MIDDLE_DILATION = 4
CHUNKS = (12, 4)
GROUP = 4
LANES = 128
SUBLANES = 16
EXP2_SCALE = HEAD_FEATURES ** (-0.5) * 1.4426950408889634
MASKED = -1e30


def partner(value, axis, mask):
    pairs = [(source, source ^ mask) for source in range(lax.axis_size(axis))]
    return lax.ppermute(value, axis, pairs)


def one_hot(mask):
    return mask.astype(jnp.float32).astype(jnp.bfloat16)


def fill_orders(order_ref):
    rows = order_ref.shape[1]
    members = rows // MIDDLE_DILATION
    group = lax.broadcasted_iota(jnp.int32, (members, rows), 0)
    token = lax.broadcasted_iota(jnp.int32, (members, rows), 1)
    for place in range(MIDDLE_DILATION):
        block = one_hot(token == MIDDLE_DILATION * group + place)
        for shift in range(MIDDLE_DILATION):
            slot = (place - shift) % MIDDLE_DILATION
            order_ref[shift, slot * members : (slot + 1) * members] = block


def dot(a, b):
    return jnp.dot(a, b, preferred_element_type=jnp.float32)


def head_columns(head):
    return slice(head * HEAD_FEATURES, (head + 1) * HEAD_FEATURES)


def prepare_kernel(chunks, middle_ref, coarse_ref, k_ref, v_ref, members_ref, vm_ref, *rest):
    vr_refs, coarse_out_ref, order_ref = rest[: len(chunks)], rest[-2], rest[-1]
    rows = k_ref.shape[0]
    members = rows // MIDDLE_DILATION
    fill_orders(order_ref)
    token = lax.broadcasted_iota(jnp.int32, (SUBLANES, rows), 1)
    first_row = lax.broadcasted_iota(jnp.int32, (SUBLANES, rows), 0) == 0
    second_row = lax.broadcasted_iota(jnp.int32, (SUBLANES, rows), 0) == 1
    head = 0
    for chunk, vr_ref in zip(chunks, vr_refs):
        for place in range(chunk):
            columns = head_columns(head)
            order = order_ref[middle_ref[head]]
            k, v = k_ref[:, columns], v_ref[:, columns]
            v_ordered = dot(order, v).astype(jnp.bfloat16)
            k_members = dot(order[:members], k).astype(jnp.bfloat16)
            members_ref[:members, columns] = k_members
            members_ref[members:, columns] = v_ordered[:members]
            vm_ref[:, columns] = v_ordered[:members]
            vr_ref[:, head_columns(place)] = v_ordered[members:]
            chosen = token == coarse_ref[head]
            picked = dot(one_hot(chosen & first_row), k) + dot(one_hot(chosen & second_row), v)
            coarse_out_ref[:, columns] = picked[:2].astype(jnp.bfloat16)
            head += 1


def reorder_kernel(middle_ref, k_ref, ordered_ref, members_ref, order_ref):
    members = members_ref.shape[0]
    fill_orders(order_ref)
    for head in range(HEAD_COUNT):
        columns = head_columns(head)
        ordered = dot(order_ref[middle_ref[head]], k_ref[:, columns]).astype(jnp.bfloat16)
        ordered_ref[:, columns] = ordered
        members_ref[:, columns] = ordered[:members]


def dot_keys(q, keys):
    return lax.dot_general(q, keys, (((1,), (1,)), ((), ())), preferred_element_type=jnp.float32)


def side_by_side(columns):
    rows = columns[0].shape[0]
    lane = lax.broadcasted_iota(jnp.int32, (rows, LANES), 1)
    result = jnp.zeros((rows, LANES), jnp.float32)
    for place, column in enumerate(columns):
        result = jnp.where(lane == place, column, result)
    return result


def member_rows(rows, shift):
    row = lax.broadcasted_iota(jnp.int32, (rows, 1), 0)
    return (row & (MIDDLE_DILATION - 1)) == shift


def lane_tiles(part):
    return [part[:, i : i + LANES] for i in range(0, part.shape[1], LANES)]


def weights(part, top):
    return jnp.exp2((part - top) * EXP2_SCALE)


def first_kernel(first, middle_ref, q_ref, k_ref, v_ref, kp_ref, own_ref, other_ref, state_ref):
    rows = q_ref.shape[0]
    members = rows // MIDDLE_DILATION
    column = lax.broadcasted_iota(jnp.int32, (1, rows), 1)
    tops, totals = [], []
    for place in range(GROUP):
        columns = head_columns(place)
        shift = middle_ref[first + GROUP * pl.program_id(0) + place]
        q = q_ref[:, columns]
        own = dot_keys(q, k_ref[:, columns])
        other = dot_keys(q, kp_ref[:, columns])
        top = functools.reduce(jnp.maximum, lane_tiles(own) + lane_tiles(other))
        top = jnp.max(top, axis=1, keepdims=True)
        row_is_member = member_rows(rows, shift)
        own, other = weights(own, top), weights(other, top)
        own_member = row_is_member & ((column & (MIDDLE_DILATION - 1)) == shift)
        own = jnp.where(own_member, own + own, own)
        twice = other[:, :LANES]
        twice = jnp.where(row_is_member & (column[:, :LANES] < members), twice + twice, twice)
        other = jnp.concatenate([twice, other[:, LANES:]], axis=1)
        total = functools.reduce(jnp.add, lane_tiles(own) + lane_tiles(other))
        tops.append(top)
        totals.append(jnp.sum(total, axis=1, keepdims=True))
        own_ref[:, columns] = dot(own.astype(jnp.bfloat16), v_ref[:, columns])
        other_ref[place] = other.astype(jnp.bfloat16)
    state_ref[...] = side_by_side(tops + totals)


def extra_kernel(
    middle_ref, coarse_ref, q_ref, own_ref, state_ref, cross_ref, diagonal_k_ref, diagonal_v_ref, coarse_kv_ref,
    sum_ref, share_ref,
):
    rows = q_ref.shape[0]
    members = rows // MIDDLE_DILATION
    row = lax.broadcasted_iota(jnp.int32, (rows, 1), 0)
    state = state_ref[...]
    devices = coarse_kv_ref.shape[0] // 2
    shares = []
    for place in range(GROUP):
        columns = head_columns(place)
        head = GROUP * pl.program_id(0) + place
        q = q_ref[:, columns]
        far_keys = jnp.concatenate([cross_ref[:members, columns], diagonal_k_ref[:, columns]], axis=0)
        far_values = jnp.concatenate([cross_ref[members:, columns], diagonal_v_ref[:, columns]], axis=0)
        far = jnp.where(member_rows(rows, middle_ref[head]), dot_keys(q, far_keys), MASKED)
        coarse = jnp.where(row == coarse_ref[head], dot_keys(q, coarse_kv_ref[:devices, columns]), MASKED)
        before = state[:, place : place + 1]
        top = jnp.maximum(before, jnp.max(far, axis=1, keepdims=True))
        top = jnp.maximum(top, jnp.max(coarse, axis=1, keepdims=True))
        far, coarse = weights(far, top), weights(coarse, top)
        kept = weights(before, top)
        total = kept * state[:, GROUP + place : GROUP + place + 1]
        total += jnp.sum(far, axis=1, keepdims=True) + jnp.sum(coarse, axis=1, keepdims=True)
        inverse = 1.0 / total
        share = kept * inverse
        summed = dot(far.astype(jnp.bfloat16), far_values) + dot(coarse.astype(jnp.bfloat16), coarse_kv_ref[devices:, columns])
        sum_ref[:, columns] = summed * inverse + own_ref[:, columns] * share
        shares.append(share)
    share_ref[...] = side_by_side(shares)


def finish_kernel(count, lane, sum_ref, share_ref, other_ref, vm_ref, vr_ref, *rest):
    out_ref = rest[-1]
    for place in range(count):
        columns = head_columns(place)
        values = jnp.concatenate([vm_ref[:, columns], vr_ref[:, columns]], axis=0)
        share = share_ref[:, lane + place : lane + place + 1]
        result = sum_ref[:, columns] + share * dot(other_ref[place], values)
        out_ref[:, columns] = result.astype(jnp.bfloat16)


def cost():
    return pl.CostEstimate(flops=0, bytes_accessed=0, transcendentals=0)


def gather_all(value, axis):
    size = lax.axis_size(axis)
    if size & (size - 1):
        return lax.all_gather(value, axis, axis=0, tiled=True)
    for j in range(size.bit_length() - 1):
        value = jnp.concatenate([value, partner(value, axis, 2**j)], axis=0)
    return value


def on_device(query, keys, values, middle_head_shift, coarse_head_shift):
    rows, width = query.shape
    members = rows // MIDDLE_DILATION
    bf16 = jnp.bfloat16
    smem = pl.BlockSpec(memory_space=pltpu.SMEM)
    vmem = pl.BlockSpec(memory_space=pltpu.VMEM)
    params = pltpu.CompilerParams(vmem_limit_bytes=32 * 1024 * 1024)
    order_scratch = pltpu.VMEM((MIDDLE_DILATION, rows, rows), bf16)

    other_keys = partner(keys, "inner", 1)
    prepared = pl.pallas_call(
        functools.partial(prepare_kernel, CHUNKS),
        out_shape=[
            jax.ShapeDtypeStruct((2 * members, width), bf16),
            jax.ShapeDtypeStruct((members, width), bf16),
            *[jax.ShapeDtypeStruct((rows - members, c * HEAD_FEATURES), bf16) for c in CHUNKS],
            jax.ShapeDtypeStruct((2, width), bf16),
        ],
        in_specs=[smem, smem, vmem, vmem],
        out_specs=[vmem] * (3 + len(CHUNKS)),
        scratch_shapes=[order_scratch],
        compiler_params=params,
        cost_estimate=cost(),
        name="prepare",
    )(middle_head_shift, coarse_head_shift, keys, values)
    own_members, own_vm, own_vr, coarse = prepared[0], prepared[1], prepared[2:-1], prepared[-1]
    cross = partner(own_members, "inner", 2)
    near = gather_all(coarse, "outer")
    near_cross = partner(near, "inner", 2)
    sent = jnp.concatenate([own_vm, near], axis=0)
    cross, own_vr = lax.optimization_barrier((cross, own_vr))
    other_vm = partner(sent, "inner", 1)
    other_vr = [partner(piece, "inner", 1) for piece in own_vr]
    other_ordered, other_km = pl.pallas_call(
        reorder_kernel,
        out_shape=[
            jax.ShapeDtypeStruct((rows, width), bf16),
            jax.ShapeDtypeStruct((members, width), bf16),
        ],
        in_specs=[smem, vmem],
        out_specs=[vmem, vmem],
        scratch_shapes=[order_scratch],
        compiler_params=params,
        cost_estimate=cost(),
        name="reorder",
    )(middle_head_shift, other_keys)
    diagonal_k = partner(other_km, "inner", 2)
    diagonal_v = partner(lax.optimization_barrier((other_vm, other_ordered))[0], "inner", 2)
    coarse = jnp.concatenate([near, near_cross, other_vm[members:], diagonal_v[members:]], axis=0)
    devices = coarse.shape[0] // 2
    coarse = coarse.reshape(devices, 2, width).transpose(1, 0, 2).reshape(2 * devices, width)

    def columns_of(count, heads=GROUP, first=0):
        return pl.BlockSpec((count, heads * HEAD_FEATURES), lambda i: (0, first // heads + i))

    groups = HEAD_COUNT // GROUP
    whole, part = columns_of(rows), columns_of(members)
    lanes = pl.BlockSpec((rows, LANES), lambda i: (0, i))
    per_head = pl.BlockSpec((GROUP, rows, rows), lambda i: (i, 0, 0))
    own_sum, other_weights, state = pl.pallas_call(
        functools.partial(first_kernel, 0),
        out_shape=[
            jax.ShapeDtypeStruct((rows, width), jnp.float32),
            jax.ShapeDtypeStruct((HEAD_COUNT, rows, rows), bf16),
            jax.ShapeDtypeStruct((rows, groups * LANES), jnp.float32),
        ],
        grid=(groups,),
        in_specs=[smem, whole, whole, whole, whole],
        out_specs=[whole, per_head, lanes],
        compiler_params=params,
        cost_estimate=cost(),
        name="first",
    )(middle_head_shift, query, keys, values, other_ordered)

    all_sum, share = pl.pallas_call(
        extra_kernel,
        out_shape=[
            jax.ShapeDtypeStruct((rows, width), jnp.float32),
            jax.ShapeDtypeStruct((rows, groups * LANES), jnp.float32),
        ],
        grid=(groups,),
        in_specs=[smem, smem, whole, whole, lanes, columns_of(2 * members), part, part, columns_of(2 * devices)],
        out_specs=[whole, lanes],
        compiler_params=params,
        cost_estimate=cost(),
        name="extra",
    )(
        middle_head_shift, coarse_head_shift, query, own_sum, state, cross, diagonal_k, diagonal_v, coarse
    )

    out = None
    first = 0
    for chunk, vr in zip(CHUNKS, other_vr):
        heads = min(GROUP, chunk)
        lane = first % GROUP
        block = columns_of(rows, heads, first)
        args = [all_sum, share, other_weights, other_vm, vr]
        specs = [
            block,
            pl.BlockSpec((rows, LANES), lambda i, first=first: (0, first // GROUP + i)),
            pl.BlockSpec((heads, rows, rows), lambda i, first=first, heads=heads: (first // heads + i, 0, 0)),
            columns_of(members, heads, first),
            columns_of(rows - members, heads),
        ]
        aliases = {}
        if out is not None:
            aliases = {len(args): 0}
            args.append(out)
            specs.append(pl.BlockSpec(memory_space=pl.ANY))
        out = pl.pallas_call(
            functools.partial(finish_kernel, heads, lane),
            out_shape=jax.ShapeDtypeStruct((rows, width), bf16),
            grid=(chunk // heads,),
            in_specs=specs,
            out_specs=block,
            input_output_aliases=aliases,
            compiler_params=params,
            cost_estimate=cost(),
            name="finish",
        )(*args)
        first += chunk
    return out


def solution(mesh):
    placed = (
        P(("outer", "inner"), None),
        P(("outer", "inner"), None),
        P(("outer", "inner"), None),
        P(),
        P(),
    )
    return jax.shard_map(
        on_device,
        mesh=mesh,
        in_specs=placed,
        out_specs=P(("outer", "inner"), None),
        check_vma=False,
    )
```

```python
import functools

import jax
import jax.numpy as jnp
from jax import lax
from jax.experimental import pallas as pl
from jax.experimental.pallas import tpu as pltpu
from jax.sharding import PartitionSpec as P

HEAD_COUNT = 16
HEAD_FEATURES = 128
MIDDLE_DILATION = 4
CHUNKS = (12, 4)
GROUP = 4
LANES = 128
SUBLANES = 16
EXP2_SCALE = HEAD_FEATURES ** (-0.5) * 1.4426950408889634
MASKED = -1e30


def partner(value, axis, mask):
    pairs = [(source, source ^ mask) for source in range(lax.axis_size(axis))]
    return lax.ppermute(value, axis, pairs)


def one_hot(mask):
    return mask.astype(jnp.float32).astype(jnp.bfloat16)


def fill_orders(order_ref):
    rows = order_ref.shape[1]
    members = rows // MIDDLE_DILATION
    group = lax.broadcasted_iota(jnp.int32, (members, rows), 0)
    token = lax.broadcasted_iota(jnp.int32, (members, rows), 1)
    for place in range(MIDDLE_DILATION):
        block = one_hot(token == MIDDLE_DILATION * group + place)
        for shift in range(MIDDLE_DILATION):
            slot = (place - shift) % MIDDLE_DILATION
            order_ref[shift, slot * members : (slot + 1) * members] = block


def dot(a, b):
    return jnp.dot(a, b, preferred_element_type=jnp.float32)


def head_columns(head):
    return slice(head * HEAD_FEATURES, (head + 1) * HEAD_FEATURES)


def prepare_kernel(chunks, middle_ref, coarse_ref, k_ref, v_ref, members_ref, vm_ref, *rest):
    vr_refs, coarse_out_ref, order_ref = rest[: len(chunks)], rest[-2], rest[-1]
    rows = k_ref.shape[0]
    members = rows // MIDDLE_DILATION
    fill_orders(order_ref)
    token = lax.broadcasted_iota(jnp.int32, (SUBLANES, rows), 1)
    first_row = lax.broadcasted_iota(jnp.int32, (SUBLANES, rows), 0) == 0
    second_row = lax.broadcasted_iota(jnp.int32, (SUBLANES, rows), 0) == 1
    head = 0
    for chunk, vr_ref in zip(chunks, vr_refs):
        for place in range(chunk):
            columns = head_columns(head)
            order = order_ref[middle_ref[head]]
            k, v = k_ref[:, columns], v_ref[:, columns]
            v_ordered = dot(order, v).astype(jnp.bfloat16)
            k_members = dot(order[:members], k).astype(jnp.bfloat16)
            members_ref[:members, columns] = k_members
            members_ref[members:, columns] = v_ordered[:members]
            vm_ref[:members, columns] = v_ordered[:members]
            vr_ref[:, head_columns(place)] = v_ordered[members:]
            chosen = token == coarse_ref[head]
            picked = dot(one_hot(chosen & first_row), k) + dot(one_hot(chosen & second_row), v)
            coarse_out_ref[:, columns] = picked[:2].astype(jnp.bfloat16)
            head += 1


def append_kernel(near_ref, vm_ref, out_ref, semaphore):
    rows = near_ref.shape[0]
    first = out_ref.shape[0] - rows
    copy = pltpu.make_async_copy(near_ref, out_ref.at[pl.ds(first, rows)], semaphore)
    copy.start()
    copy.wait()


def reorder_kernel(middle_ref, k_ref, near_ref, ordered_ref, members_ref, order_ref):
    members = k_ref.shape[0] // MIDDLE_DILATION
    fill_orders(order_ref)
    members_ref[members:] = near_ref[...]
    for head in range(HEAD_COUNT):
        columns = head_columns(head)
        ordered = dot(order_ref[middle_ref[head]], k_ref[:, columns]).astype(jnp.bfloat16)
        ordered_ref[:, columns] = ordered
        members_ref[:members, columns] = ordered[:members]


def dot_keys(q, keys):
    return lax.dot_general(q, keys, (((1,), (1,)), ((), ())), preferred_element_type=jnp.float32)


def dot_rows(a, b):
    return lax.dot_general(a, b, (((0,), (0,)), ((), ())), preferred_element_type=jnp.float32)


def side_by_side(columns):
    rows = columns[0].shape[0]
    lane = lax.broadcasted_iota(jnp.int32, (rows, LANES), 1)
    result = jnp.zeros((rows, LANES), jnp.float32)
    for place, column in enumerate(columns):
        result = jnp.where(lane == place, column, result)
    return result


def member_rows(rows, shift):
    row = lax.broadcasted_iota(jnp.int32, (rows, 1), 0)
    return (row & (MIDDLE_DILATION - 1)) == shift


def lane_tiles(part):
    return [part[:, i : i + LANES] for i in range(0, part.shape[1], LANES)]


def weights(part, top):
    return jnp.exp2((part - top) * EXP2_SCALE)


def first_kernel(first, middle_ref, q_ref, k_ref, v_ref, kp_ref, own_ref, other_ref, state_ref):
    rows = q_ref.shape[0]
    members = rows // MIDDLE_DILATION
    column = lax.broadcasted_iota(jnp.int32, (1, rows), 1)
    tops, totals = [], []
    for place in range(GROUP):
        columns = head_columns(place)
        shift = middle_ref[first + GROUP * pl.program_id(0) + place]
        q = q_ref[:, columns]
        own = dot_keys(q, k_ref[:, columns])
        other = dot_keys(q, kp_ref[:, columns])
        top = functools.reduce(jnp.maximum, lane_tiles(own) + lane_tiles(other))
        top = jnp.max(top, axis=1, keepdims=True)
        row_is_member = member_rows(rows, shift)
        own, other = weights(own, top), weights(other, top)
        own_member = row_is_member & ((column & (MIDDLE_DILATION - 1)) == shift)
        own = jnp.where(own_member, own + own, own)
        twice = other[:, :LANES]
        twice = jnp.where(row_is_member & (column[:, :LANES] < members), twice + twice, twice)
        other = jnp.concatenate([twice, other[:, LANES:]], axis=1)
        total = functools.reduce(jnp.add, lane_tiles(own) + lane_tiles(other))
        tops.append(top)
        totals.append(jnp.sum(total, axis=1, keepdims=True))
        own_ref[:, columns] = dot(own.astype(jnp.bfloat16), v_ref[:, columns])
        other_ref[place] = other.astype(jnp.bfloat16)
    state_ref[...] = side_by_side(tops + totals)


def extra_kernel(
    middle_ref, coarse_ref, q_ref, state_ref, cross_ref, diagonal_k_ref, diagonal_v_ref, near_ref, other_ref,
    sum_ref, share_ref,
):
    rows = q_ref.shape[0]
    members = rows // MIDDLE_DILATION
    token = lax.broadcasted_iota(jnp.int32, (1, rows), 1)
    state = state_ref[...].T
    shares = []
    for place in range(GROUP):
        columns = head_columns(place)
        head = GROUP * pl.program_id(0) + place
        q = q_ref[:, columns]
        far_keys = jnp.concatenate([cross_ref[:members, columns], diagonal_k_ref[:members, columns]], axis=0)
        far_values = jnp.concatenate([cross_ref[members:, columns], diagonal_v_ref[:members, columns]], axis=0)
        pieces = [near_ref[:, columns]] + [
            ref[members:, columns] for ref in (other_ref, diagonal_k_ref, diagonal_v_ref)
        ]
        pairs = jnp.concatenate(pieces, axis=0)
        is_key = (lax.broadcasted_iota(jnp.int32, (pairs.shape[0], 1), 0) & 1) == 0
        row_is_member = (token & (MIDDLE_DILATION - 1)) == middle_ref[head]
        far = jnp.where(row_is_member, dot_keys(far_keys, q), MASKED)
        coarse = jnp.where(is_key & (token == coarse_ref[head]), dot_keys(pairs, q), MASKED)
        before = state[place : place + 1]
        top = jnp.maximum(before, jnp.max(far, axis=0, keepdims=True))
        top = jnp.maximum(top, jnp.max(coarse, axis=0, keepdims=True))
        far, coarse = weights(far, top), weights(coarse, top)
        kept = weights(before, top)
        total = kept * state[GROUP + place : GROUP + place + 1]
        total += jnp.sum(far, axis=0, keepdims=True) + jnp.sum(coarse, axis=0, keepdims=True)
        inverse = 1.0 / total
        coarse = pltpu.roll(coarse, 1, 0)
        summed = dot_rows(far_values, far.astype(jnp.bfloat16)) + dot_rows(pairs, coarse.astype(jnp.bfloat16))
        sum_ref[:, columns] = (summed * inverse).T
        shares.append(kept * inverse)
    shares.append(jnp.zeros((SUBLANES - GROUP, rows), jnp.float32))
    share_ref[:, :SUBLANES] = jnp.concatenate(shares, axis=0).T


def finish_kernel(count, lane, sum_ref, share_ref, own_ref, other_ref, vm_ref, vr_ref, *rest):
    out_ref = rest[-1]
    for place in range(count):
        columns = head_columns(place)
        values = jnp.concatenate([vm_ref[:, columns], vr_ref[:, columns]], axis=0)
        share = share_ref[:, lane + place : lane + place + 1]
        result = own_ref[:, columns] + dot(other_ref[place], values)
        out_ref[:, columns] = (sum_ref[:, columns] + share * result).astype(jnp.bfloat16)


def cost():
    return pl.CostEstimate(flops=0, bytes_accessed=0, transcendentals=0)


def gather_all(value, axis):
    size = lax.axis_size(axis)
    if size & (size - 1):
        return lax.all_gather(value, axis, axis=0, tiled=True)
    bits = [2**j for j in range(size.bit_length() - 1)]
    for step in [bits[:1]] + [bits[j : j + 2] for j in range(1, len(bits), 2)]:
        masks = step + [sum(step)] if len(step) == 2 else step
        value = jnp.concatenate([value] + [partner(value, axis, mask) for mask in masks], axis=0)
    return value


def on_device(query, keys, values, middle_head_shift, coarse_head_shift):
    rows, width = query.shape
    members = rows // MIDDLE_DILATION
    near_rows = 2 * lax.axis_size("outer")
    bf16 = jnp.bfloat16
    smem = pl.BlockSpec(memory_space=pltpu.SMEM)
    vmem = pl.BlockSpec(memory_space=pltpu.VMEM)
    anywhere = pl.BlockSpec(memory_space=pl.ANY)
    params = pltpu.CompilerParams(vmem_limit_bytes=24 * 1024 * 1024)
    order_scratch = pltpu.VMEM((MIDDLE_DILATION, rows, rows), bf16)

    def columns_of(count, heads=GROUP, first=0):
        return pl.BlockSpec((count, heads * HEAD_FEATURES), lambda i: (0, first // heads + i))

    def call(kernel, name, **options):
        return pl.pallas_call(kernel, name=name, compiler_params=params, cost_estimate=cost(), **options)

    other_keys = partner(keys, "inner", 1)
    prepared = call(
        functools.partial(prepare_kernel, CHUNKS),
        "prepare",
        out_shape=[
            pltpu.HBM((2 * members, width), bf16),
            pltpu.HBM((members + near_rows, width), bf16),
            *[pltpu.HBM((rows - members, c * HEAD_FEATURES), bf16) for c in CHUNKS],
            jax.ShapeDtypeStruct((2, width), bf16),
        ],
        in_specs=[smem, smem, vmem, vmem],
        out_specs=[vmem] * (3 + len(CHUNKS)),
        scratch_shapes=[order_scratch],
    )(middle_head_shift, coarse_head_shift, keys, values)
    own_members, own_vm, own_vr, coarse = prepared[0], prepared[1], prepared[2:-1], prepared[-1]
    cross = partner(own_members, "inner", 2)
    near = gather_all(coarse, "outer")
    own_vm = call(
        append_kernel,
        "append",
        out_shape=pltpu.HBM(own_vm.shape, bf16),
        in_specs=[vmem, anywhere],
        out_specs=anywhere,
        input_output_aliases={1: 0},
        scratch_shapes=[pltpu.SemaphoreType.DMA],
    )(near, own_vm)
    other_vm = partner(own_vm, "inner", 1)
    cross, own_vr = lax.optimization_barrier((cross, own_vr))
    other_vr = [partner(piece, "inner", 1) for piece in own_vr]
    other_ordered, other_km = call(
        reorder_kernel,
        "reorder",
        out_shape=[pltpu.HBM((rows, width), bf16), pltpu.HBM((members + near_rows, width), bf16)],
        in_specs=[smem, vmem, vmem],
        out_specs=[vmem, vmem],
        scratch_shapes=[order_scratch],
    )(middle_head_shift, other_keys, near)
    diagonal_k = partner(other_km, "inner", 2)
    diagonal_v = partner(lax.optimization_barrier((other_vm, other_ordered))[0], "inner", 2)

    groups = HEAD_COUNT // GROUP
    whole, with_near = columns_of(rows), columns_of(members + near_rows)
    lanes = pl.BlockSpec((rows, LANES), lambda i: (0, i))
    own_sum, other_weights, state = call(
        functools.partial(first_kernel, 0),
        "first",
        out_shape=[
            pltpu.HBM((rows, width), jnp.float32),
            pltpu.HBM((HEAD_COUNT, rows, rows), bf16),
            pltpu.HBM((rows, groups * LANES), jnp.float32),
        ],
        grid=(groups,),
        in_specs=[smem, whole, whole, whole, whole],
        out_specs=[whole, pl.BlockSpec((GROUP, rows, rows), lambda i: (i, 0, 0)), lanes],
    )(middle_head_shift, query, keys, values, other_ordered)
    extra_sum, share = call(
        extra_kernel,
        "extra",
        out_shape=[pltpu.HBM((rows, width), jnp.float32), pltpu.HBM((rows, groups * LANES), jnp.float32)],
        grid=(groups,),
        in_specs=[
            smem, smem, whole, lanes, columns_of(2 * members), with_near, with_near, columns_of(near_rows), with_near
        ],
        out_specs=[whole, lanes],
    )(middle_head_shift, coarse_head_shift, query, state, cross, diagonal_k, diagonal_v, near, other_vm)

    out = None
    first = 0
    for chunk, vr in zip(CHUNKS, other_vr):
        heads = min(GROUP, chunk)
        block = columns_of(rows, heads, first)
        args = [extra_sum, share, own_sum, other_weights, other_vm, vr]
        specs = [
            block,
            pl.BlockSpec((rows, LANES), lambda i, first=first: (0, first // GROUP + i)),
            block,
            pl.BlockSpec((heads, rows, rows), lambda i, first=first, heads=heads: (first // heads + i, 0, 0)),
            columns_of(members, heads, first),
            columns_of(rows - members, heads),
        ]
        aliases = {}
        if out is not None:
            aliases = {len(args): 0}
            args.append(out)
            specs.append(anywhere)
        out = call(
            functools.partial(finish_kernel, heads, first % GROUP),
            "finish",
            out_shape=jax.ShapeDtypeStruct((rows, width), bf16),
            grid=(chunk // heads,),
            in_specs=specs,
            out_specs=block,
            input_output_aliases=aliases,
        )(*args)
        first += chunk
    return out


def solution(mesh):
    placed = (
        P(("outer", "inner"), None),
        P(("outer", "inner"), None),
        P(("outer", "inner"), None),
        P(),
        P(),
    )
    return jax.shard_map(
        on_device,
        mesh=mesh,
        in_specs=placed,
        out_specs=P(("outer", "inner"), None),
        check_vma=False,
    )
```

```python
import functools

import jax
import jax.numpy as jnp
from jax import lax
from jax.experimental import pallas as pl
from jax.experimental.pallas import tpu as pltpu
from jax.sharding import PartitionSpec as P

HEAD_COUNT = 16
HEAD_FEATURES = 128
MIDDLE_DILATION = 4
CHUNKS = (12, 4)
GROUP = 4
LANES = 128
SUBLANES = 16
EXP2_SCALE = HEAD_FEATURES ** (-0.5) * 1.4426950408889634
MASKED = -1e30


def partner(value, axis, mask):
    pairs = [(source, source ^ mask) for source in range(lax.axis_size(axis))]
    return lax.ppermute(value, axis, pairs)


def one_hot(mask):
    return mask.astype(jnp.float32).astype(jnp.bfloat16)


def fill_orders(order_ref):
    rows = order_ref.shape[1]
    members = rows // MIDDLE_DILATION
    group = lax.broadcasted_iota(jnp.int32, (members, rows), 0)
    token = lax.broadcasted_iota(jnp.int32, (members, rows), 1)
    for place in range(MIDDLE_DILATION):
        block = one_hot(token == MIDDLE_DILATION * group + place)
        for shift in range(MIDDLE_DILATION):
            slot = (place - shift) % MIDDLE_DILATION
            order_ref[shift, slot * members : (slot + 1) * members] = block


def dot(a, b):
    return jnp.dot(a, b, preferred_element_type=jnp.float32)


def head_columns(head):
    return slice(head * HEAD_FEATURES, (head + 1) * HEAD_FEATURES)


def prepare_kernel(chunks, middle_ref, coarse_ref, k_ref, v_ref, members_ref, vm_ref, *rest):
    vr_refs, coarse_out_ref, order_ref = rest[: len(chunks)], rest[-2], rest[-1]
    rows = k_ref.shape[0]
    members = rows // MIDDLE_DILATION
    fill_orders(order_ref)
    token = lax.broadcasted_iota(jnp.int32, (SUBLANES, rows), 1)
    first_row = lax.broadcasted_iota(jnp.int32, (SUBLANES, rows), 0) == 0
    second_row = lax.broadcasted_iota(jnp.int32, (SUBLANES, rows), 0) == 1
    head = 0
    for chunk, vr_ref in zip(chunks, vr_refs):
        for place in range(chunk):
            columns = head_columns(head)
            order = order_ref[middle_ref[head]]
            k, v = k_ref[:, columns], v_ref[:, columns]
            v_ordered = dot(order, v).astype(jnp.bfloat16)
            k_members = dot(order[:members], k).astype(jnp.bfloat16)
            members_ref[:members, columns] = k_members
            members_ref[members:, columns] = v_ordered[:members]
            vm_ref[:members, columns] = v_ordered[:members]
            vr_ref[:, head_columns(place)] = v_ordered[members:]
            chosen = token == coarse_ref[head]
            picked = dot(one_hot(chosen & first_row), k) + dot(one_hot(chosen & second_row), v)
            coarse_out_ref[:, columns] = picked[:2].astype(jnp.bfloat16)
            head += 1


def append_kernel(near_ref, vm_ref, out_ref, semaphore):
    rows = near_ref.shape[0]
    first = out_ref.shape[0] - rows
    copy = pltpu.make_async_copy(near_ref, out_ref.at[pl.ds(first, rows)], semaphore)
    copy.start()
    copy.wait()


def pick_kernel(middle_ref, k_ref, near_ref, members_ref):
    rows = k_ref.shape[0]
    members = rows // MIDDLE_DILATION
    members_ref[members:] = near_ref[...]
    group = lax.broadcasted_iota(jnp.int32, (members, rows), 0)
    token = lax.broadcasted_iota(jnp.int32, (members, rows), 1)
    offset = token - MIDDLE_DILATION * group
    for head in range(HEAD_COUNT):
        columns = head_columns(head)
        chosen = one_hot(offset == middle_ref[head])
        members_ref[:members, columns] = dot(chosen, k_ref[:, columns]).astype(jnp.bfloat16)


def dot_keys(q, keys):
    return lax.dot_general(q, keys, (((1,), (1,)), ((), ())), preferred_element_type=jnp.float32)


def dot_rows(a, b):
    return lax.dot_general(a, b, (((0,), (0,)), ((), ())), preferred_element_type=jnp.float32)


def side_by_side(columns):
    rows = columns[0].shape[0]
    lane = lax.broadcasted_iota(jnp.int32, (rows, LANES), 1)
    result = jnp.zeros((rows, LANES), jnp.float32)
    for place, column in enumerate(columns):
        result = jnp.where(lane == place, column, result)
    return result


def member_rows(rows, shift):
    row = lax.broadcasted_iota(jnp.int32, (rows, 1), 0)
    return (row & (MIDDLE_DILATION - 1)) == shift


def lane_tiles(part):
    return [part[:, i : i + LANES] for i in range(0, part.shape[1], LANES)]


def weights(part, top):
    return jnp.exp2((part - top) * EXP2_SCALE)


def first_kernel(first, middle_ref, q_ref, k_ref, v_ref, kp_ref, *rest):
    own_ref, other_ref, state_ref, order_ref = rest[-4:]

    @pl.when(pl.program_id(0) == 0)
    def _():
        fill_orders(order_ref)

    rows = q_ref.shape[0]
    members = rows // MIDDLE_DILATION
    column = lax.broadcasted_iota(jnp.int32, (1, rows), 1)
    tops, totals = [], []
    for place in range(GROUP):
        columns = head_columns(place)
        shift = middle_ref[first + GROUP * pl.program_id(0) + place]
        q = q_ref[:, columns]
        own = dot_keys(q, k_ref[:, columns])
        other_keys = dot(order_ref[shift], kp_ref[:, columns]).astype(jnp.bfloat16)
        other = dot_keys(q, other_keys)
        top = functools.reduce(jnp.maximum, lane_tiles(own) + lane_tiles(other))
        top = jnp.max(top, axis=1, keepdims=True)
        row_is_member = member_rows(rows, shift)
        own, other = weights(own, top), weights(other, top)
        own_member = row_is_member & ((column & (MIDDLE_DILATION - 1)) == shift)
        own = jnp.where(own_member, own + own, own)
        twice = other[:, :LANES]
        twice = jnp.where(row_is_member & (column[:, :LANES] < members), twice + twice, twice)
        other = jnp.concatenate([twice, other[:, LANES:]], axis=1)
        total = functools.reduce(jnp.add, lane_tiles(own) + lane_tiles(other))
        tops.append(top)
        totals.append(jnp.sum(total, axis=1, keepdims=True))
        own_ref[:, columns] = dot(own.astype(jnp.bfloat16), v_ref[:, columns])
        other_ref[place] = other.astype(jnp.bfloat16)
    state_ref[...] = side_by_side(tops + totals)


def extra_kernel(
    middle_ref, coarse_ref, q_ref, state_ref, cross_ref, diagonal_k_ref, diagonal_v_ref, near_ref, other_ref,
    sum_ref, share_ref,
):
    rows = q_ref.shape[0]
    members = rows // MIDDLE_DILATION
    token = lax.broadcasted_iota(jnp.int32, (1, rows), 1)
    state = state_ref[...].T
    shares = []
    for place in range(GROUP):
        columns = head_columns(place)
        head = GROUP * pl.program_id(0) + place
        q = q_ref[:, columns]
        far_keys = jnp.concatenate([cross_ref[:members, columns], diagonal_k_ref[:members, columns]], axis=0)
        far_values = jnp.concatenate([cross_ref[members:, columns], diagonal_v_ref[:members, columns]], axis=0)
        pieces = [near_ref[:, columns]] + [
            ref[members:, columns] for ref in (other_ref, diagonal_k_ref, diagonal_v_ref)
        ]
        pairs = jnp.concatenate(pieces, axis=0)
        is_key = (lax.broadcasted_iota(jnp.int32, (pairs.shape[0], 1), 0) & 1) == 0
        row_is_member = (token & (MIDDLE_DILATION - 1)) == middle_ref[head]
        far = jnp.where(row_is_member, dot_keys(far_keys, q), MASKED)
        coarse = jnp.where(is_key & (token == coarse_ref[head]), dot_keys(pairs, q), MASKED)
        before = state[place : place + 1]
        top = jnp.maximum(before, jnp.max(far, axis=0, keepdims=True))
        top = jnp.maximum(top, jnp.max(coarse, axis=0, keepdims=True))
        far, coarse = weights(far, top), weights(coarse, top)
        kept = weights(before, top)
        total = kept * state[GROUP + place : GROUP + place + 1]
        total += jnp.sum(far, axis=0, keepdims=True) + jnp.sum(coarse, axis=0, keepdims=True)
        inverse = 1.0 / total
        coarse = pltpu.roll(coarse, 1, 0)
        summed = dot_rows(far_values, far.astype(jnp.bfloat16)) + dot_rows(pairs, coarse.astype(jnp.bfloat16))
        sum_ref[:, columns] = (summed * inverse).T
        shares.append(kept * inverse)
    shares.append(jnp.zeros((SUBLANES - GROUP, rows), jnp.float32))
    share_ref[:, :SUBLANES] = jnp.concatenate(shares, axis=0).T


def finish_kernel(count, lane, sum_ref, share_ref, own_ref, other_ref, vm_ref, vr_ref, *rest):
    out_ref = rest[-1]
    for place in range(count):
        columns = head_columns(place)
        values = jnp.concatenate([vm_ref[:, columns], vr_ref[:, columns]], axis=0)
        share = share_ref[:, lane + place : lane + place + 1]
        result = own_ref[:, columns] + dot(other_ref[place], values)
        out_ref[:, columns] = (sum_ref[:, columns] + share * result).astype(jnp.bfloat16)


def in_hbm(array):
    return pltpu.with_memory_space_constraint(array, pltpu.HBM)


def cost():
    return pl.CostEstimate(flops=0, bytes_accessed=0, transcendentals=0)


def gather_all(value, axis):
    size = lax.axis_size(axis)
    if size & (size - 1):
        return lax.all_gather(value, axis, axis=0, tiled=True)
    bits = [2**j for j in range(size.bit_length() - 1)]
    for step in [bits[:1]] + [bits[j : j + 2] for j in range(1, len(bits), 2)]:
        masks = step + [sum(step)] if len(step) == 2 else step
        value = jnp.concatenate([value] + [partner(value, axis, mask) for mask in masks], axis=0)
    return value


def on_device(query, keys, values, middle_head_shift, coarse_head_shift):
    rows, width = query.shape
    members = rows // MIDDLE_DILATION
    near_rows = 2 * lax.axis_size("outer")
    bf16 = jnp.bfloat16
    smem = pl.BlockSpec(memory_space=pltpu.SMEM)
    vmem = pl.BlockSpec(memory_space=pltpu.VMEM)
    anywhere = pl.BlockSpec(memory_space=pl.ANY)
    params = pltpu.CompilerParams(vmem_limit_bytes=24 * 1024 * 1024)
    order_scratch = pltpu.VMEM((MIDDLE_DILATION, rows, rows), bf16)

    def columns_of(count, heads=GROUP, first=0):
        return pl.BlockSpec((count, heads * HEAD_FEATURES), lambda i: (0, first // heads + i))

    def call(kernel, name, **options):
        return pl.pallas_call(kernel, name=name, compiler_params=params, cost_estimate=cost(), **options)

    other_keys = partner(keys, "inner", 1)
    prepared = call(
        functools.partial(prepare_kernel, CHUNKS),
        "prepare",
        out_shape=[
            pltpu.HBM((2 * members, width), bf16),
            pltpu.HBM((members + near_rows, width), bf16),
            *[pltpu.HBM((rows - members, c * HEAD_FEATURES), bf16) for c in CHUNKS],
            jax.ShapeDtypeStruct((2, width), bf16),
        ],
        in_specs=[smem, smem, vmem, vmem],
        out_specs=[vmem] * (3 + len(CHUNKS)),
        scratch_shapes=[order_scratch],
    )(middle_head_shift, coarse_head_shift, keys, values)
    own_members, own_vm, own_vr, coarse = prepared[0], prepared[1], prepared[2:-1], prepared[-1]
    cross = partner(own_members, "inner", 2)
    near = gather_all(coarse, "outer")
    own_vm = call(
        append_kernel,
        "append",
        out_shape=pltpu.HBM(own_vm.shape, bf16),
        in_specs=[vmem, anywhere],
        out_specs=anywhere,
        input_output_aliases={1: 0},
        scratch_shapes=[pltpu.SemaphoreType.DMA],
    )(near, own_vm)
    other_vm = partner(own_vm, "inner", 1)
    cross, own_vr = lax.optimization_barrier((cross, own_vr))
    other_vr = [partner(piece, "inner", 1) for piece in own_vr]
    other_km = call(
        pick_kernel,
        "pick",
        out_shape=pltpu.HBM((members + near_rows, width), bf16),
        in_specs=[smem, vmem, vmem],
        out_specs=vmem,
    )(middle_head_shift, other_keys, near)
    diagonal_k = partner(other_km, "inner", 2)

    groups = HEAD_COUNT // GROUP
    whole, with_near = columns_of(rows), columns_of(members + near_rows)
    lanes = pl.BlockSpec((rows, LANES), lambda i: (0, i))

    keys_after = lax.optimization_barrier((other_keys, other_km))[0]

    def first_part(first, heads, before):
        def columns(count, width):
            return pl.BlockSpec((count, width), lambda i: (0, first // GROUP + i))

        block = columns(rows, GROUP * HEAD_FEATURES)
        return call(
            functools.partial(first_kernel, first),
            "first",
            out_shape=[
                pltpu.HBM((rows, width), jnp.float32),
                pltpu.HBM((HEAD_COUNT, rows, rows), bf16),
                pltpu.HBM((rows, groups * LANES), jnp.float32),
            ],
            grid=(heads // GROUP,),
            in_specs=[smem, block, block, block, block] + [anywhere] * len(before),
            out_specs=[
                block,
                pl.BlockSpec((GROUP, rows, rows), lambda i: (first // GROUP + i, 0, 0)),
                columns(rows, LANES),
            ],
            input_output_aliases={5 + i: i for i in range(len(before))},
            scratch_shapes=[order_scratch],
        )(middle_head_shift, in_hbm(query), in_hbm(keys), in_hbm(values), keys_after, *before)

    early = groups // 2 * GROUP
    begun = first_part(0, early, ())
    diagonal_v = partner(lax.optimization_barrier((other_vm, begun[2]))[0], "inner", 2)
    own_sum, other_weights, state = first_part(early, HEAD_COUNT - early, begun)
    extra_sum, share = call(
        extra_kernel,
        "extra",
        out_shape=[pltpu.HBM((rows, width), jnp.float32), pltpu.HBM((rows, groups * LANES), jnp.float32)],
        grid=(groups,),
        in_specs=[
            smem, smem, whole, lanes, columns_of(2 * members), with_near, with_near, columns_of(near_rows), with_near
        ],
        out_specs=[whole, lanes],
    )(
        middle_head_shift, coarse_head_shift, in_hbm(query), in_hbm(state), cross, diagonal_k, diagonal_v, near, other_vm
    )

    out = None
    first = 0
    for chunk, vr in zip(CHUNKS, other_vr):
        heads = min(GROUP, chunk)
        block = columns_of(rows, heads, first)
        args = [*map(in_hbm, (extra_sum, share, own_sum, other_weights)), other_vm, vr]
        specs = [
            block,
            pl.BlockSpec((rows, LANES), lambda i, first=first: (0, first // GROUP + i)),
            block,
            pl.BlockSpec((heads, rows, rows), lambda i, first=first, heads=heads: (first // heads + i, 0, 0)),
            columns_of(members, heads, first),
            columns_of(rows - members, heads),
        ]
        aliases = {}
        if out is not None:
            aliases = {len(args): 0}
            args.append(out)
            specs.append(anywhere)
        out = call(
            functools.partial(finish_kernel, heads, first % GROUP),
            "finish",
            out_shape=jax.ShapeDtypeStruct((rows, width), bf16),
            grid=(chunk // heads,),
            in_specs=specs,
            out_specs=block,
            input_output_aliases=aliases,
        )(*args)
        first += chunk
    return out


def solution(mesh):
    placed = (
        P(("outer", "inner"), None),
        P(("outer", "inner"), None),
        P(("outer", "inner"), None),
        P(),
        P(),
    )
    return jax.shard_map(
        on_device,
        mesh=mesh,
        in_specs=placed,
        out_specs=P(("outer", "inner"), None),
        check_vma=False,
    )
```

```python
import functools

import jax
import jax.numpy as jnp
from jax import lax
from jax.experimental import pallas as pl
from jax.experimental.pallas import tpu as pltpu
from jax.sharding import PartitionSpec as P

HEAD_COUNT = 16
HEAD_FEATURES = 128
MIDDLE_DILATION = 4
CHUNKS = (12, 4)
LANES = 128
SUBLANES = 16
EXP2_SCALE = HEAD_FEATURES ** (-0.5) * 1.4426950408889634
MASKED = -1e30


def partner(value, axis, mask):
    pairs = [(source, source ^ mask) for source in range(lax.axis_size(axis))]
    return lax.ppermute(value, axis, pairs)


def one_hot(mask):
    return mask.astype(jnp.float32).astype(jnp.bfloat16)


def fill_orders(order_ref):
    rows = order_ref.shape[1]
    members = rows // MIDDLE_DILATION
    group = lax.broadcasted_iota(jnp.int32, (members, rows), 0)
    token = lax.broadcasted_iota(jnp.int32, (members, rows), 1)
    for place in range(MIDDLE_DILATION):
        block = one_hot(token == MIDDLE_DILATION * group + place)
        for shift in range(MIDDLE_DILATION):
            slot = (place - shift) % MIDDLE_DILATION
            order_ref[shift, slot * members : (slot + 1) * members] = block


def dot(a, b):
    return jnp.dot(a, b, preferred_element_type=jnp.float32)


def head_columns(head):
    return slice(head * HEAD_FEATURES, (head + 1) * HEAD_FEATURES)


def prepare_kernel(chunks, middle_ref, coarse_ref, q_hbm, k_hbm, v_hbm, *rest):
    q_ref, k_ref, v_ref, members_ref, vm_ref, *vr_refs, coarse_out_ref, order_ref, semaphores = rest
    pairs = ((k_hbm, k_ref), (v_hbm, v_ref), (q_hbm, q_ref))
    copies = [pltpu.make_async_copy(*pair, semaphores.at[i]) for i, pair in enumerate(pairs)]
    for copy in copies:
        copy.start()
    rows = k_ref.shape[0]
    members = rows // MIDDLE_DILATION
    fill_orders(order_ref)
    token = lax.broadcasted_iota(jnp.int32, (SUBLANES, rows), 1)
    first_row = lax.broadcasted_iota(jnp.int32, (SUBLANES, rows), 0) == 0
    second_row = lax.broadcasted_iota(jnp.int32, (SUBLANES, rows), 0) == 1
    copies[0].wait()
    copies[1].wait()
    head = 0
    for chunk, vr_ref in zip(chunks, vr_refs):
        for place in range(chunk):
            columns = head_columns(head)
            order = order_ref[middle_ref[head]]
            k, v = k_ref[:, columns], v_ref[:, columns]
            v_ordered = dot(order, v).astype(jnp.bfloat16)
            members_ref[:members, columns] = dot(order[:members], k).astype(jnp.bfloat16)
            members_ref[members:, columns] = v_ordered[:members]
            vm_ref[:, columns] = v_ordered[:members]
            vr_ref[:, head_columns(place)] = v_ordered[members:]
            chosen = token == coarse_ref[head]
            picked = dot(one_hot(chosen & first_row), k) + dot(one_hot(chosen & second_row), v)
            coarse_out_ref[:, columns] = picked[:2].astype(jnp.bfloat16)
            head += 1
    copies[2].wait()


def join_kernel(vm_ref, near_ref, out_ref):
    members = vm_ref.shape[0]
    out_ref[:members] = vm_ref[...]
    out_ref[members:] = near_ref[...]


def pick_kernel(middle_ref, k_ref, near_ref, members_ref):
    rows = k_ref.shape[0]
    members = rows // MIDDLE_DILATION
    members_ref[members:] = near_ref[...]
    group = lax.broadcasted_iota(jnp.int32, (members, rows), 0)
    token = lax.broadcasted_iota(jnp.int32, (members, rows), 1)
    offset = token - MIDDLE_DILATION * group
    for head in range(HEAD_COUNT):
        columns = head_columns(head)
        chosen = one_hot(offset == middle_ref[head])
        members_ref[:members, columns] = dot(chosen, k_ref[:, columns]).astype(jnp.bfloat16)


def dot_keys(q, keys):
    return lax.dot_general(q, keys, (((1,), (1,)), ((), ())), preferred_element_type=jnp.float32)


def dot_rows(a, b):
    return lax.dot_general(a, b, (((0,), (0,)), ((), ())), preferred_element_type=jnp.float32)


def side_by_side(columns):
    rows = columns[0].shape[0]
    lane = lax.broadcasted_iota(jnp.int32, (rows, LANES), 1)
    result = jnp.zeros((rows, LANES), jnp.float32)
    for place, column in enumerate(columns):
        result = jnp.where(lane == place, column, result)
    return result


def member_rows(rows, shift):
    row = lax.broadcasted_iota(jnp.int32, (rows, 1), 0)
    return (row & (MIDDLE_DILATION - 1)) == shift


def lane_tiles(part):
    return [part[:, i : i + LANES] for i in range(0, part.shape[1], LANES)]


def weights(part, top):
    return jnp.exp2((part - top) * EXP2_SCALE)


def first_kernel(first, middle_ref, q_ref, k_ref, v_ref, kp_ref, own_ref, other_ref, state_ref, order_ref):
    fill_orders(order_ref)
    rows = q_ref.shape[0]
    members = rows // MIDDLE_DILATION
    column = lax.broadcasted_iota(jnp.int32, (1, rows), 1)
    tops, totals = [], []
    heads = other_ref.shape[0]
    for place in range(heads):
        columns = head_columns(first + place)
        shift = middle_ref[first + place]
        q = q_ref[:, columns]
        own = dot_keys(q, k_ref[:, columns])
        other_keys = dot(order_ref[shift], kp_ref[:, columns]).astype(jnp.bfloat16)
        other = dot_keys(q, other_keys)
        top = functools.reduce(jnp.maximum, lane_tiles(own) + lane_tiles(other))
        top = jnp.max(top, axis=1, keepdims=True)
        row_is_member = member_rows(rows, shift)
        own, other = weights(own, top), weights(other, top)
        own_member = row_is_member & ((column & (MIDDLE_DILATION - 1)) == shift)
        own = jnp.where(own_member, own + own, own)
        twice = other[:, :LANES]
        twice = jnp.where(row_is_member & (column[:, :LANES] < members), twice + twice, twice)
        other = jnp.concatenate([twice, other[:, LANES:]], axis=1)
        total = functools.reduce(jnp.add, lane_tiles(own) + lane_tiles(other))
        tops.append(top)
        totals.append(jnp.sum(total, axis=1, keepdims=True))
        own_ref[:, head_columns(place)] = dot(own.astype(jnp.bfloat16), v_ref[:, columns])
        other_ref[place] = other.astype(jnp.bfloat16)
    state_ref[...] = side_by_side(tops + totals)


def extra_kernel(
    middle_ref, coarse_ref, q_ref, state_a_ref, state_b_ref, cross_ref, diagonal_k_ref, diagonal_v_ref, near_ref,
    other_ref, sum_ref, share_ref,
):
    rows = q_ref.shape[0]
    members = rows // MIDDLE_DILATION
    half = HEAD_COUNT // 2
    token = lax.broadcasted_iota(jnp.int32, (1, rows), 1)
    states = [ref[...].T for ref in (state_a_ref, state_b_ref)]
    shares = []
    for head in range(HEAD_COUNT):
        columns = head_columns(head)
        state, place = states[head // half], head % half
        q = q_ref[:, columns]
        far_keys = jnp.concatenate([cross_ref[:members, columns], diagonal_k_ref[:members, columns]], axis=0)
        far_values = jnp.concatenate([cross_ref[members:, columns], diagonal_v_ref[:members, columns]], axis=0)
        pieces = [near_ref[:, columns]] + [
            ref[members:, columns] for ref in (other_ref, diagonal_k_ref, diagonal_v_ref)
        ]
        pairs = jnp.concatenate(pieces, axis=0)
        is_key = (lax.broadcasted_iota(jnp.int32, (pairs.shape[0], 1), 0) & 1) == 0
        row_is_member = (token & (MIDDLE_DILATION - 1)) == middle_ref[head]
        far = jnp.where(row_is_member, dot_keys(far_keys, q), MASKED)
        coarse = jnp.where(is_key & (token == coarse_ref[head]), dot_keys(pairs, q), MASKED)
        before = state[place : place + 1]
        top = jnp.maximum(before, jnp.max(far, axis=0, keepdims=True))
        top = jnp.maximum(top, jnp.max(coarse, axis=0, keepdims=True))
        far, coarse = weights(far, top), weights(coarse, top)
        kept = weights(before, top)
        total = kept * state[half + place : half + place + 1]
        total += jnp.sum(far, axis=0, keepdims=True) + jnp.sum(coarse, axis=0, keepdims=True)
        inverse = 1.0 / total
        coarse = pltpu.roll(coarse, 1, 0)
        summed = dot_rows(far_values, far.astype(jnp.bfloat16)) + dot_rows(pairs, coarse.astype(jnp.bfloat16))
        sum_ref[:, columns] = (summed * inverse).T
        shares.append(kept * inverse)
    share_ref[:, :HEAD_COUNT] = jnp.concatenate(shares, axis=0).T


def finish_kernel(heads, sum_ref, share_ref, own_a_ref, own_b_ref, other_a_ref, other_b_ref, vm_ref, vr_ref, *rest):
    out_ref, ready_ref, semaphores = rest[-3:]
    members = vr_ref.shape[0] // (MIDDLE_DILATION - 1)
    half = HEAD_COUNT // 2
    copies = []
    for place, head in enumerate(heads):
        columns = head_columns(head)
        own_ref, other_ref = ((own_a_ref, other_a_ref), (own_b_ref, other_b_ref))[head // half]
        values = jnp.concatenate([vm_ref[:members, columns], vr_ref[:, head_columns(place)]], axis=0)
        result = own_ref[:, head_columns(head % half)] + dot(other_ref[head % half], values)
        result = sum_ref[:, columns] + share_ref[:, head : head + 1] * result
        ready_ref[place] = result.astype(jnp.bfloat16)
        copies.append(pltpu.make_async_copy(ready_ref.at[place], out_ref.at[:, columns], semaphores.at[place]))
        copies[-1].start()
    for copy in copies:
        copy.wait()


def in_hbm(array):
    return pltpu.with_memory_space_constraint(array, pltpu.HBM)


def cost():
    return pl.CostEstimate(flops=0, bytes_accessed=0, transcendentals=0)


def gather_all(value, axis):
    size = lax.axis_size(axis)
    if size & (size - 1):
        return lax.all_gather(value, axis, axis=0, tiled=True)
    bits = [2**j for j in range(size.bit_length() - 1)]
    for step in [bits[:1]] + [bits[j : j + 2] for j in range(1, len(bits), 2)]:
        masks = step + [sum(step)] if len(step) == 2 else step
        value = jnp.concatenate([value] + [partner(value, axis, mask) for mask in masks], axis=0)
    return value


def on_device(query, keys, values, middle_head_shift, coarse_head_shift):
    rows, width = query.shape
    members = rows // MIDDLE_DILATION
    near_rows = 2 * lax.axis_size("outer")
    half = HEAD_COUNT // 2
    bf16, f32 = jnp.bfloat16, jnp.float32
    smem = pl.BlockSpec(memory_space=pltpu.SMEM)
    vmem = pl.BlockSpec(memory_space=pltpu.VMEM)
    anywhere = pl.BlockSpec(memory_space=pl.ANY)
    params = pltpu.CompilerParams(vmem_limit_bytes=16 * 1024 * 1024)
    orders = pltpu.VMEM((MIDDLE_DILATION, rows, rows), bf16)

    def call(kernel, name, *args, **options):
        return pl.pallas_call(kernel, name=name, compiler_params=params, cost_estimate=cost(), **options)(*args)

    other_keys = partner(keys, "inner", 1)
    q, k, v, own_members, own_vm, *own_vr, coarse = call(
        functools.partial(prepare_kernel, CHUNKS),
        "prepare",
        middle_head_shift, coarse_head_shift, in_hbm(query), in_hbm(keys), in_hbm(values),
        out_shape=[
            *[pltpu.VMEM((rows, width), bf16)] * 3,
            pltpu.VMEM((2 * members, width), bf16),
            pltpu.VMEM((members, width), bf16),
            *[pltpu.VMEM((rows - members, c * HEAD_FEATURES), bf16) for c in CHUNKS],
            pltpu.VMEM((2, width), bf16),
        ],
        in_specs=[smem, smem, anywhere, anywhere, anywhere],
        out_specs=[vmem] * (6 + len(CHUNKS)),
        scratch_shapes=[orders, pltpu.SemaphoreType.DMA((3,))],
    )
    cross = partner(own_members, "inner", 2)
    near = gather_all(coarse, "outer")
    own_vm = call(
        join_kernel,
        "join",
        own_vm, near,
        out_shape=pltpu.VMEM((members + near_rows, width), bf16),
        in_specs=[vmem, vmem],
        out_specs=vmem,
    )
    other_vm = partner(own_vm, "inner", 1)
    cross, own_vr = lax.optimization_barrier((cross, own_vr))
    other_vr = [partner(piece, "inner", 1) for piece in own_vr]
    other_km = call(
        pick_kernel,
        "pick",
        middle_head_shift, other_keys, near,
        out_shape=pltpu.VMEM((members + near_rows, width), bf16),
        in_specs=[smem, vmem, vmem],
        out_specs=vmem,
    )
    diagonal_k = partner(other_km, "inner", 2)
    other_keys = lax.optimization_barrier((other_keys, other_km))[0]

    def first_part(first, query):
        return call(
            functools.partial(first_kernel, first),
            "first",
            middle_head_shift, query, k, v, other_keys,
            out_shape=[
                pltpu.VMEM((rows, half * HEAD_FEATURES), f32),
                pltpu.VMEM((half, rows, rows), bf16),
                pltpu.VMEM((rows, LANES), f32),
            ],
            in_specs=[smem] + [vmem] * 4,
            out_specs=[vmem] * 3,
            scratch_shapes=[orders],
        )

    own_a, weights_a, state_a = first_part(0, q)
    diagonal_v = partner(lax.optimization_barrier((other_vm, state_a))[0], "inner", 2)
    own_b, weights_b, state_b = first_part(half, lax.optimization_barrier((q, state_a))[0])
    extra_sum, share = call(
        extra_kernel,
        "extra",
        middle_head_shift, coarse_head_shift, q, state_a, state_b, cross, diagonal_k, diagonal_v, near, other_vm,
        out_shape=[pltpu.VMEM((rows, width), f32), pltpu.VMEM((rows, LANES), f32)],
        in_specs=[smem, smem] + [vmem] * 8,
        out_specs=[vmem] * 2,
    )

    out = []
    first = 0
    for chunk, vr in zip(CHUNKS, other_vr):
        args = [extra_sum, share, own_a, own_b, weights_a, weights_b, other_vm, vr]
        out = [
            call(
                functools.partial(finish_kernel, range(first, first + chunk)),
                "finish",
                *args, *out,
                out_shape=jax.ShapeDtypeStruct((rows, width), bf16),
                in_specs=[vmem] * len(args) + [anywhere] * len(out),
                out_specs=anywhere,
                input_output_aliases={len(args): 0} if out else {},
                scratch_shapes=[pltpu.VMEM((chunk, rows, HEAD_FEATURES), bf16), pltpu.SemaphoreType.DMA((chunk,))],
            )
        ]
        first += chunk
    return out[0]


def solution(mesh):
    placed = (
        P(("outer", "inner"), None),
        P(("outer", "inner"), None),
        P(("outer", "inner"), None),
        P(),
        P(),
    )
    return jax.shard_map(
        on_device,
        mesh=mesh,
        in_specs=placed,
        out_specs=P(("outer", "inner"), None),
        check_vma=False,
    )
```

```python
import functools

import jax
import jax.numpy as jnp
from jax import lax
from jax.experimental import pallas as pl
from jax.experimental.pallas import tpu as pltpu
from jax.sharding import PartitionSpec as P

HEAD_COUNT = 16
HEAD_FEATURES = 128
MIDDLE_DILATION = 4
CHUNKS = (12, 4)
LANES = 128
SUBLANES = 16
EXP2_SCALE = HEAD_FEATURES ** (-0.5) * 1.4426950408889634
MASKED = -1e30


def partner(value, axis, mask):
    pairs = [(source, source ^ mask) for source in range(lax.axis_size(axis))]
    return lax.ppermute(value, axis, pairs)


def one_hot(mask):
    return mask.astype(jnp.float32).astype(jnp.bfloat16)


def fill_orders(order_ref):
    rows = order_ref.shape[1]
    members = rows // MIDDLE_DILATION
    group = lax.broadcasted_iota(jnp.int32, (members, rows), 0)
    token = lax.broadcasted_iota(jnp.int32, (members, rows), 1)
    for place in range(MIDDLE_DILATION):
        block = one_hot(token == MIDDLE_DILATION * group + place)
        for shift in range(MIDDLE_DILATION):
            slot = (place - shift) % MIDDLE_DILATION
            order_ref[shift, slot * members : (slot + 1) * members] = block


def dot(a, b):
    return jnp.dot(a, b, preferred_element_type=jnp.float32)


def head_columns(head):
    return slice(head * HEAD_FEATURES, (head + 1) * HEAD_FEATURES)


def prepare_kernel(chunks, middle_ref, coarse_ref, q_hbm, k_hbm, v_hbm, *rest):
    q_ref, k_ref, v_ref, members_ref, vm_ref, *vr_refs, coarse_out_ref, order_ref, semaphores = rest
    pairs = ((k_hbm, k_ref), (v_hbm, v_ref), (q_hbm, q_ref))
    copies = [pltpu.make_async_copy(*pair, semaphores.at[i]) for i, pair in enumerate(pairs)]
    for copy in copies:
        copy.start()
    rows = k_ref.shape[0]
    members = rows // MIDDLE_DILATION
    fill_orders(order_ref)
    token = lax.broadcasted_iota(jnp.int32, (SUBLANES, rows), 1)
    first_row = lax.broadcasted_iota(jnp.int32, (SUBLANES, rows), 0) == 0
    second_row = lax.broadcasted_iota(jnp.int32, (SUBLANES, rows), 0) == 1
    copies[0].wait()
    copies[1].wait()
    head = 0
    for chunk, vr_ref in zip(chunks, vr_refs):
        for place in range(chunk):
            columns = head_columns(head)
            order = order_ref[middle_ref[head]]
            k, v = k_ref[:, columns], v_ref[:, columns]
            v_ordered = dot(order, v).astype(jnp.bfloat16)
            members_ref[:members, columns] = dot(order[:members], k).astype(jnp.bfloat16)
            members_ref[members:, columns] = v_ordered[:members]
            vm_ref[:, columns] = v_ordered[:members]
            vr_ref[:, head_columns(place)] = v_ordered[members:]
            chosen = token == coarse_ref[head]
            picked = dot(one_hot(chosen & first_row), k) + dot(one_hot(chosen & second_row), v)
            coarse_out_ref[:, columns] = picked[:2].astype(jnp.bfloat16)
            head += 1
    copies[2].wait()


def join_kernel(vm_ref, near_ref, out_ref):
    members = vm_ref.shape[0]
    out_ref[:members] = vm_ref[...]
    out_ref[members:] = near_ref[...]


def stack_kernel(near_ref, *refs):
    out_ref = refs[-1]
    rows = near_ref.shape[0]
    out_ref[:rows] = near_ref[...]
    for place, ref in enumerate(refs[:-1]):
        out_ref[(place + 1) * rows : (place + 2) * rows] = ref[ref.shape[0] - rows :]


def pick_kernel(middle_ref, k_ref, near_ref, members_ref):
    rows = k_ref.shape[0]
    members = rows // MIDDLE_DILATION
    members_ref[members:] = near_ref[...]
    group = lax.broadcasted_iota(jnp.int32, (members, rows), 0)
    token = lax.broadcasted_iota(jnp.int32, (members, rows), 1)
    offset = token - MIDDLE_DILATION * group
    for head in range(HEAD_COUNT):
        columns = head_columns(head)
        chosen = one_hot(offset == middle_ref[head])
        members_ref[:members, columns] = dot(chosen, k_ref[:, columns]).astype(jnp.bfloat16)


def dot_keys(q, keys):
    return lax.dot_general(q, keys, (((1,), (1,)), ((), ())), preferred_element_type=jnp.float32)


def dot_rows(a, b):
    return lax.dot_general(a, b, (((0,), (0,)), ((), ())), preferred_element_type=jnp.float32)


def side_by_side(columns):
    rows = columns[0].shape[0]
    lane = lax.broadcasted_iota(jnp.int32, (rows, LANES), 1)
    result = jnp.zeros((rows, LANES), jnp.float32)
    for place, column in enumerate(columns):
        result = jnp.where(lane == place, column, result)
    return result


def member_rows(rows, shift):
    row = lax.broadcasted_iota(jnp.int32, (rows, 1), 0)
    return (row & (MIDDLE_DILATION - 1)) == shift


def lane_tiles(part):
    return [part[:, i : i + LANES] for i in range(0, part.shape[1], LANES)]


def weights(part, top):
    return jnp.exp2((part - top) * EXP2_SCALE)


def first_kernel(first, middle_ref, q_ref, k_ref, v_ref, kp_ref, own_ref, other_ref, state_ref, order_ref):
    fill_orders(order_ref)
    rows = q_ref.shape[0]
    members = rows // MIDDLE_DILATION
    column = lax.broadcasted_iota(jnp.int32, (1, rows), 1)
    tops, totals = [], []
    heads = other_ref.shape[0]
    for place in range(heads):
        columns = head_columns(first + place)
        shift = middle_ref[first + place]
        q = q_ref[:, columns]
        own = dot_keys(q, k_ref[:, columns])
        other_keys = dot(order_ref[shift], kp_ref[:, columns]).astype(jnp.bfloat16)
        other = dot_keys(q, other_keys)
        top = functools.reduce(jnp.maximum, lane_tiles(own) + lane_tiles(other))
        top = jnp.max(top, axis=1, keepdims=True)
        row_is_member = member_rows(rows, shift)
        own, other = weights(own, top), weights(other, top)
        own_member = row_is_member & ((column & (MIDDLE_DILATION - 1)) == shift)
        own = jnp.where(own_member, own + own, own)
        twice = other[:, :LANES]
        twice = jnp.where(row_is_member & (column[:, :LANES] < members), twice + twice, twice)
        other = jnp.concatenate([twice, other[:, LANES:]], axis=1)
        total = functools.reduce(jnp.add, lane_tiles(own) + lane_tiles(other))
        tops.append(top)
        totals.append(jnp.sum(total, axis=1, keepdims=True))
        own_ref[:, head_columns(place)] = dot(own.astype(jnp.bfloat16), v_ref[:, columns])
        other_ref[place] = other.astype(jnp.bfloat16)
    state_ref[...] = side_by_side(tops + totals)


def extra_kernel(
    middle_ref, coarse_ref, q_ref, state_a_ref, state_b_ref, cross_ref, diagonal_k_ref, diagonal_v_ref, mine_ref,
    other_ref, sum_ref, share_ref,
):
    rows = q_ref.shape[0]
    members = rows // MIDDLE_DILATION
    half = HEAD_COUNT // 2
    far_rows, coarse_rows = 2 * members, 2 * mine_ref.shape[0]
    token = lax.broadcasted_iota(jnp.int32, (1, rows), 1)
    is_key = (lax.broadcasted_iota(jnp.int32, (coarse_rows, 1), 0) & 1) == 0
    states = [ref[...].T for ref in (state_a_ref, state_b_ref)]
    shares = []
    for head in range(HEAD_COUNT):
        columns = head_columns(head)
        state, place = states[head // half], head % half
        pairs = [mine_ref[:, columns], other_ref[:, columns]]
        keys = jnp.concatenate([cross_ref[:members, columns], diagonal_k_ref[:members, columns], *pairs], axis=0)
        values = jnp.concatenate([cross_ref[members:, columns], diagonal_v_ref[:members, columns], *pairs], axis=0)
        scores = dot_keys(keys, q_ref[:, columns])
        far = jnp.where((token & (MIDDLE_DILATION - 1)) == middle_ref[head], scores[:far_rows], MASKED)
        coarse = jnp.where(is_key & (token == coarse_ref[head]), scores[far_rows:], MASKED)
        before = state[place : place + 1]
        top = jnp.maximum(before, jnp.max(far, axis=0, keepdims=True))
        top = jnp.maximum(top, jnp.max(coarse, axis=0, keepdims=True))
        far, coarse = weights(far, top), weights(coarse, top)
        kept = weights(before, top)
        total = kept * state[half + place : half + place + 1]
        total += jnp.sum(far, axis=0, keepdims=True) + jnp.sum(coarse, axis=0, keepdims=True)
        inverse = 1.0 / total
        shifted = pltpu.roll(coarse, 1, 0)
        mixed = jnp.concatenate([(far * inverse).astype(jnp.bfloat16), (shifted * inverse).astype(jnp.bfloat16)], axis=0)
        sum_ref[:, columns] = dot_rows(mixed, values)
        shares.append(kept * inverse)
    share_ref[:, :HEAD_COUNT] = jnp.concatenate(shares, axis=0).T


def finish_kernel(heads, sum_ref, share_ref, own_a_ref, own_b_ref, other_a_ref, other_b_ref, vm_ref, vr_ref, *rest):
    out_ref, ready_ref, semaphores = rest[-3:]
    members = vr_ref.shape[0] // (MIDDLE_DILATION - 1)
    half = HEAD_COUNT // 2
    copies = []
    for place, head in enumerate(heads):
        columns = head_columns(head)
        own_ref, other_ref = ((own_a_ref, other_a_ref), (own_b_ref, other_b_ref))[head // half]
        values = jnp.concatenate([vm_ref[:members, columns], vr_ref[:, head_columns(place)]], axis=0)
        result = own_ref[:, head_columns(head % half)] + dot(other_ref[head % half], values)
        result = sum_ref[:, columns] + share_ref[:, head : head + 1] * result
        ready_ref[place] = result.astype(jnp.bfloat16)
        copies.append(pltpu.make_async_copy(ready_ref.at[place], out_ref.at[:, columns], semaphores.at[place]))
        copies[-1].start()
    for copy in copies:
        copy.wait()


def in_hbm(array):
    return pltpu.with_memory_space_constraint(array, pltpu.HBM)


def cost():
    return pl.CostEstimate(flops=0, bytes_accessed=0, transcendentals=0)


def gather_upper(value, axis):
    size = lax.axis_size(axis)
    assert size & (size - 1) == 0
    bits = [2**j for j in range(1, size.bit_length() - 1)]
    for step in [bits[j : j + 2] for j in range(0, len(bits), 2)]:
        masks = step + [sum(step)] if len(step) == 2 else step
        value = jnp.concatenate([value] + [partner(value, axis, mask) for mask in masks], axis=0)
    return value


def on_device(query, keys, values, middle_head_shift, coarse_head_shift):
    rows, width = query.shape
    members = rows // MIDDLE_DILATION
    near_rows = lax.axis_size("outer")
    half = HEAD_COUNT // 2
    bf16, f32 = jnp.bfloat16, jnp.float32
    smem = pl.BlockSpec(memory_space=pltpu.SMEM)
    vmem = pl.BlockSpec(memory_space=pltpu.VMEM)
    anywhere = pl.BlockSpec(memory_space=pl.ANY)
    params = pltpu.CompilerParams(vmem_limit_bytes=16 * 1024 * 1024)
    orders = pltpu.VMEM((MIDDLE_DILATION, rows, rows), bf16)

    def call(kernel, name, *args, **options):
        return pl.pallas_call(kernel, name=name, compiler_params=params, cost_estimate=cost(), **options)(*args)

    other_keys = partner(keys, "inner", 1)
    q, k, v, own_members, own_vm, *own_vr, coarse = call(
        functools.partial(prepare_kernel, CHUNKS),
        "prepare",
        middle_head_shift, coarse_head_shift, in_hbm(query), in_hbm(keys), in_hbm(values),
        out_shape=[
            *[pltpu.VMEM((rows, width), bf16)] * 3,
            pltpu.VMEM((2 * members, width), bf16),
            pltpu.VMEM((members, width), bf16),
            *[pltpu.VMEM((rows - members, c * HEAD_FEATURES), bf16) for c in CHUNKS],
            pltpu.VMEM((2, width), bf16),
        ],
        in_specs=[smem, smem, anywhere, anywhere, anywhere],
        out_specs=[vmem] * (6 + len(CHUNKS)),
        scratch_shapes=[orders, pltpu.SemaphoreType.DMA((3,))],
    )
    cross = partner(own_members, "inner", 2)
    near = gather_upper(coarse, "outer")
    own_vm = call(
        join_kernel,
        "join",
        own_vm, near,
        out_shape=pltpu.VMEM((members + near_rows, width), bf16),
        in_specs=[vmem, vmem],
        out_specs=vmem,
    )
    other_vm = partner(own_vm, "inner", 1)
    cross, own_vr = lax.optimization_barrier((cross, own_vr))
    other_vr = [partner(piece, "inner", 1) for piece in own_vr]
    other_km = call(
        pick_kernel,
        "pick",
        middle_head_shift, other_keys, near,
        out_shape=pltpu.VMEM((members + near_rows, width), bf16),
        in_specs=[smem, vmem, vmem],
        out_specs=vmem,
    )
    diagonal_k = partner(other_km, "inner", 2)
    other_keys = lax.optimization_barrier((other_keys, other_km))[0]

    def first_part(first, query):
        return call(
            functools.partial(first_kernel, first),
            "first",
            middle_head_shift, query, k, v, other_keys,
            out_shape=[
                pltpu.VMEM((rows, half * HEAD_FEATURES), f32),
                pltpu.VMEM((half, rows, rows), bf16),
                pltpu.VMEM((rows, LANES), f32),
            ],
            in_specs=[smem] + [vmem] * 4,
            out_specs=[vmem] * 3,
            scratch_shapes=[orders],
        )

    own_a, weights_a, state_a = first_part(0, q)
    diagonal_v = partner(lax.optimization_barrier((other_vm, state_a))[0], "inner", 2)
    own_b, weights_b, state_b = first_part(half, lax.optimization_barrier((q, state_a))[0])
    diagonal_v = lax.optimization_barrier((diagonal_v, state_b))[0]
    mine = call(
        stack_kernel,
        "stack",
        near, other_vm, diagonal_k, diagonal_v,
        out_shape=pltpu.VMEM((lax.axis_size("inner") * near_rows, width), bf16),
        in_specs=[vmem] * 4,
        out_specs=vmem,
    )
    extra_sum, share = call(
        extra_kernel,
        "extra",
        middle_head_shift, coarse_head_shift, q, state_a, state_b, cross, diagonal_k, diagonal_v, mine,
        partner(mine, "outer", 1),
        out_shape=[pltpu.VMEM((rows, width), f32), pltpu.VMEM((rows, LANES), f32)],
        in_specs=[smem, smem] + [vmem] * 8,
        out_specs=[vmem] * 2,
    )

    out = []
    first = 0
    for chunk, vr in zip(CHUNKS, other_vr):
        args = [extra_sum, share, own_a, own_b, weights_a, weights_b, other_vm, vr]
        out = [
            call(
                functools.partial(finish_kernel, range(first, first + chunk)),
                "finish",
                *args, *out,
                out_shape=jax.ShapeDtypeStruct((rows, width), bf16),
                in_specs=[vmem] * len(args) + [anywhere] * len(out),
                out_specs=anywhere,
                input_output_aliases={len(args): 0} if out else {},
                scratch_shapes=[pltpu.VMEM((chunk, rows, HEAD_FEATURES), bf16), pltpu.SemaphoreType.DMA((chunk,))],
            )
        ]
        first += chunk
    return out[0]


def solution(mesh):
    placed = (
        P(("outer", "inner"), None),
        P(("outer", "inner"), None),
        P(("outer", "inner"), None),
        P(),
        P(),
    )
    return jax.shard_map(
        on_device,
        mesh=mesh,
        in_specs=placed,
        out_specs=P(("outer", "inner"), None),
        check_vma=False,
    )
```

```python
import functools

import jax
import jax.numpy as jnp
from jax import lax
from jax.experimental import pallas as pl
from jax.experimental.pallas import tpu as pltpu
from jax.sharding import PartitionSpec as P

HEAD_COUNT = 16
HEAD_FEATURES = 128
MIDDLE_DILATION = 4
CHUNKS = (12, 4)
LANES = 128
SUBLANES = 16
EXP2_SCALE = HEAD_FEATURES ** (-0.5) * 1.4426950408889634
MASKED = -1e30


def partner(value, axis, mask):
    pairs = [(source, source ^ mask) for source in range(lax.axis_size(axis))]
    return lax.ppermute(value, axis, pairs)


def one_hot(mask):
    return mask.astype(jnp.float32).astype(jnp.bfloat16)


def fill_orders(order_ref):
    rows = order_ref.shape[1]
    members = rows // MIDDLE_DILATION
    group = lax.broadcasted_iota(jnp.int32, (members, rows), 0)
    token = lax.broadcasted_iota(jnp.int32, (members, rows), 1)
    for place in range(MIDDLE_DILATION):
        block = one_hot(token == MIDDLE_DILATION * group + place)
        for shift in range(MIDDLE_DILATION):
            slot = (place - shift) % MIDDLE_DILATION
            order_ref[shift, slot * members : (slot + 1) * members] = block


def dot(a, b):
    return jnp.dot(a, b, preferred_element_type=jnp.float32)


def head_columns(head):
    return slice(head * HEAD_FEATURES, (head + 1) * HEAD_FEATURES)


def prepare_kernel(chunks, middle_ref, coarse_ref, q_hbm, k_hbm, v_hbm, *rest):
    q_ref, k_ref, v_ref, members_ref, vm_ref, *vr_refs, coarse_out_ref, order_ref, semaphores = rest
    pairs = ((k_hbm, k_ref), (v_hbm, v_ref), (q_hbm, q_ref))
    copies = [pltpu.make_async_copy(*pair, semaphores.at[i]) for i, pair in enumerate(pairs)]
    for copy in copies:
        copy.start()
    rows = k_ref.shape[0]
    members = rows // MIDDLE_DILATION
    fill_orders(order_ref)
    token = lax.broadcasted_iota(jnp.int32, (SUBLANES, rows), 1)
    first_row = lax.broadcasted_iota(jnp.int32, (SUBLANES, rows), 0) == 0
    second_row = lax.broadcasted_iota(jnp.int32, (SUBLANES, rows), 0) == 1
    copies[0].wait()
    copies[1].wait()
    head = 0
    for chunk, vr_ref in zip(chunks, vr_refs):
        for place in range(chunk):
            columns = head_columns(head)
            order = order_ref[middle_ref[head]]
            k, v = k_ref[:, columns], v_ref[:, columns]
            v_ordered = dot(order, v).astype(jnp.bfloat16)
            members_ref[:members, columns] = dot(order[:members], k).astype(jnp.bfloat16)
            members_ref[members:, columns] = v_ordered[:members]
            vm_ref[:, columns] = v_ordered[:members]
            vr_ref[:, head_columns(place)] = v_ordered[members:]
            chosen = token == coarse_ref[head]
            picked = dot(one_hot(chosen & first_row), k) + dot(one_hot(chosen & second_row), v)
            coarse_out_ref[:, columns] = picked[:2].astype(jnp.bfloat16)
            head += 1
    copies[2].wait()


def join_kernel(vm_ref, near_ref, out_ref):
    members = vm_ref.shape[0]
    out_ref[:members] = vm_ref[...]
    out_ref[members:] = near_ref[...]


def stack_kernel(near_ref, *refs):
    out_ref = refs[-1]
    rows = near_ref.shape[0]
    out_ref[:rows] = near_ref[...]
    for place, ref in enumerate(refs[:-1]):
        out_ref[(place + 1) * rows : (place + 2) * rows] = ref[ref.shape[0] - rows :]


def pick_kernel(middle_ref, k_ref, near_ref, members_ref):
    rows = k_ref.shape[0]
    members = rows // MIDDLE_DILATION
    members_ref[members:] = near_ref[...]
    group = lax.broadcasted_iota(jnp.int32, (members, rows), 0)
    token = lax.broadcasted_iota(jnp.int32, (members, rows), 1)
    offset = token - MIDDLE_DILATION * group
    for head in range(HEAD_COUNT):
        columns = head_columns(head)
        chosen = one_hot(offset == middle_ref[head])
        members_ref[:members, columns] = dot(chosen, k_ref[:, columns]).astype(jnp.bfloat16)


def dot_keys(q, keys):
    return lax.dot_general(q, keys, (((1,), (1,)), ((), ())), preferred_element_type=jnp.float32)


def dot_rows(a, b):
    return lax.dot_general(a, b, (((0,), (0,)), ((), ())), preferred_element_type=jnp.float32)


def side_by_side(columns):
    rows = columns[0].shape[0]
    lane = lax.broadcasted_iota(jnp.int32, (rows, LANES), 1)
    result = jnp.zeros((rows, LANES), jnp.float32)
    for place, column in enumerate(columns):
        result = jnp.where(lane == place, column, result)
    return result


def member_rows(rows, shift):
    row = lax.broadcasted_iota(jnp.int32, (rows, 1), 0)
    return (row & (MIDDLE_DILATION - 1)) == shift


def lane_tiles(part):
    return [part[:, i : i + LANES] for i in range(0, part.shape[1], LANES)]


def weights(part, top):
    return jnp.exp2((part - top) * EXP2_SCALE)


def first_kernel(first, middle_ref, q_ref, k_ref, v_ref, kp_ref, own_ref, other_ref, state_ref, order_ref):
    fill_orders(order_ref)
    rows = q_ref.shape[0]
    members = rows // MIDDLE_DILATION
    column = lax.broadcasted_iota(jnp.int32, (1, rows), 1)
    tops, totals = [], []
    heads = other_ref.shape[0]
    for place in range(heads):
        columns = head_columns(first + place)
        shift = middle_ref[first + place]
        q = q_ref[:, columns]
        own = dot_keys(q, k_ref[:, columns])
        other_keys = dot(order_ref[shift], kp_ref[:, columns]).astype(jnp.bfloat16)
        other = dot_keys(q, other_keys)
        top = functools.reduce(jnp.maximum, lane_tiles(own) + lane_tiles(other))
        top = jnp.max(top, axis=1, keepdims=True)
        row_is_member = member_rows(rows, shift)
        own, other = weights(own, top), weights(other, top)
        own_member = row_is_member & ((column & (MIDDLE_DILATION - 1)) == shift)
        own = jnp.where(own_member, own + own, own)
        twice = other[:, :LANES]
        twice = jnp.where(row_is_member & (column[:, :LANES] < members), twice + twice, twice)
        other = jnp.concatenate([twice, other[:, LANES:]], axis=1)
        total = functools.reduce(jnp.add, lane_tiles(own) + lane_tiles(other))
        tops.append(top)
        totals.append(jnp.sum(total, axis=1, keepdims=True))
        own_ref[:, head_columns(place)] = dot(own.astype(jnp.bfloat16), v_ref[:, columns])
        other_ref[place] = other.astype(jnp.bfloat16)
    state_ref[...] = side_by_side(tops + totals)


def extra_kernel(
    middle_ref, coarse_ref, q_ref, state_a_ref, state_b_ref, cross_ref, diagonal_k_ref, diagonal_v_ref, mine_ref,
    other_ref, sum_ref, share_ref,
):
    rows = q_ref.shape[0]
    members = rows // MIDDLE_DILATION
    half = HEAD_COUNT // 2
    far_rows, coarse_rows = 2 * members, 2 * mine_ref.shape[0]
    token = lax.broadcasted_iota(jnp.int32, (1, rows), 1)
    is_key = (lax.broadcasted_iota(jnp.int32, (coarse_rows, 1), 0) & 1) == 0
    states = [ref[...].T for ref in (state_a_ref, state_b_ref)]
    shares = []
    for head in range(HEAD_COUNT):
        columns = head_columns(head)
        state, place = states[head // half], head % half
        pairs = [mine_ref[:, columns], other_ref[:, columns]]
        keys = jnp.concatenate([cross_ref[:members, columns], diagonal_k_ref[:members, columns], *pairs], axis=0)
        values = jnp.concatenate([cross_ref[members:, columns], diagonal_v_ref[:members, columns], *pairs], axis=0)
        scores = dot_keys(keys, q_ref[:, columns])
        far = jnp.where((token & (MIDDLE_DILATION - 1)) == middle_ref[head], scores[:far_rows], MASKED)
        coarse = jnp.where(is_key & (token == coarse_ref[head]), scores[far_rows:], MASKED)
        before = state[place : place + 1]
        top = jnp.maximum(before, jnp.max(far, axis=0, keepdims=True))
        top = jnp.maximum(top, jnp.max(coarse, axis=0, keepdims=True))
        far, coarse = weights(far, top), weights(coarse, top)
        kept = weights(before, top)
        total = kept * state[half + place : half + place + 1]
        total += jnp.sum(far, axis=0, keepdims=True) + jnp.sum(coarse, axis=0, keepdims=True)
        inverse = 1.0 / total
        shifted = pltpu.roll(coarse, 1, 0)
        mixed = jnp.concatenate([(far * inverse).astype(jnp.bfloat16), (shifted * inverse).astype(jnp.bfloat16)], axis=0)
        sum_ref[:, columns] = dot_rows(mixed, values)
        shares.append(kept * inverse)
    share_ref[:, :HEAD_COUNT] = jnp.concatenate(shares, axis=0).T


def finish_kernel(heads, sum_ref, share_ref, own_a_ref, own_b_ref, other_a_ref, other_b_ref, vm_ref, vr_ref, *rest):
    out_ref, ready_ref, semaphores = rest[-3:]
    members = vr_ref.shape[0] // (MIDDLE_DILATION - 1)
    half = HEAD_COUNT // 2
    copies = []
    for place, head in enumerate(heads):
        columns = head_columns(head)
        own_ref, other_ref = ((own_a_ref, other_a_ref), (own_b_ref, other_b_ref))[head // half]
        values = jnp.concatenate([vm_ref[:members, columns], vr_ref[:, head_columns(place)]], axis=0)
        result = own_ref[:, head_columns(head % half)] + dot(other_ref[head % half], values)
        result = sum_ref[:, columns] + share_ref[:, head : head + 1] * result
        ready_ref[place] = result.astype(jnp.bfloat16)
        copies.append(pltpu.make_async_copy(ready_ref.at[place], out_ref.at[:, columns], semaphores.at[place]))
        copies[-1].start()
    for copy in copies:
        copy.wait()


def in_hbm(array):
    return pltpu.with_memory_space_constraint(array, pltpu.HBM)


def cost():
    return pl.CostEstimate(flops=0, bytes_accessed=0, transcendentals=0)


def gather_upper(value, axis):
    size = lax.axis_size(axis)
    assert size & (size - 1) == 0
    bits = [2**j for j in range(1, size.bit_length() - 1)]
    for step in [bits[j : j + 2] for j in range(0, len(bits), 2)]:
        masks = step + [sum(step)] if len(step) == 2 else step
        value = jnp.concatenate([value] + [partner(value, axis, mask) for mask in masks], axis=0)
    return value


def on_device(query, keys, values, middle_head_shift, coarse_head_shift):
    rows, width = query.shape
    members = rows // MIDDLE_DILATION
    near_rows = lax.axis_size("outer")
    half = HEAD_COUNT // 2
    bf16, f32 = jnp.bfloat16, jnp.float32
    smem = pl.BlockSpec(memory_space=pltpu.SMEM)
    vmem = pl.BlockSpec(memory_space=pltpu.VMEM)
    anywhere = pl.BlockSpec(memory_space=pl.ANY)
    params = pltpu.CompilerParams(vmem_limit_bytes=16 * 1024 * 1024)
    orders = pltpu.VMEM((MIDDLE_DILATION, rows, rows), bf16)

    def call(kernel, name, *args, **options):
        return pl.pallas_call(kernel, name=name, compiler_params=params, cost_estimate=cost(), **options)(*args)

    other_keys = partner(keys, "inner", 1)
    q, k, v, own_members, own_vm, *own_vr, coarse = call(
        functools.partial(prepare_kernel, CHUNKS),
        "prepare",
        middle_head_shift, coarse_head_shift, in_hbm(query), in_hbm(keys), in_hbm(values),
        out_shape=[
            *[pltpu.VMEM((rows, width), bf16)] * 3,
            pltpu.VMEM((2 * members, width), bf16),
            pltpu.VMEM((members, width), bf16),
            *[pltpu.VMEM((rows - members, c * HEAD_FEATURES), bf16) for c in CHUNKS],
            pltpu.VMEM((2, width), bf16),
        ],
        in_specs=[smem, smem, anywhere, anywhere, anywhere],
        out_specs=[vmem] * (6 + len(CHUNKS)),
        scratch_shapes=[orders, pltpu.SemaphoreType.DMA((3,))],
    )
    cross = partner(own_members, "inner", 2)
    near = gather_upper(coarse, "outer")
    own_vm = call(
        join_kernel,
        "join",
        own_vm, near,
        out_shape=pltpu.VMEM((members + near_rows, width), bf16),
        in_specs=[vmem, vmem],
        out_specs=vmem,
    )
    other_vm = partner(own_vm, "inner", 1)
    cross, own_vr = lax.optimization_barrier((cross, own_vr))
    other_vr = [partner(piece, "inner", 1) for piece in own_vr]
    other_km = call(
        pick_kernel,
        "pick",
        middle_head_shift, other_keys, near,
        out_shape=pltpu.VMEM((members + near_rows, width), bf16),
        in_specs=[smem, vmem, vmem],
        out_specs=vmem,
    )
    diagonal_k = partner(other_km, "inner", 2)
    other_keys = lax.optimization_barrier((other_keys, other_km))[0]

    def first_part(first, query):
        return call(
            functools.partial(first_kernel, first),
            "first",
            middle_head_shift, query, k, v, other_keys,
            out_shape=[
                pltpu.VMEM((rows, half * HEAD_FEATURES), f32),
                pltpu.VMEM((half, rows, rows), bf16),
                pltpu.VMEM((rows, LANES), f32),
            ],
            in_specs=[smem] + [vmem] * 4,
            out_specs=[vmem] * 3,
            scratch_shapes=[orders],
        )

    own_a, weights_a, state_a = first_part(0, q)
    diagonal_v = partner(lax.optimization_barrier((other_vm, state_a))[0], "inner", 2)
    own_b, weights_b, state_b = first_part(half, lax.optimization_barrier((q, state_a, diagonal_k))[0])
    diagonal_v = lax.optimization_barrier((diagonal_v, state_b))[0]
    mine = call(
        stack_kernel,
        "stack",
        near, other_vm, diagonal_k, diagonal_v,
        out_shape=pltpu.VMEM((lax.axis_size("inner") * near_rows, width), bf16),
        in_specs=[vmem] * 4,
        out_specs=vmem,
    )
    extra_sum, share = call(
        extra_kernel,
        "extra",
        middle_head_shift, coarse_head_shift, q, state_a, state_b, cross, diagonal_k, diagonal_v, mine,
        partner(mine, "outer", 1),
        out_shape=[pltpu.VMEM((rows, width), f32), pltpu.VMEM((rows, LANES), f32)],
        in_specs=[smem, smem] + [vmem] * 8,
        out_specs=[vmem] * 2,
    )

    out = []
    first = 0
    for chunk, vr in zip(CHUNKS, other_vr):
        args = [extra_sum, share, own_a, own_b, weights_a, weights_b, other_vm, vr]
        out = [
            call(
                functools.partial(finish_kernel, range(first, first + chunk)),
                "finish",
                *args, *out,
                out_shape=jax.ShapeDtypeStruct((rows, width), bf16),
                in_specs=[vmem] * len(args) + [anywhere] * len(out),
                out_specs=anywhere,
                input_output_aliases={len(args): 0} if out else {},
                scratch_shapes=[pltpu.VMEM((chunk, rows, HEAD_FEATURES), bf16), pltpu.SemaphoreType.DMA((chunk,))],
            )
        ]
        first += chunk
    return out[0]


def solution(mesh):
    placed = (
        P(("outer", "inner"), None),
        P(("outer", "inner"), None),
        P(("outer", "inner"), None),
        P(),
        P(),
    )
    return jax.shard_map(
        on_device,
        mesh=mesh,
        in_specs=placed,
        out_specs=P(("outer", "inner"), None),
        check_vma=False,
    )
```

```python
import functools

import jax
import jax.numpy as jnp
from jax import lax
from jax.experimental import pallas as pl
from jax.experimental.pallas import tpu as pltpu
from jax.sharding import PartitionSpec as P

HEAD_COUNT = 16
HEAD_FEATURES = 128
MIDDLE_DILATION = 4
CHUNKS = (14, 2)
LANES = 128
SUBLANES = 16
EXP2_SCALE = HEAD_FEATURES ** (-0.5) * 1.4426950408889634
MASKED = -1e30


def partner(value, axis, mask):
    pairs = [(source, source ^ mask) for source in range(lax.axis_size(axis))]
    return lax.ppermute(value, axis, pairs)


def partner_elsewhere(value, inner_mask):
    outer = lax.axis_size("outer")
    outer_mask = 2 if outer > 2 else 0
    pairs = []
    for i in range(lax.axis_size("inner")):
        for o in range(outer):
            pairs.append((i * outer + o, (i ^ inner_mask) * outer + (o ^ outer_mask)))
    return lax.ppermute(value, ("inner", "outer"), pairs)


def one_hot(mask):
    return mask.astype(jnp.float32).astype(jnp.bfloat16)


def fill_orders(order_ref):
    rows = order_ref.shape[1]
    members = rows // MIDDLE_DILATION
    group = lax.broadcasted_iota(jnp.int32, (members, rows), 0)
    token = lax.broadcasted_iota(jnp.int32, (members, rows), 1)
    for place in range(MIDDLE_DILATION):
        block = one_hot(token == MIDDLE_DILATION * group + place)
        for shift in range(MIDDLE_DILATION):
            slot = (place - shift) % MIDDLE_DILATION
            order_ref[shift, slot * members : (slot + 1) * members] = block


def dot(a, b):
    return jnp.dot(a, b, preferred_element_type=jnp.float32)


def head_columns(head):
    return slice(head * HEAD_FEATURES, (head + 1) * HEAD_FEATURES)


def prepare_kernel(chunks, middle_ref, coarse_ref, q_hbm, k_hbm, v_hbm, *rest):
    q_ref, k_ref, v_ref, members_ref, vm_ref, *vr_refs, coarse_out_ref, order_ref, semaphores = rest
    pairs = ((k_hbm, k_ref), (v_hbm, v_ref), (q_hbm, q_ref))
    copies = [pltpu.make_async_copy(*pair, semaphores.at[i]) for i, pair in enumerate(pairs)]
    for copy in copies:
        copy.start()
    rows = k_ref.shape[0]
    members = rows // MIDDLE_DILATION
    fill_orders(order_ref)
    token = lax.broadcasted_iota(jnp.int32, (SUBLANES, rows), 1)
    first_row = lax.broadcasted_iota(jnp.int32, (SUBLANES, rows), 0) == 0
    second_row = lax.broadcasted_iota(jnp.int32, (SUBLANES, rows), 0) == 1
    copies[0].wait()
    copies[1].wait()
    head = 0
    for chunk, vr_ref in zip(chunks, vr_refs):
        for place in range(chunk):
            columns = head_columns(head)
            order = order_ref[middle_ref[head]]
            k, v = k_ref[:, columns], v_ref[:, columns]
            v_ordered = dot(order, v).astype(jnp.bfloat16)
            members_ref[:members, columns] = dot(order[:members], k).astype(jnp.bfloat16)
            members_ref[members:, columns] = v_ordered[:members]
            vm_ref[:, columns] = v_ordered[:members]
            vr_ref[:, head_columns(place)] = v_ordered[members:]
            chosen = token == coarse_ref[head]
            picked = dot(one_hot(chosen & first_row), k) + dot(one_hot(chosen & second_row), v)
            coarse_out_ref[:, columns] = picked[:2].astype(jnp.bfloat16)
            head += 1
    copies[2].wait()


def pick_kernel(middle_ref, k_ref, members_ref):
    rows = k_ref.shape[0]
    members = rows // MIDDLE_DILATION
    group = lax.broadcasted_iota(jnp.int32, (members, rows), 0)
    token = lax.broadcasted_iota(jnp.int32, (members, rows), 1)
    offset = token - MIDDLE_DILATION * group
    for head in range(HEAD_COUNT):
        columns = head_columns(head)
        chosen = one_hot(offset == middle_ref[head])
        members_ref[:, columns] = dot(chosen, k_ref[:, columns]).astype(jnp.bfloat16)


def dot_keys(q, keys):
    return lax.dot_general(q, keys, (((1,), (1,)), ((), ())), preferred_element_type=jnp.float32)


def dot_rows(a, b):
    return lax.dot_general(a, b, (((0,), (0,)), ((), ())), preferred_element_type=jnp.float32)


def side_by_side(columns):
    rows = columns[0].shape[0]
    lane = lax.broadcasted_iota(jnp.int32, (rows, LANES), 1)
    result = jnp.zeros((rows, LANES), jnp.float32)
    for place, column in enumerate(columns):
        result = jnp.where(lane == place, column, result)
    return result


def member_rows(rows, shift):
    row = lax.broadcasted_iota(jnp.int32, (rows, 1), 0)
    return (row & (MIDDLE_DILATION - 1)) == shift


def lane_tiles(part):
    return [part[:, i : i + LANES] for i in range(0, part.shape[1], LANES)]


def weights(part, top):
    return jnp.exp2((part - top) * EXP2_SCALE)


def first_kernel(first, middle_ref, q_ref, k_ref, v_ref, kp_ref, own_ref, other_ref, state_ref, order_ref):
    fill_orders(order_ref)
    rows = q_ref.shape[0]
    members = rows // MIDDLE_DILATION
    column = lax.broadcasted_iota(jnp.int32, (1, rows), 1)
    tops, totals = [], []
    heads = other_ref.shape[0]
    for place in range(heads):
        columns = head_columns(first + place)
        shift = middle_ref[first + place]
        q = q_ref[:, columns]
        own = dot_keys(q, k_ref[:, columns])
        other_keys = dot(order_ref[shift], kp_ref[:, columns]).astype(jnp.bfloat16)
        other = dot_keys(q, other_keys)
        top = functools.reduce(jnp.maximum, lane_tiles(own) + lane_tiles(other))
        top = jnp.max(top, axis=1, keepdims=True)
        row_is_member = member_rows(rows, shift)
        own, other = weights(own, top), weights(other, top)
        own_member = row_is_member & ((column & (MIDDLE_DILATION - 1)) == shift)
        own = jnp.where(own_member, own + own, own)
        twice = other[:, :LANES]
        twice = jnp.where(row_is_member & (column[:, :LANES] < members), twice + twice, twice)
        other = jnp.concatenate([twice, other[:, LANES:]], axis=1)
        total = functools.reduce(jnp.add, lane_tiles(own) + lane_tiles(other))
        tops.append(top)
        totals.append(jnp.sum(total, axis=1, keepdims=True))
        own_ref[:, head_columns(place)] = dot(own.astype(jnp.bfloat16), v_ref[:, columns])
        other_ref[place] = other.astype(jnp.bfloat16)
    state_ref[...] = side_by_side(tops + totals)


def extra_kernel(
    middle_ref, coarse_ref, q_ref, state_a_ref, state_b_ref, cross_ref, diagonal_k_ref, diagonal_v_ref, mine_ref,
    other_ref, sum_ref, share_ref,
):
    rows = q_ref.shape[0]
    members = rows // MIDDLE_DILATION
    half = HEAD_COUNT // 2
    far_rows, coarse_rows = 2 * members, 2 * mine_ref.shape[0]
    token = lax.broadcasted_iota(jnp.int32, (1, rows), 1)
    is_key = (lax.broadcasted_iota(jnp.int32, (coarse_rows, 1), 0) & 1) == 0
    states = [ref[...].T for ref in (state_a_ref, state_b_ref)]
    shares = []
    for head in range(HEAD_COUNT):
        columns = head_columns(head)
        state, place = states[head // half], head % half
        pairs = [mine_ref[:, columns], other_ref[:, columns]]
        keys = jnp.concatenate([cross_ref[:members, columns], diagonal_k_ref[:, columns], *pairs], axis=0)
        values = jnp.concatenate([cross_ref[members:, columns], diagonal_v_ref[:, columns], *pairs], axis=0)
        scores = dot_keys(keys, q_ref[:, columns])
        far = jnp.where((token & (MIDDLE_DILATION - 1)) == middle_ref[head], scores[:far_rows], MASKED)
        coarse = jnp.where(is_key & (token == coarse_ref[head]), scores[far_rows:], MASKED)
        before = state[place : place + 1]
        top = jnp.maximum(before, jnp.max(far, axis=0, keepdims=True))
        top = jnp.maximum(top, jnp.max(coarse, axis=0, keepdims=True))
        far, coarse = weights(far, top), weights(coarse, top)
        kept = weights(before, top)
        total = kept * state[half + place : half + place + 1]
        total += jnp.sum(far, axis=0, keepdims=True) + jnp.sum(coarse, axis=0, keepdims=True)
        inverse = 1.0 / total
        shifted = pltpu.roll(coarse, 1, 0)
        mixed = jnp.concatenate([(far * inverse).astype(jnp.bfloat16), (shifted * inverse).astype(jnp.bfloat16)], axis=0)
        sum_ref[:, columns] = dot_rows(mixed, values)
        shares.append(kept * inverse)
    share_ref[:, :HEAD_COUNT] = jnp.concatenate(shares, axis=0).T


def finish_kernel(heads, sum_ref, share_ref, own_a_ref, own_b_ref, other_a_ref, other_b_ref, vm_ref, vr_ref, *rest):
    out_ref, ready_ref, semaphores = rest[-3:]
    half = HEAD_COUNT // 2
    copies = []
    for place, head in enumerate(heads):
        columns = head_columns(head)
        own_ref, other_ref = ((own_a_ref, other_a_ref), (own_b_ref, other_b_ref))[head // half]
        values = jnp.concatenate([vm_ref[:, columns], vr_ref[:, head_columns(place)]], axis=0)
        result = own_ref[:, head_columns(head % half)] + dot(other_ref[head % half], values)
        result = sum_ref[:, columns] + share_ref[:, head : head + 1] * result
        ready_ref[place] = result.astype(jnp.bfloat16)
        copies.append(pltpu.make_async_copy(ready_ref.at[place], out_ref.at[:, columns], semaphores.at[place]))
        copies[-1].start()
    for copy in copies:
        copy.wait()


def in_hbm(array):
    return pltpu.with_memory_space_constraint(array, pltpu.HBM)


def cost():
    return pl.CostEstimate(flops=0, bytes_accessed=0, transcendentals=0)


def gather_upper(value, axis):
    size = lax.axis_size(axis)
    assert size & (size - 1) == 0
    bits = [2**j for j in range(1, size.bit_length() - 1)]
    for step in [bits[j : j + 2] for j in range(0, len(bits), 2)]:
        masks = step + [sum(step)] if len(step) == 2 else step
        value = jnp.concatenate([value] + [partner(value, axis, mask) for mask in masks], axis=0)
    return value


def on_device(query, keys, values, middle_head_shift, coarse_head_shift):
    rows, width = query.shape
    members = rows // MIDDLE_DILATION
    half = HEAD_COUNT // 2
    bf16, f32 = jnp.bfloat16, jnp.float32
    smem = pl.BlockSpec(memory_space=pltpu.SMEM)
    vmem = pl.BlockSpec(memory_space=pltpu.VMEM)
    anywhere = pl.BlockSpec(memory_space=pl.ANY)
    params = pltpu.CompilerParams(vmem_limit_bytes=16 * 1024 * 1024)
    orders = pltpu.VMEM((MIDDLE_DILATION, rows, rows), bf16)

    def call(kernel, name, *args, **options):
        return pl.pallas_call(kernel, name=name, compiler_params=params, cost_estimate=cost(), **options)(*args)

    other_keys = partner(keys, "inner", 1)
    q, k, v, own_members, own_vm, *own_vr, coarse = call(
        functools.partial(prepare_kernel, CHUNKS),
        "prepare",
        middle_head_shift, coarse_head_shift, in_hbm(query), in_hbm(keys), in_hbm(values),
        out_shape=[
            *[pltpu.VMEM((rows, width), bf16)] * 3,
            pltpu.VMEM((2 * members, width), bf16),
            pltpu.VMEM((members, width), bf16),
            *[pltpu.VMEM((rows - members, c * HEAD_FEATURES), bf16) for c in CHUNKS],
            pltpu.VMEM((2, width), bf16),
        ],
        in_specs=[smem, smem, anywhere, anywhere, anywhere],
        out_specs=[vmem] * (6 + len(CHUNKS)),
        scratch_shapes=[orders, pltpu.SemaphoreType.DMA((3,))],
    )
    cross = partner(own_members, "inner", 2)
    other_vm = partner(own_vm, "inner", 1)
    coarse = jnp.concatenate([coarse, partner_elsewhere(coarse, 1)], axis=0)
    coarse = gather_upper(coarse, "outer")
    coarse, own_vr = lax.optimization_barrier((coarse, own_vr))
    other_vr = [partner(piece, "inner", 1) for piece in own_vr]
    other_km = call(
        pick_kernel,
        "pick",
        middle_head_shift, lax.optimization_barrier((other_keys, cross))[0],
        out_shape=pltpu.VMEM((members, width), bf16),
        in_specs=[smem, vmem],
        out_specs=vmem,
    )
    diagonal_k = partner(other_km, "inner", 2)
    mine = jnp.concatenate([coarse, partner_elsewhere(coarse, 2)], axis=0)
    other_cores = partner(mine, "outer", 1)
    other_keys = lax.optimization_barrier((other_keys, other_km, other_cores))[0]

    def first_part(first, query):
        return call(
            functools.partial(first_kernel, first),
            "first",
            middle_head_shift, query, k, v, other_keys,
            out_shape=[
                pltpu.VMEM((rows, half * HEAD_FEATURES), f32),
                pltpu.VMEM((half, rows, rows), bf16),
                pltpu.VMEM((rows, LANES), f32),
            ],
            in_specs=[smem] + [vmem] * 4,
            out_specs=[vmem] * 3,
            scratch_shapes=[orders],
        )

    own_a, weights_a, state_a = first_part(0, q)
    diagonal_v = partner(lax.optimization_barrier((other_vm, state_a))[0], "inner", 2)
    own_b, weights_b, state_b = first_part(half, lax.optimization_barrier((q, state_a, diagonal_k))[0])
    extra_sum, share = call(
        extra_kernel,
        "extra",
        middle_head_shift, coarse_head_shift, q, state_a, state_b, cross, diagonal_k, diagonal_v, mine,
        other_cores,
        out_shape=[pltpu.VMEM((rows, width), f32), pltpu.VMEM((rows, LANES), f32)],
        in_specs=[smem, smem] + [vmem] * 8,
        out_specs=[vmem] * 2,
    )

    out = []
    first = 0
    for chunk, vr in zip(CHUNKS, other_vr):
        args = [extra_sum, share, own_a, own_b, weights_a, weights_b, other_vm, vr]
        out = [
            call(
                functools.partial(finish_kernel, range(first, first + chunk)),
                "finish",
                *args, *out,
                out_shape=jax.ShapeDtypeStruct((rows, width), bf16),
                in_specs=[vmem] * len(args) + [anywhere] * len(out),
                out_specs=anywhere,
                input_output_aliases={len(args): 0} if out else {},
                scratch_shapes=[pltpu.VMEM((chunk, rows, HEAD_FEATURES), bf16), pltpu.SemaphoreType.DMA((chunk,))],
            )
        ]
        first += chunk
    return out[0]


def solution(mesh):
    placed = (
        P(("outer", "inner"), None),
        P(("outer", "inner"), None),
        P(("outer", "inner"), None),
        P(),
        P(),
    )
    return jax.shard_map(
        on_device,
        mesh=mesh,
        in_specs=placed,
        out_specs=P(("outer", "inner"), None),
        check_vma=False,
    )
```

```python
import functools

import jax
import jax.numpy as jnp
from jax import lax
from jax.experimental import pallas as pl
from jax.experimental.pallas import tpu as pltpu
from jax.sharding import PartitionSpec as P

HEAD_COUNT = 16
HEAD_FEATURES = 128
MIDDLE_DILATION = 4
CHUNKS = (12, 4)
LANES = 128
SUBLANES = 16
EXP2_SCALE = HEAD_FEATURES ** (-0.5) * 1.4426950408889634
MASKED = -1e30


def partner(value, axis, mask):
    pairs = [(source, source ^ mask) for source in range(lax.axis_size(axis))]
    return lax.ppermute(value, axis, pairs)


def partner_elsewhere(value, inner_mask):
    outer = lax.axis_size("outer")
    outer_mask = 2 if outer > 2 else 0
    pairs = []
    for i in range(lax.axis_size("inner")):
        for o in range(outer):
            pairs.append((i * outer + o, (i ^ inner_mask) * outer + (o ^ outer_mask)))
    return lax.ppermute(value, ("inner", "outer"), pairs)


def one_hot(mask):
    return mask.astype(jnp.float32).astype(jnp.bfloat16)


def fill_orders(order_ref):
    rows = order_ref.shape[1]
    members = rows // MIDDLE_DILATION
    group = lax.broadcasted_iota(jnp.int32, (members, rows), 0)
    token = lax.broadcasted_iota(jnp.int32, (members, rows), 1)
    for place in range(MIDDLE_DILATION):
        block = one_hot(token == MIDDLE_DILATION * group + place)
        for shift in range(MIDDLE_DILATION):
            slot = (place - shift) % MIDDLE_DILATION
            order_ref[shift, slot * members : (slot + 1) * members] = block


def dot(a, b):
    return jnp.dot(a, b, preferred_element_type=jnp.float32)


def head_columns(head):
    return slice(head * HEAD_FEATURES, (head + 1) * HEAD_FEATURES)


def prepare_kernel(chunks, middle_ref, coarse_ref, q_hbm, k_hbm, v_hbm, *rest):
    q_ref, k_ref, v_ref, members_ref, vm_ref, *vr_refs, coarse_out_ref, order_ref, semaphores = rest
    pairs = ((k_hbm, k_ref), (v_hbm, v_ref), (q_hbm, q_ref))
    copies = [pltpu.make_async_copy(*pair, semaphores.at[i]) for i, pair in enumerate(pairs)]
    for copy in copies:
        copy.start()
    rows = k_ref.shape[0]
    members = rows // MIDDLE_DILATION
    fill_orders(order_ref)
    token = lax.broadcasted_iota(jnp.int32, (SUBLANES, rows), 1)
    first_row = lax.broadcasted_iota(jnp.int32, (SUBLANES, rows), 0) == 0
    second_row = lax.broadcasted_iota(jnp.int32, (SUBLANES, rows), 0) == 1
    copies[0].wait()
    copies[1].wait()
    head = 0
    for chunk, vr_ref in zip(chunks, vr_refs):
        for place in range(chunk):
            columns = head_columns(head)
            order = order_ref[middle_ref[head]]
            k, v = k_ref[:, columns], v_ref[:, columns]
            v_ordered = dot(order, v).astype(jnp.bfloat16)
            members_ref[:members, columns] = dot(order[:members], k).astype(jnp.bfloat16)
            members_ref[members:, columns] = v_ordered[:members]
            vm_ref[:, columns] = v_ordered[:members]
            vr_ref[:, head_columns(place)] = v_ordered[members:]
            chosen = token == coarse_ref[head]
            picked = dot(one_hot(chosen & first_row), k) + dot(one_hot(chosen & second_row), v)
            coarse_out_ref[:, columns] = picked[:2].astype(jnp.bfloat16)
            head += 1
    copies[2].wait()


def pick_kernel(middle_ref, k_ref, members_ref):
    rows = k_ref.shape[0]
    members = rows // MIDDLE_DILATION
    group = lax.broadcasted_iota(jnp.int32, (members, rows), 0)
    token = lax.broadcasted_iota(jnp.int32, (members, rows), 1)
    offset = token - MIDDLE_DILATION * group
    for head in range(HEAD_COUNT):
        columns = head_columns(head)
        chosen = one_hot(offset == middle_ref[head])
        members_ref[:, columns] = dot(chosen, k_ref[:, columns]).astype(jnp.bfloat16)


def dot_keys(q, keys):
    return lax.dot_general(q, keys, (((1,), (1,)), ((), ())), preferred_element_type=jnp.float32)


def dot_rows(a, b):
    return lax.dot_general(a, b, (((0,), (0,)), ((), ())), preferred_element_type=jnp.float32)


def side_by_side(columns):
    rows = columns[0].shape[0]
    lane = lax.broadcasted_iota(jnp.int32, (rows, LANES), 1)
    result = jnp.zeros((rows, LANES), jnp.float32)
    for place, column in enumerate(columns):
        result = jnp.where(lane == place, column, result)
    return result


def member_rows(rows, shift):
    row = lax.broadcasted_iota(jnp.int32, (rows, 1), 0)
    return (row & (MIDDLE_DILATION - 1)) == shift


def lane_tiles(part):
    return [part[:, i : i + LANES] for i in range(0, part.shape[1], LANES)]


def weights(part, top):
    return jnp.exp2((part - top) * EXP2_SCALE)


def first_kernel(first, middle_ref, q_ref, k_ref, v_ref, kp_ref, own_ref, other_ref, state_ref, order_ref):
    fill_orders(order_ref)
    rows = q_ref.shape[0]
    members = rows // MIDDLE_DILATION
    column = lax.broadcasted_iota(jnp.int32, (1, rows), 1)
    tops, totals = [], []
    heads = other_ref.shape[0]
    for place in range(heads):
        columns = head_columns(first + place)
        shift = middle_ref[first + place]
        q = q_ref[:, columns]
        own = dot_keys(q, k_ref[:, columns])
        other_keys = dot(order_ref[shift], kp_ref[:, columns]).astype(jnp.bfloat16)
        other = dot_keys(q, other_keys)
        top = functools.reduce(jnp.maximum, lane_tiles(own) + lane_tiles(other))
        top = jnp.max(top, axis=1, keepdims=True)
        row_is_member = member_rows(rows, shift)
        own, other = weights(own, top), weights(other, top)
        own_member = row_is_member & ((column & (MIDDLE_DILATION - 1)) == shift)
        own = jnp.where(own_member, own + own, own)
        twice = other[:, :LANES]
        twice = jnp.where(row_is_member & (column[:, :LANES] < members), twice + twice, twice)
        other = jnp.concatenate([twice, other[:, LANES:]], axis=1)
        total = functools.reduce(jnp.add, lane_tiles(own) + lane_tiles(other))
        tops.append(top)
        totals.append(jnp.sum(total, axis=1, keepdims=True))
        own_ref[:, head_columns(place)] = dot(own.astype(jnp.bfloat16), v_ref[:, columns])
        other_ref[place] = other.astype(jnp.bfloat16)
    state_ref[...] = side_by_side(tops + totals)


def extra_kernel(
    middle_ref, coarse_ref, q_ref, state_a_ref, state_b_ref, cross_ref, diagonal_k_ref, diagonal_v_ref, mine_ref,
    other_ref, sum_ref, share_ref,
):
    rows = q_ref.shape[0]
    members = rows // MIDDLE_DILATION
    half = HEAD_COUNT // 2
    far_rows, coarse_rows = 2 * members, 2 * mine_ref.shape[0]
    token = lax.broadcasted_iota(jnp.int32, (1, rows), 1)
    is_key = (lax.broadcasted_iota(jnp.int32, (coarse_rows, 1), 0) & 1) == 0
    states = [ref[...].T for ref in (state_a_ref, state_b_ref)]
    shares = []
    for head in range(HEAD_COUNT):
        columns = head_columns(head)
        state, place = states[head // half], head % half
        pairs = [mine_ref[:, columns], other_ref[:, columns]]
        keys = jnp.concatenate([cross_ref[:members, columns], diagonal_k_ref[:, columns], *pairs], axis=0)
        values = jnp.concatenate([cross_ref[members:, columns], diagonal_v_ref[:, columns], *pairs], axis=0)
        scores = dot_keys(keys, q_ref[:, columns])
        far = jnp.where((token & (MIDDLE_DILATION - 1)) == middle_ref[head], scores[:far_rows], MASKED)
        coarse = jnp.where(is_key & (token == coarse_ref[head]), scores[far_rows:], MASKED)
        before = state[place : place + 1]
        top = jnp.maximum(before, jnp.max(far, axis=0, keepdims=True))
        top = jnp.maximum(top, jnp.max(coarse, axis=0, keepdims=True))
        far, coarse = weights(far, top), weights(coarse, top)
        kept = weights(before, top)
        total = kept * state[half + place : half + place + 1]
        total += jnp.sum(far, axis=0, keepdims=True) + jnp.sum(coarse, axis=0, keepdims=True)
        inverse = 1.0 / total
        shifted = pltpu.roll(coarse, 1, 0)
        mixed = jnp.concatenate([(far * inverse).astype(jnp.bfloat16), (shifted * inverse).astype(jnp.bfloat16)], axis=0)
        sum_ref[:, columns] = dot_rows(mixed, values)
        shares.append(kept * inverse)
    share_ref[:, :HEAD_COUNT] = jnp.concatenate(shares, axis=0).T


def finish_kernel(heads, sum_ref, share_ref, own_a_ref, own_b_ref, other_a_ref, other_b_ref, vm_ref, vr_ref, *rest):
    out_ref, ready_ref, semaphores = rest[-3:]
    half = HEAD_COUNT // 2
    copies = []
    for place, head in enumerate(heads):
        columns = head_columns(head)
        own_ref, other_ref = ((own_a_ref, other_a_ref), (own_b_ref, other_b_ref))[head // half]
        values = jnp.concatenate([vm_ref[:, columns], vr_ref[:, head_columns(place)]], axis=0)
        result = own_ref[:, head_columns(head % half)] + dot(other_ref[head % half], values)
        result = sum_ref[:, columns] + share_ref[:, head : head + 1] * result
        ready_ref[place] = result.astype(jnp.bfloat16)
        copies.append(pltpu.make_async_copy(ready_ref.at[place], out_ref.at[:, columns], semaphores.at[place]))
        copies[-1].start()
    for copy in copies:
        copy.wait()


def in_hbm(array):
    return pltpu.with_memory_space_constraint(array, pltpu.HBM)


def cost():
    return pl.CostEstimate(flops=0, bytes_accessed=0, transcendentals=0)


def gather_upper(value, axis):
    size = lax.axis_size(axis)
    assert size & (size - 1) == 0
    bits = [2**j for j in range(1, size.bit_length() - 1)]
    for step in [bits[j : j + 2] for j in range(0, len(bits), 2)]:
        masks = step + [sum(step)] if len(step) == 2 else step
        value = jnp.concatenate([value] + [partner(value, axis, mask) for mask in masks], axis=0)
    return value


def on_device(query, keys, values, middle_head_shift, coarse_head_shift):
    rows, width = query.shape
    members = rows // MIDDLE_DILATION
    half = HEAD_COUNT // 2
    bf16, f32 = jnp.bfloat16, jnp.float32
    smem = pl.BlockSpec(memory_space=pltpu.SMEM)
    vmem = pl.BlockSpec(memory_space=pltpu.VMEM)
    anywhere = pl.BlockSpec(memory_space=pl.ANY)
    params = pltpu.CompilerParams(vmem_limit_bytes=8 * 1024 * 1024)
    orders = pltpu.VMEM((MIDDLE_DILATION, rows, rows), bf16)

    def call(kernel, name, *args, **options):
        return pl.pallas_call(kernel, name=name, compiler_params=params, cost_estimate=cost(), **options)(*args)

    other_keys = partner(keys, "inner", 1)
    q, k, v, own_members, own_vm, *own_vr, coarse = call(
        functools.partial(prepare_kernel, CHUNKS),
        "prepare",
        middle_head_shift, coarse_head_shift, in_hbm(query), in_hbm(keys), in_hbm(values),
        out_shape=[
            *[pltpu.VMEM((rows, width), bf16)] * 3,
            pltpu.VMEM((2 * members, width), bf16),
            pltpu.VMEM((members, width), bf16),
            *[pltpu.VMEM((rows - members, c * HEAD_FEATURES), bf16) for c in CHUNKS],
            pltpu.VMEM((2, width), bf16),
        ],
        in_specs=[smem, smem, anywhere, anywhere, anywhere],
        out_specs=[vmem] * (6 + len(CHUNKS)),
        scratch_shapes=[orders, pltpu.SemaphoreType.DMA((3,))],
    )
    cross = partner(own_members, "inner", 2)
    near = gather_upper(jnp.concatenate([coarse, partner_elsewhere(coarse, 1)], axis=0), "outer")
    near, own_vm = lax.optimization_barrier((near, own_vm))
    other_vm = partner(own_vm, "inner", 1)
    cross, own_vr = lax.optimization_barrier((cross, own_vr))
    other_vr = [partner(piece, "inner", 1) for piece in own_vr]
    other_km = call(
        pick_kernel,
        "pick",
        middle_head_shift, other_keys,
        out_shape=pltpu.VMEM((members, width), bf16),
        in_specs=[smem, vmem],
        out_specs=vmem,
    )
    diagonal_k = partner(other_km, "inner", 2)
    other_keys = lax.optimization_barrier((other_keys, other_km))[0]

    def first_part(first, query):
        return call(
            functools.partial(first_kernel, first),
            "first",
            middle_head_shift, query, k, v, other_keys,
            out_shape=[
                pltpu.VMEM((rows, half * HEAD_FEATURES), f32),
                pltpu.VMEM((half, rows, rows), bf16),
                pltpu.VMEM((rows, LANES), f32),
            ],
            in_specs=[smem] + [vmem] * 4,
            out_specs=[vmem] * 3,
            scratch_shapes=[orders],
        )

    own_a, weights_a, state_a = first_part(0, q)
    diagonal_v = partner(lax.optimization_barrier((other_vm, state_a))[0], "inner", 2)
    own_b, weights_b, state_b = first_part(half, lax.optimization_barrier((q, state_a, diagonal_k))[0])
    mine = jnp.concatenate([near, partner_elsewhere(near, 2)], axis=0)
    extra_sum, share = call(
        extra_kernel,
        "extra",
        middle_head_shift, coarse_head_shift, q, state_a, state_b, cross, diagonal_k, diagonal_v, mine,
        partner(mine, "outer", 1),
        out_shape=[pltpu.VMEM((rows, width), f32), pltpu.VMEM((rows, LANES), f32)],
        in_specs=[smem, smem] + [vmem] * 8,
        out_specs=[vmem] * 2,
    )

    out = []
    first = 0
    for chunk, vr in zip(CHUNKS, other_vr):
        args = [extra_sum, share, own_a, own_b, weights_a, weights_b, other_vm, vr]
        out = [
            call(
                functools.partial(finish_kernel, range(first, first + chunk)),
                "finish",
                *args, *out,
                out_shape=jax.ShapeDtypeStruct((rows, width), bf16),
                in_specs=[vmem] * len(args) + [anywhere] * len(out),
                out_specs=anywhere,
                input_output_aliases={len(args): 0} if out else {},
                scratch_shapes=[pltpu.VMEM((chunk, rows, HEAD_FEATURES), bf16), pltpu.SemaphoreType.DMA((chunk,))],
            )
        ]
        first += chunk
    return out[0]


def solution(mesh):
    placed = (
        P(("outer", "inner"), None),
        P(("outer", "inner"), None),
        P(("outer", "inner"), None),
        P(),
        P(),
    )
    return jax.shard_map(
        on_device,
        mesh=mesh,
        in_specs=placed,
        out_specs=P(("outer", "inner"), None),
        check_vma=False,
    )
```

```python
import functools

import jax
import jax.numpy as jnp
from jax import lax
from jax.experimental import pallas as pl
from jax.experimental.pallas import tpu as pltpu
from jax.sharding import PartitionSpec as P

HEAD_COUNT = 16
HEAD_FEATURES = 128
MIDDLE_DILATION = 4
CHUNKS = (12, 4)
LANES = 128
SUBLANES = 16
EXP2_SCALE = HEAD_FEATURES ** (-0.5) * 1.4426950408889634
MASKED = -1e30


def partner(value, axis, mask):
    pairs = [(source, source ^ mask) for source in range(lax.axis_size(axis))]
    return lax.ppermute(value, axis, pairs)


def partner_elsewhere(value, inner_mask):
    outer = lax.axis_size("outer")
    outer_mask = 2 if outer > 2 else 0
    pairs = []
    for i in range(lax.axis_size("inner")):
        for o in range(outer):
            pairs.append((i * outer + o, (i ^ inner_mask) * outer + (o ^ outer_mask)))
    return lax.ppermute(value, ("inner", "outer"), pairs)


def one_hot(mask):
    return mask.astype(jnp.float32).astype(jnp.bfloat16)


def fill_orders(order_ref):
    rows = order_ref.shape[1]
    members = rows // MIDDLE_DILATION
    group = lax.broadcasted_iota(jnp.int32, (members, rows), 0)
    token = lax.broadcasted_iota(jnp.int32, (members, rows), 1)
    for place in range(MIDDLE_DILATION):
        block = one_hot(token == MIDDLE_DILATION * group + place)
        for shift in range(MIDDLE_DILATION):
            slot = (place - shift) % MIDDLE_DILATION
            order_ref[shift, slot * members : (slot + 1) * members] = block


def dot(a, b):
    return jnp.dot(a, b, preferred_element_type=jnp.float32)


def head_columns(head):
    return slice(head * HEAD_FEATURES, (head + 1) * HEAD_FEATURES)


def prepare_kernel(chunks, middle_ref, coarse_ref, q_hbm, k_hbm, v_hbm, *rest):
    q_ref, k_ref, v_ref, members_ref, vm_ref, *vr_refs, coarse_out_ref, order_ref, semaphores = rest
    pairs = ((k_hbm, k_ref), (v_hbm, v_ref), (q_hbm, q_ref))
    copies = [pltpu.make_async_copy(*pair, semaphores.at[i]) for i, pair in enumerate(pairs)]
    for copy in copies:
        copy.start()
    rows = k_ref.shape[0]
    members = rows // MIDDLE_DILATION
    fill_orders(order_ref)
    token = lax.broadcasted_iota(jnp.int32, (SUBLANES, rows), 1)
    first_row = lax.broadcasted_iota(jnp.int32, (SUBLANES, rows), 0) == 0
    second_row = lax.broadcasted_iota(jnp.int32, (SUBLANES, rows), 0) == 1
    copies[0].wait()
    copies[1].wait()
    head = 0
    for chunk, vr_ref in zip(chunks, vr_refs):
        for place in range(chunk):
            columns = head_columns(head)
            order = order_ref[middle_ref[head]]
            k, v = k_ref[:, columns], v_ref[:, columns]
            v_ordered = dot(order, v).astype(jnp.bfloat16)
            members_ref[:members, columns] = dot(order[:members], k).astype(jnp.bfloat16)
            members_ref[members:, columns] = v_ordered[:members]
            vm_ref[:, columns] = v_ordered[:members]
            vr_ref[:, head_columns(place)] = v_ordered[members:]
            chosen = token == coarse_ref[head]
            picked = dot(one_hot(chosen & first_row), k) + dot(one_hot(chosen & second_row), v)
            coarse_out_ref[:, columns] = picked[:2].astype(jnp.bfloat16)
            head += 1
    copies[2].wait()


def pick_kernel(middle_ref, k_ref, members_ref):
    rows = k_ref.shape[0]
    members = rows // MIDDLE_DILATION
    group = lax.broadcasted_iota(jnp.int32, (members, rows), 0)
    token = lax.broadcasted_iota(jnp.int32, (members, rows), 1)
    offset = token - MIDDLE_DILATION * group
    for head in range(HEAD_COUNT):
        columns = head_columns(head)
        chosen = one_hot(offset == middle_ref[head])
        members_ref[:, columns] = dot(chosen, k_ref[:, columns]).astype(jnp.bfloat16)


def dot_keys(q, keys):
    return lax.dot_general(q, keys, (((1,), (1,)), ((), ())), preferred_element_type=jnp.float32)


def dot_rows(a, b):
    return lax.dot_general(a, b, (((0,), (0,)), ((), ())), preferred_element_type=jnp.float32)


def side_by_side(columns):
    rows = columns[0].shape[0]
    lane = lax.broadcasted_iota(jnp.int32, (rows, LANES), 1)
    result = jnp.zeros((rows, LANES), jnp.float32)
    for place, column in enumerate(columns):
        result = jnp.where(lane == place, column, result)
    return result


def member_rows(rows, shift):
    row = lax.broadcasted_iota(jnp.int32, (rows, 1), 0)
    return (row & (MIDDLE_DILATION - 1)) == shift


def lane_tiles(part):
    return [part[:, i : i + LANES] for i in range(0, part.shape[1], LANES)]


def weights(part, top):
    return jnp.exp2((part - top) * EXP2_SCALE)


def first_kernel(first, middle_ref, q_ref, k_ref, v_ref, kp_ref, own_ref, other_ref, state_ref, order_ref):
    fill_orders(order_ref)
    rows = q_ref.shape[0]
    members = rows // MIDDLE_DILATION
    column = lax.broadcasted_iota(jnp.int32, (1, rows), 1)
    tops, totals = [], []
    heads = other_ref.shape[0]
    for place in range(heads):
        columns = head_columns(first + place)
        shift = middle_ref[first + place]
        q = q_ref[:, columns]
        own = dot_keys(q, k_ref[:, columns])
        other_keys = dot(order_ref[shift], kp_ref[:, columns]).astype(jnp.bfloat16)
        other = dot_keys(q, other_keys)
        top = functools.reduce(jnp.maximum, lane_tiles(own) + lane_tiles(other))
        top = jnp.max(top, axis=1, keepdims=True)
        row_is_member = member_rows(rows, shift)
        own, other = weights(own, top), weights(other, top)
        own_member = row_is_member & ((column & (MIDDLE_DILATION - 1)) == shift)
        own = jnp.where(own_member, own + own, own)
        twice = other[:, :LANES]
        twice = jnp.where(row_is_member & (column[:, :LANES] < members), twice + twice, twice)
        other = jnp.concatenate([twice, other[:, LANES:]], axis=1)
        total = functools.reduce(jnp.add, lane_tiles(own) + lane_tiles(other))
        tops.append(top)
        totals.append(jnp.sum(total, axis=1, keepdims=True))
        own_ref[:, head_columns(place)] = dot(own.astype(jnp.bfloat16), v_ref[:, columns])
        other_ref[place] = other.astype(jnp.bfloat16)
    state_ref[...] = side_by_side(tops + totals)


def extra_kernel(
    middle_ref, coarse_ref, q_ref, state_a_ref, state_b_ref, cross_ref, diagonal_k_ref, diagonal_v_ref, mine_ref,
    other_ref, sum_ref, share_ref,
):
    rows = q_ref.shape[0]
    members = rows // MIDDLE_DILATION
    half = HEAD_COUNT // 2
    far_rows, coarse_rows = 2 * members, 2 * mine_ref.shape[0]
    token = lax.broadcasted_iota(jnp.int32, (1, rows), 1)
    is_key = (lax.broadcasted_iota(jnp.int32, (coarse_rows, 1), 0) & 1) == 0
    states = [ref[...].T for ref in (state_a_ref, state_b_ref)]
    shares = []
    for head in range(HEAD_COUNT):
        columns = head_columns(head)
        state, place = states[head // half], head % half
        pairs = [mine_ref[:, columns], other_ref[:, columns]]
        keys = jnp.concatenate([cross_ref[:members, columns], diagonal_k_ref[:, columns], *pairs], axis=0)
        values = jnp.concatenate([cross_ref[members:, columns], diagonal_v_ref[:, columns], *pairs], axis=0)
        scores = dot_keys(keys, q_ref[:, columns])
        far = jnp.where((token & (MIDDLE_DILATION - 1)) == middle_ref[head], scores[:far_rows], MASKED)
        coarse = jnp.where(is_key & (token == coarse_ref[head]), scores[far_rows:], MASKED)
        before = state[place : place + 1]
        top = jnp.maximum(before, jnp.max(far, axis=0, keepdims=True))
        top = jnp.maximum(top, jnp.max(coarse, axis=0, keepdims=True))
        far, coarse = weights(far, top), weights(coarse, top)
        kept = weights(before, top)
        total = kept * state[half + place : half + place + 1]
        total += jnp.sum(far, axis=0, keepdims=True) + jnp.sum(coarse, axis=0, keepdims=True)
        inverse = 1.0 / total
        shifted = pltpu.roll(coarse, 1, 0)
        mixed = jnp.concatenate([(far * inverse).astype(jnp.bfloat16), (shifted * inverse).astype(jnp.bfloat16)], axis=0)
        sum_ref[:, columns] = dot_rows(mixed, values)
        shares.append(kept * inverse)
    share_ref[:, :HEAD_COUNT] = jnp.concatenate(shares, axis=0).T


def finish_kernel(heads, sum_ref, share_ref, own_a_ref, own_b_ref, other_a_ref, other_b_ref, vm_ref, vr_ref, *rest):
    out_ref, ready_ref, semaphores = rest[-3:]
    half = HEAD_COUNT // 2
    copies = []
    for place, head in enumerate(heads):
        columns = head_columns(head)
        own_ref, other_ref = ((own_a_ref, other_a_ref), (own_b_ref, other_b_ref))[head // half]
        values = jnp.concatenate([vm_ref[:, columns], vr_ref[:, head_columns(place)]], axis=0)
        result = own_ref[:, head_columns(head % half)] + dot(other_ref[head % half], values)
        result = sum_ref[:, columns] + share_ref[:, head : head + 1] * result
        ready_ref[place] = result.astype(jnp.bfloat16)
        copies.append(pltpu.make_async_copy(ready_ref.at[place], out_ref.at[:, columns], semaphores.at[place]))
        copies[-1].start()
    for copy in copies:
        copy.wait()


def in_hbm(array):
    return pltpu.with_memory_space_constraint(array, pltpu.HBM)


def cost():
    return pl.CostEstimate(flops=0, bytes_accessed=0, transcendentals=0)


def stack_kernel(*refs):
    out_ref, row = refs[-1], 0
    for ref in refs[:-1]:
        out_ref[row : row + ref.shape[0]] = ref[...]
        row += ref.shape[0]


def stack(*pieces):
    vmem = pl.BlockSpec(memory_space=pltpu.VMEM)
    rows = sum(piece.shape[0] for piece in pieces)
    return pl.pallas_call(
        stack_kernel,
        name="stack",
        out_shape=pltpu.VMEM((rows, pieces[0].shape[1]), pieces[0].dtype),
        in_specs=[vmem] * len(pieces),
        out_specs=vmem,
        compiler_params=pltpu.CompilerParams(vmem_limit_bytes=8 * 1024 * 1024),
        cost_estimate=cost(),
    )(*pieces)


def gather_upper(value, axis):
    size = lax.axis_size(axis)
    assert size & (size - 1) == 0
    bits = [2**j for j in range(1, size.bit_length() - 1)]
    for step in [bits[j : j + 2] for j in range(0, len(bits), 2)]:
        masks = step + [sum(step)] if len(step) == 2 else step
        value = stack(value, *[partner(value, axis, mask) for mask in masks])
    return value


def on_device(query, keys, values, middle_head_shift, coarse_head_shift):
    rows, width = query.shape
    members = rows // MIDDLE_DILATION
    half = HEAD_COUNT // 2
    bf16, f32 = jnp.bfloat16, jnp.float32
    smem = pl.BlockSpec(memory_space=pltpu.SMEM)
    vmem = pl.BlockSpec(memory_space=pltpu.VMEM)
    anywhere = pl.BlockSpec(memory_space=pl.ANY)
    params = pltpu.CompilerParams(vmem_limit_bytes=8 * 1024 * 1024)
    orders = pltpu.VMEM((MIDDLE_DILATION, rows, rows), bf16)

    def call(kernel, name, *args, **options):
        return pl.pallas_call(kernel, name=name, compiler_params=params, cost_estimate=cost(), **options)(*args)

    other_keys = partner(keys, "inner", 1)
    q, k, v, own_members, own_vm, *own_vr, coarse = call(
        functools.partial(prepare_kernel, CHUNKS),
        "prepare",
        middle_head_shift, coarse_head_shift, in_hbm(query), in_hbm(keys), in_hbm(values),
        out_shape=[
            *[pltpu.VMEM((rows, width), bf16)] * 3,
            pltpu.VMEM((2 * members, width), bf16),
            pltpu.VMEM((members, width), bf16),
            *[pltpu.VMEM((rows - members, c * HEAD_FEATURES), bf16) for c in CHUNKS],
            pltpu.VMEM((2, width), bf16),
        ],
        in_specs=[smem, smem, anywhere, anywhere, anywhere],
        out_specs=[vmem] * (6 + len(CHUNKS)),
        scratch_shapes=[orders, pltpu.SemaphoreType.DMA((3,))],
    )
    cross = partner(own_members, "inner", 2)
    near = gather_upper(stack(coarse, partner_elsewhere(coarse, 1)), "outer")
    near, own_vm = lax.optimization_barrier((near, own_vm))
    other_vm = partner(own_vm, "inner", 1)
    cross, own_vr = lax.optimization_barrier((cross, own_vr))
    other_vr = [partner(piece, "inner", 1) for piece in own_vr]
    other_km = call(
        pick_kernel,
        "pick",
        middle_head_shift, other_keys,
        out_shape=pltpu.VMEM((members, width), bf16),
        in_specs=[smem, vmem],
        out_specs=vmem,
    )
    diagonal_k = partner(other_km, "inner", 2)
    other_keys = lax.optimization_barrier((other_keys, other_km))[0]

    def first_part(first, query):
        return call(
            functools.partial(first_kernel, first),
            "first",
            middle_head_shift, query, k, v, other_keys,
            out_shape=[
                pltpu.VMEM((rows, half * HEAD_FEATURES), f32),
                pltpu.VMEM((half, rows, rows), bf16),
                pltpu.VMEM((rows, LANES), f32),
            ],
            in_specs=[smem] + [vmem] * 4,
            out_specs=[vmem] * 3,
            scratch_shapes=[orders],
        )

    own_a, weights_a, state_a = first_part(0, q)
    diagonal_v = partner(lax.optimization_barrier((other_vm, state_a))[0], "inner", 2)
    own_b, weights_b, state_b = first_part(half, lax.optimization_barrier((q, state_a, diagonal_k))[0])
    mine = stack(near, partner_elsewhere(near, 2))
    extra_sum, share = call(
        extra_kernel,
        "extra",
        middle_head_shift, coarse_head_shift, q, state_a, state_b, cross, diagonal_k, diagonal_v, mine,
        partner(mine, "outer", 1),
        out_shape=[pltpu.VMEM((rows, width), f32), pltpu.VMEM((rows, LANES), f32)],
        in_specs=[smem, smem] + [vmem] * 8,
        out_specs=[vmem] * 2,
    )

    out = []
    first = 0
    for chunk, vr in zip(CHUNKS, other_vr):
        args = [extra_sum, share, own_a, own_b, weights_a, weights_b, other_vm, vr]
        out = [
            call(
                functools.partial(finish_kernel, range(first, first + chunk)),
                "finish",
                *args, *out,
                out_shape=jax.ShapeDtypeStruct((rows, width), bf16),
                in_specs=[vmem] * len(args) + [anywhere] * len(out),
                out_specs=anywhere,
                input_output_aliases={len(args): 0} if out else {},
                scratch_shapes=[pltpu.VMEM((chunk, rows, HEAD_FEATURES), bf16), pltpu.SemaphoreType.DMA((chunk,))],
            )
        ]
        first += chunk
    return out[0]


def solution(mesh):
    placed = (
        P(("outer", "inner"), None),
        P(("outer", "inner"), None),
        P(("outer", "inner"), None),
        P(),
        P(),
    )
    return jax.shard_map(
        on_device,
        mesh=mesh,
        in_specs=placed,
        out_specs=P(("outer", "inner"), None),
        check_vma=False,
    )
```

```python
import functools

import jax
import jax.numpy as jnp
from jax import lax
from jax.experimental import pallas as pl
from jax.experimental.pallas import tpu as pltpu
from jax.sharding import PartitionSpec as P

HEAD_COUNT = 16
HEAD_FEATURES = 128
MIDDLE_DILATION = 4
CHUNKS = (12, 4)
LANES = 128
SUBLANES = 16
EXP2_SCALE = HEAD_FEATURES ** (-0.5) * 1.4426950408889634
MASKED = -1e30


def partner(value, axis, mask):
    pairs = [(source, source ^ mask) for source in range(lax.axis_size(axis))]
    return lax.ppermute(value, axis, pairs)


def partner_elsewhere(value, inner_mask):
    outer = lax.axis_size("outer")
    outer_mask = 2 if outer > 2 else 0
    pairs = []
    for i in range(lax.axis_size("inner")):
        for o in range(outer):
            pairs.append((i * outer + o, (i ^ inner_mask) * outer + (o ^ outer_mask)))
    return lax.ppermute(value, ("inner", "outer"), pairs)


def one_hot(mask):
    return mask.astype(jnp.float32).astype(jnp.bfloat16)


def fill_orders(order_ref):
    rows = order_ref.shape[1]
    members = rows // MIDDLE_DILATION
    group = lax.broadcasted_iota(jnp.int32, (members, rows), 0)
    token = lax.broadcasted_iota(jnp.int32, (members, rows), 1)
    for place in range(MIDDLE_DILATION):
        block = one_hot(token == MIDDLE_DILATION * group + place)
        for shift in range(MIDDLE_DILATION):
            slot = (place - shift) % MIDDLE_DILATION
            order_ref[shift, slot * members : (slot + 1) * members] = block


def dot(a, b):
    return jnp.dot(a, b, preferred_element_type=jnp.float32)


def head_columns(head):
    return slice(head * HEAD_FEATURES, (head + 1) * HEAD_FEATURES)


def prepare_kernel(chunks, middle_ref, coarse_ref, q_hbm, k_hbm, v_hbm, *rest):
    q_ref, k_ref, v_ref, members_ref, vm_ref, *vr_refs, coarse_out_ref, order_ref, semaphores = rest
    pairs = ((k_hbm, k_ref), (v_hbm, v_ref), (q_hbm, q_ref))
    copies = [pltpu.make_async_copy(*pair, semaphores.at[i]) for i, pair in enumerate(pairs)]
    for copy in copies:
        copy.start()
    rows = k_ref.shape[0]
    members = rows // MIDDLE_DILATION
    fill_orders(order_ref)
    token = lax.broadcasted_iota(jnp.int32, (SUBLANES, rows), 1)
    first_row = lax.broadcasted_iota(jnp.int32, (SUBLANES, rows), 0) == 0
    second_row = lax.broadcasted_iota(jnp.int32, (SUBLANES, rows), 0) == 1
    copies[0].wait()
    copies[1].wait()
    head = 0
    for chunk, vr_ref in zip(chunks, vr_refs):
        for place in range(chunk):
            columns = head_columns(head)
            order = order_ref[middle_ref[head]]
            k, v = k_ref[:, columns], v_ref[:, columns]
            v_ordered = dot(order, v).astype(jnp.bfloat16)
            members_ref[:members, columns] = dot(order[:members], k).astype(jnp.bfloat16)
            members_ref[members:, columns] = v_ordered[:members]
            vm_ref[:, columns] = v_ordered[:members]
            vr_ref[:, head_columns(place)] = v_ordered[members:]
            chosen = token == coarse_ref[head]
            picked = dot(one_hot(chosen & first_row), k) + dot(one_hot(chosen & second_row), v)
            coarse_out_ref[:, columns] = picked[:2].astype(jnp.bfloat16)
            head += 1
    copies[2].wait()


def pick_kernel(middle_ref, k_ref, members_ref):
    rows = k_ref.shape[0]
    members = rows // MIDDLE_DILATION
    group = lax.broadcasted_iota(jnp.int32, (members, rows), 0)
    token = lax.broadcasted_iota(jnp.int32, (members, rows), 1)
    offset = token - MIDDLE_DILATION * group
    for head in range(HEAD_COUNT):
        columns = head_columns(head)
        chosen = one_hot(offset == middle_ref[head])
        members_ref[:, columns] = dot(chosen, k_ref[:, columns]).astype(jnp.bfloat16)


def dot_keys(q, keys):
    return lax.dot_general(q, keys, (((1,), (1,)), ((), ())), preferred_element_type=jnp.float32)


def dot_rows(a, b):
    return lax.dot_general(a, b, (((0,), (0,)), ((), ())), preferred_element_type=jnp.float32)


def side_by_side(columns):
    rows = columns[0].shape[0]
    lane = lax.broadcasted_iota(jnp.int32, (rows, LANES), 1)
    result = jnp.zeros((rows, LANES), jnp.float32)
    for place, column in enumerate(columns):
        result = jnp.where(lane == place, column, result)
    return result


def member_rows(rows, shift):
    row = lax.broadcasted_iota(jnp.int32, (rows, 1), 0)
    return (row & (MIDDLE_DILATION - 1)) == shift


def lane_tiles(part):
    return [part[:, i : i + LANES] for i in range(0, part.shape[1], LANES)]


def weights(part, top):
    return jnp.exp2((part - top) * EXP2_SCALE)


def first_kernel(first, middle_ref, q_ref, k_ref, v_ref, kp_ref, own_ref, other_ref, state_ref, order_ref):
    fill_orders(order_ref)
    rows = q_ref.shape[0]
    members = rows // MIDDLE_DILATION
    column = lax.broadcasted_iota(jnp.int32, (1, rows), 1)
    tops, totals = [], []
    heads = other_ref.shape[0]
    for place in range(heads):
        columns = head_columns(first + place)
        shift = middle_ref[first + place]
        q = q_ref[:, columns]
        own = dot_keys(q, k_ref[:, columns])
        other_keys = dot(order_ref[shift], kp_ref[:, columns]).astype(jnp.bfloat16)
        other = dot_keys(q, other_keys)
        top = functools.reduce(jnp.maximum, lane_tiles(own) + lane_tiles(other))
        top = jnp.max(top, axis=1, keepdims=True)
        row_is_member = member_rows(rows, shift)
        own, other = weights(own, top), weights(other, top)
        own_member = row_is_member & ((column & (MIDDLE_DILATION - 1)) == shift)
        own = jnp.where(own_member, own + own, own)
        twice = other[:, :LANES]
        twice = jnp.where(row_is_member & (column[:, :LANES] < members), twice + twice, twice)
        other = jnp.concatenate([twice, other[:, LANES:]], axis=1)
        total = functools.reduce(jnp.add, lane_tiles(own) + lane_tiles(other))
        tops.append(top)
        totals.append(jnp.sum(total, axis=1, keepdims=True))
        own_ref[:, head_columns(place)] = dot(own.astype(jnp.bfloat16), v_ref[:, columns])
        other_ref[place] = other.astype(jnp.bfloat16)
    state_ref[...] = side_by_side(tops + totals)


def extra_kernel(
    middle_ref, coarse_ref, q_ref, state_a_ref, state_b_ref, cross_ref, diagonal_k_ref, diagonal_v_ref, mine_ref,
    other_ref, sum_ref, share_ref,
):
    rows = q_ref.shape[0]
    members = rows // MIDDLE_DILATION
    half = HEAD_COUNT // 2
    far_rows, coarse_rows = 2 * members, 2 * mine_ref.shape[0]
    token = lax.broadcasted_iota(jnp.int32, (1, rows), 1)
    is_key = (lax.broadcasted_iota(jnp.int32, (coarse_rows, 1), 0) & 1) == 0
    states = [ref[...].T for ref in (state_a_ref, state_b_ref)]
    shares = []
    for head in range(HEAD_COUNT):
        columns = head_columns(head)
        state, place = states[head // half], head % half
        pairs = [mine_ref[:, columns], other_ref[:, columns]]
        keys = jnp.concatenate([cross_ref[:members, columns], diagonal_k_ref[:, columns], *pairs], axis=0)
        values = jnp.concatenate([cross_ref[members:, columns], diagonal_v_ref[:, columns], *pairs], axis=0)
        scores = dot_keys(keys, q_ref[:, columns])
        far = jnp.where((token & (MIDDLE_DILATION - 1)) == middle_ref[head], scores[:far_rows], MASKED)
        coarse = jnp.where(is_key & (token == coarse_ref[head]), scores[far_rows:], MASKED)
        before = state[place : place + 1]
        top = jnp.maximum(before, jnp.max(far, axis=0, keepdims=True))
        top = jnp.maximum(top, jnp.max(coarse, axis=0, keepdims=True))
        far, coarse = weights(far, top), weights(coarse, top)
        kept = weights(before, top)
        total = kept * state[half + place : half + place + 1]
        total += jnp.sum(far, axis=0, keepdims=True) + jnp.sum(coarse, axis=0, keepdims=True)
        inverse = 1.0 / total
        shifted = pltpu.roll(coarse, 1, 0)
        mixed = jnp.concatenate([(far * inverse).astype(jnp.bfloat16), (shifted * inverse).astype(jnp.bfloat16)], axis=0)
        sum_ref[:, columns] = dot_rows(mixed, values)
        shares.append(kept * inverse)
    share_ref[:, :HEAD_COUNT] = jnp.concatenate(shares, axis=0).T


def finish_kernel(heads, sum_ref, share_ref, own_a_ref, own_b_ref, other_a_ref, other_b_ref, vm_ref, vr_ref, *rest):
    out_ref, ready_ref, semaphores = rest[-3:]
    half = HEAD_COUNT // 2
    copies = []
    for place, head in enumerate(heads):
        columns = head_columns(head)
        own_ref, other_ref = ((own_a_ref, other_a_ref), (own_b_ref, other_b_ref))[head // half]
        values = jnp.concatenate([vm_ref[:, columns], vr_ref[:, head_columns(place)]], axis=0)
        result = own_ref[:, head_columns(head % half)] + dot(other_ref[head % half], values)
        result = sum_ref[:, columns] + share_ref[:, head : head + 1] * result
        ready_ref[place] = result.astype(jnp.bfloat16)
        copies.append(pltpu.make_async_copy(ready_ref.at[place], out_ref.at[:, columns], semaphores.at[place]))
        copies[-1].start()
    for copy in copies:
        copy.wait()


def in_hbm(array):
    return pltpu.with_memory_space_constraint(array, pltpu.HBM)


def cost():
    return pl.CostEstimate(flops=0, bytes_accessed=0, transcendentals=0)


def stack_kernel(*refs):
    out_ref, row = refs[-1], 0
    for ref in refs[:-1]:
        out_ref[row : row + ref.shape[0]] = ref[...]
        row += ref.shape[0]


def stack(*pieces):
    vmem = pl.BlockSpec(memory_space=pltpu.VMEM)
    rows = sum(piece.shape[0] for piece in pieces)
    return pl.pallas_call(
        stack_kernel,
        name="stack",
        out_shape=pltpu.VMEM((rows, pieces[0].shape[1]), pieces[0].dtype),
        in_specs=[vmem] * len(pieces),
        out_specs=vmem,
        compiler_params=pltpu.CompilerParams(vmem_limit_bytes=8 * 1024 * 1024),
        cost_estimate=cost(),
    )(*pieces)


def gather_upper(value, axis):
    size = lax.axis_size(axis)
    assert size & (size - 1) == 0
    bits = [2**j for j in range(1, size.bit_length() - 1)]
    for step in [bits[j : j + 2] for j in range(0, len(bits), 2)]:
        masks = step + [sum(step)] if len(step) == 2 else step
        value = stack(value, *[partner(value, axis, mask) for mask in masks])
    return value


def on_device(query, keys, values, middle_head_shift, coarse_head_shift):
    rows, width = query.shape
    members = rows // MIDDLE_DILATION
    half = HEAD_COUNT // 2
    bf16, f32 = jnp.bfloat16, jnp.float32
    smem = pl.BlockSpec(memory_space=pltpu.SMEM)
    vmem = pl.BlockSpec(memory_space=pltpu.VMEM)
    anywhere = pl.BlockSpec(memory_space=pl.ANY)
    params = pltpu.CompilerParams(vmem_limit_bytes=8 * 1024 * 1024)
    orders = pltpu.VMEM((MIDDLE_DILATION, rows, rows), bf16)

    def call(kernel, name, *args, **options):
        return pl.pallas_call(kernel, name=name, compiler_params=params, cost_estimate=cost(), **options)(*args)

    other_keys = partner(keys, "inner", 1)
    q, k, v, own_members, own_vm, *own_vr, coarse = call(
        functools.partial(prepare_kernel, CHUNKS),
        "prepare",
        middle_head_shift, coarse_head_shift, in_hbm(query), in_hbm(keys), in_hbm(values),
        out_shape=[
            *[pltpu.VMEM((rows, width), bf16)] * 3,
            pltpu.VMEM((2 * members, width), bf16),
            pltpu.VMEM((members, width), bf16),
            *[pltpu.VMEM((rows - members, c * HEAD_FEATURES), bf16) for c in CHUNKS],
            pltpu.VMEM((2, width), bf16),
        ],
        in_specs=[smem, smem, anywhere, anywhere, anywhere],
        out_specs=[vmem] * (6 + len(CHUNKS)),
        scratch_shapes=[orders, pltpu.SemaphoreType.DMA((3,))],
    )
    cross = partner(own_members, "inner", 2)
    near = gather_upper(stack(coarse, partner_elsewhere(coarse, 1)), "outer")
    near, own_vm = lax.optimization_barrier((near, own_vm))
    other_vm = partner(own_vm, "inner", 1)
    cross, own_vr = lax.optimization_barrier((cross, own_vr))
    other_vr = [partner(piece, "inner", 1) for piece in own_vr]
    other_km = call(
        pick_kernel,
        "pick",
        middle_head_shift, other_keys,
        out_shape=pltpu.VMEM((members, width), bf16),
        in_specs=[smem, vmem],
        out_specs=vmem,
    )
    diagonal_k = partner(other_km, "inner", 2)
    other_keys = lax.optimization_barrier((other_keys, other_km))[0]

    def first_part(first, query):
        return call(
            functools.partial(first_kernel, first),
            "first",
            middle_head_shift, query, k, v, other_keys,
            out_shape=[
                pltpu.VMEM((rows, half * HEAD_FEATURES), f32),
                pltpu.VMEM((half, rows, rows), bf16),
                pltpu.VMEM((rows, LANES), f32),
            ],
            in_specs=[smem] + [vmem] * 4,
            out_specs=[vmem] * 3,
            scratch_shapes=[orders],
        )

    own_a, weights_a, state_a = first_part(0, q)
    diagonal_v = partner(lax.optimization_barrier((other_vm, state_a))[0], "inner", 2)
    own_b, weights_b, state_b = first_part(half, lax.optimization_barrier((q, state_a, diagonal_k))[0])
    mine = jnp.concatenate([near, partner_elsewhere(near, 2)], axis=0)
    extra_sum, share = call(
        extra_kernel,
        "extra",
        middle_head_shift, coarse_head_shift, q, state_a, state_b, cross, diagonal_k, diagonal_v, mine,
        partner(mine, "outer", 1),
        out_shape=[pltpu.VMEM((rows, width), f32), pltpu.VMEM((rows, LANES), f32)],
        in_specs=[smem, smem] + [vmem] * 8,
        out_specs=[vmem] * 2,
    )

    out = []
    first = 0
    for chunk, vr in zip(CHUNKS, other_vr):
        args = [extra_sum, share, own_a, own_b, weights_a, weights_b, other_vm, vr]
        out = [
            call(
                functools.partial(finish_kernel, range(first, first + chunk)),
                "finish",
                *args, *out,
                out_shape=jax.ShapeDtypeStruct((rows, width), bf16),
                in_specs=[vmem] * len(args) + [anywhere] * len(out),
                out_specs=anywhere,
                input_output_aliases={len(args): 0} if out else {},
                scratch_shapes=[pltpu.VMEM((chunk, rows, HEAD_FEATURES), bf16), pltpu.SemaphoreType.DMA((chunk,))],
            )
        ]
        first += chunk
    return out[0]


def solution(mesh):
    placed = (
        P(("outer", "inner"), None),
        P(("outer", "inner"), None),
        P(("outer", "inner"), None),
        P(),
        P(),
    )
    return jax.shard_map(
        on_device,
        mesh=mesh,
        in_specs=placed,
        out_specs=P(("outer", "inner"), None),
        check_vma=False,
    )
```

```python
import functools

import jax
import jax.numpy as jnp
from jax import lax
from jax.experimental import pallas as pl
from jax.experimental.pallas import tpu as pltpu
from jax.sharding import PartitionSpec as P

HEAD_COUNT = 16
HEAD_FEATURES = 128
MIDDLE_DILATION = 4
CHUNKS = (12, 4)
LANES = 128
SUBLANES = 16
EXP2_SCALE = HEAD_FEATURES ** (-0.5) * 1.4426950408889634
MASKED = -1e30


def partner(value, axis, mask):
    pairs = [(source, source ^ mask) for source in range(lax.axis_size(axis))]
    return lax.ppermute(value, axis, pairs)


def partner_elsewhere(value, inner_mask):
    outer = lax.axis_size("outer")
    outer_mask = 2 if outer > 2 else 0
    pairs = []
    for i in range(lax.axis_size("inner")):
        for o in range(outer):
            pairs.append((i * outer + o, (i ^ inner_mask) * outer + (o ^ outer_mask)))
    return lax.ppermute(value, ("inner", "outer"), pairs)


def one_hot(mask):
    return mask.astype(jnp.float32).astype(jnp.bfloat16)


def fill_orders(order_ref):
    rows = order_ref.shape[1]
    members = rows // MIDDLE_DILATION
    group = lax.broadcasted_iota(jnp.int32, (members, rows), 0)
    token = lax.broadcasted_iota(jnp.int32, (members, rows), 1)
    for place in range(MIDDLE_DILATION):
        block = one_hot(token == MIDDLE_DILATION * group + place)
        for shift in range(MIDDLE_DILATION):
            slot = (place - shift) % MIDDLE_DILATION
            order_ref[shift, slot * members : (slot + 1) * members] = block


def dot(a, b):
    return jnp.dot(a, b, preferred_element_type=jnp.float32)


def head_columns(head):
    return slice(head * HEAD_FEATURES, (head + 1) * HEAD_FEATURES)


def prepare_kernel(chunks, middle_ref, coarse_ref, q_hbm, k_hbm, v_hbm, *rest):
    q_ref, k_ref, v_ref, members_ref, vm_ref, *vr_refs, coarse_out_ref, order_ref, semaphores = rest
    pairs = ((k_hbm, k_ref), (v_hbm, v_ref), (q_hbm, q_ref))
    copies = [pltpu.make_async_copy(*pair, semaphores.at[i]) for i, pair in enumerate(pairs)]
    for copy in copies:
        copy.start()
    rows = k_ref.shape[0]
    members = rows // MIDDLE_DILATION
    fill_orders(order_ref)
    token = lax.broadcasted_iota(jnp.int32, (SUBLANES, rows), 1)
    first_row = lax.broadcasted_iota(jnp.int32, (SUBLANES, rows), 0) == 0
    second_row = lax.broadcasted_iota(jnp.int32, (SUBLANES, rows), 0) == 1
    copies[0].wait()
    copies[1].wait()
    head = 0
    for chunk, vr_ref in zip(chunks, vr_refs):
        for place in range(chunk):
            columns = head_columns(head)
            order = order_ref[middle_ref[head]]
            k, v = k_ref[:, columns], v_ref[:, columns]
            v_ordered = dot(order, v).astype(jnp.bfloat16)
            members_ref[:members, columns] = dot(order[:members], k).astype(jnp.bfloat16)
            members_ref[members:, columns] = v_ordered[:members]
            vm_ref[:, columns] = v_ordered[:members]
            vr_ref[:, head_columns(place)] = v_ordered[members:]
            chosen = token == coarse_ref[head]
            picked = dot(one_hot(chosen & first_row), k) + dot(one_hot(chosen & second_row), v)
            coarse_out_ref[:, columns] = picked[:2].astype(jnp.bfloat16)
            head += 1
    copies[2].wait()


def pick_kernel(middle_ref, k_ref, members_ref):
    rows = k_ref.shape[0]
    members = rows // MIDDLE_DILATION
    group = lax.broadcasted_iota(jnp.int32, (members, rows), 0)
    token = lax.broadcasted_iota(jnp.int32, (members, rows), 1)
    offset = token - MIDDLE_DILATION * group
    for head in range(HEAD_COUNT):
        columns = head_columns(head)
        chosen = one_hot(offset == middle_ref[head])
        members_ref[:, columns] = dot(chosen, k_ref[:, columns]).astype(jnp.bfloat16)


def dot_keys(q, keys):
    return lax.dot_general(q, keys, (((1,), (1,)), ((), ())), preferred_element_type=jnp.float32)


def dot_rows(a, b):
    return lax.dot_general(a, b, (((0,), (0,)), ((), ())), preferred_element_type=jnp.float32)


def side_by_side(columns):
    rows = columns[0].shape[0]
    lane = lax.broadcasted_iota(jnp.int32, (rows, LANES), 1)
    result = jnp.zeros((rows, LANES), jnp.float32)
    for place, column in enumerate(columns):
        result = jnp.where(lane == place, column, result)
    return result


def member_rows(rows, shift):
    row = lax.broadcasted_iota(jnp.int32, (rows, 1), 0)
    return (row & (MIDDLE_DILATION - 1)) == shift


def lane_tiles(part):
    return [part[:, i : i + LANES] for i in range(0, part.shape[1], LANES)]


def weights(part, top):
    return jnp.exp2((part - top) * EXP2_SCALE)


def first_kernel(first, middle_ref, q_ref, k_ref, v_ref, kp_ref, own_ref, other_ref, state_ref, order_ref):
    fill_orders(order_ref)
    rows = q_ref.shape[0]
    members = rows // MIDDLE_DILATION
    column = lax.broadcasted_iota(jnp.int32, (1, rows), 1)
    tops, totals = [], []
    heads = other_ref.shape[0]
    for place in range(heads):
        columns = head_columns(first + place)
        shift = middle_ref[first + place]
        q = q_ref[:, columns]
        own = dot_keys(q, k_ref[:, columns])
        other_keys = dot(order_ref[shift], kp_ref[:, columns]).astype(jnp.bfloat16)
        other = dot_keys(q, other_keys)
        top = functools.reduce(jnp.maximum, lane_tiles(own) + lane_tiles(other))
        top = jnp.max(top, axis=1, keepdims=True)
        row_is_member = member_rows(rows, shift)
        own, other = weights(own, top), weights(other, top)
        own_member = row_is_member & ((column & (MIDDLE_DILATION - 1)) == shift)
        own = jnp.where(own_member, own + own, own)
        twice = other[:, :LANES]
        twice = jnp.where(row_is_member & (column[:, :LANES] < members), twice + twice, twice)
        other = jnp.concatenate([twice, other[:, LANES:]], axis=1)
        total = functools.reduce(jnp.add, lane_tiles(own) + lane_tiles(other))
        tops.append(top)
        totals.append(jnp.sum(total, axis=1, keepdims=True))
        own_ref[:, head_columns(place)] = dot(own.astype(jnp.bfloat16), v_ref[:, columns])
        other_ref[place] = other.astype(jnp.bfloat16)
    state_ref[...] = side_by_side(tops + totals)


def extra_kernel(
    middle_ref, coarse_ref, q_ref, state_a_ref, state_b_ref, cross_ref, diagonal_k_ref, diagonal_v_ref, mine_ref,
    other_ref, sum_ref, share_ref,
):
    rows = q_ref.shape[0]
    members = rows // MIDDLE_DILATION
    half = HEAD_COUNT // 2
    far_rows, coarse_rows = 2 * members, 2 * mine_ref.shape[0]
    token = lax.broadcasted_iota(jnp.int32, (1, rows), 1)
    is_key = (lax.broadcasted_iota(jnp.int32, (coarse_rows, 1), 0) & 1) == 0
    states = [ref[...].T for ref in (state_a_ref, state_b_ref)]
    shares = []
    for head in range(HEAD_COUNT):
        columns = head_columns(head)
        state, place = states[head // half], head % half
        pairs = [mine_ref[:, columns], other_ref[:, columns]]
        keys = jnp.concatenate([cross_ref[:members, columns], diagonal_k_ref[:, columns], *pairs], axis=0)
        values = jnp.concatenate([cross_ref[members:, columns], diagonal_v_ref[:, columns], *pairs], axis=0)
        scores = dot_keys(keys, q_ref[:, columns])
        far = jnp.where((token & (MIDDLE_DILATION - 1)) == middle_ref[head], scores[:far_rows], MASKED)
        coarse = jnp.where(is_key & (token == coarse_ref[head]), scores[far_rows:], MASKED)
        before = state[place : place + 1]
        top = jnp.maximum(before, jnp.max(far, axis=0, keepdims=True))
        top = jnp.maximum(top, jnp.max(coarse, axis=0, keepdims=True))
        far, coarse = weights(far, top), weights(coarse, top)
        kept = weights(before, top)
        total = kept * state[half + place : half + place + 1]
        total += jnp.sum(far, axis=0, keepdims=True) + jnp.sum(coarse, axis=0, keepdims=True)
        inverse = 1.0 / total
        shifted = pltpu.roll(coarse, 1, 0)
        mixed = jnp.concatenate([(far * inverse).astype(jnp.bfloat16), (shifted * inverse).astype(jnp.bfloat16)], axis=0)
        sum_ref[:, columns] = dot_rows(mixed, values)
        shares.append(kept * inverse)
    share_ref[:, :HEAD_COUNT] = jnp.concatenate(shares, axis=0).T


def base_kernel(heads, sum_ref, share_ref, own_a_ref, own_b_ref, base_ref, spread_ref):
    half = HEAD_COUNT // 2
    rows = sum_ref.shape[0]
    for place, head in enumerate(heads):
        own_ref = (own_a_ref, own_b_ref)[head // half]
        share = jnp.broadcast_to(share_ref[:, head : head + 1], (rows, HEAD_FEATURES))
        columns = head_columns(place)
        base_ref[:, columns] = sum_ref[:, head_columns(head)] + share * own_ref[:, head_columns(head % half)]
        spread_ref[:, columns] = share


def finish_kernel(heads, base_ref, spread_ref, other_a_ref, other_b_ref, vm_ref, vr_ref, *rest):
    out_ref, ready_ref, semaphores = rest[-3:]
    half = HEAD_COUNT // 2
    copies = []
    for place, head in enumerate(heads):
        columns = head_columns(place)
        other_ref = (other_a_ref, other_b_ref)[head // half]
        values = jnp.concatenate([vm_ref[:, head_columns(head)], vr_ref[:, columns]], axis=0)
        result = base_ref[:, columns] + spread_ref[:, columns] * dot(other_ref[head % half], values)
        ready_ref[place] = result.astype(jnp.bfloat16)
        target = out_ref.at[:, head_columns(head)]
        copies.append(pltpu.make_async_copy(ready_ref.at[place], target, semaphores.at[place]))
        copies[-1].start()
    for copy in copies:
        copy.wait()


def in_hbm(array):
    return pltpu.with_memory_space_constraint(array, pltpu.HBM)


def cost():
    return pl.CostEstimate(flops=0, bytes_accessed=0, transcendentals=0)


def stack_kernel(*refs):
    out_ref = refs[-1]
    out_ref[...] = jnp.concatenate([ref[...].astype(jnp.float32) for ref in refs[:-1]], axis=0).astype(out_ref.dtype)


def stack(*pieces):
    vmem = pl.BlockSpec(memory_space=pltpu.VMEM)
    rows = sum(piece.shape[0] for piece in pieces)
    return pl.pallas_call(
        stack_kernel,
        name="stack",
        out_shape=pltpu.VMEM((rows, pieces[0].shape[1]), pieces[0].dtype),
        in_specs=[vmem] * len(pieces),
        out_specs=vmem,
        compiler_params=pltpu.CompilerParams(vmem_limit_bytes=8 * 1024 * 1024),
        cost_estimate=cost(),
    )(*pieces)


def gather_upper(value, axis):
    size = lax.axis_size(axis)
    assert size & (size - 1) == 0
    bits = [2**j for j in range(1, size.bit_length() - 1)]
    for step in [bits[j : j + 2] for j in range(0, len(bits), 2)]:
        masks = step + [sum(step)] if len(step) == 2 else step
        value = stack(value, *[partner(value, axis, mask) for mask in masks])
    return value


def on_device(query, keys, values, middle_head_shift, coarse_head_shift):
    rows, width = query.shape
    members = rows // MIDDLE_DILATION
    half = HEAD_COUNT // 2
    bf16, f32 = jnp.bfloat16, jnp.float32
    smem = pl.BlockSpec(memory_space=pltpu.SMEM)
    vmem = pl.BlockSpec(memory_space=pltpu.VMEM)
    anywhere = pl.BlockSpec(memory_space=pl.ANY)
    params = pltpu.CompilerParams(vmem_limit_bytes=8 * 1024 * 1024)
    orders = pltpu.VMEM((MIDDLE_DILATION, rows, rows), bf16)

    def call(kernel, name, *args, **options):
        return pl.pallas_call(kernel, name=name, compiler_params=params, cost_estimate=cost(), **options)(*args)

    other_keys = partner(keys, "inner", 1)
    q, k, v, own_members, own_vm, *own_vr, coarse = call(
        functools.partial(prepare_kernel, CHUNKS),
        "prepare",
        middle_head_shift, coarse_head_shift, in_hbm(query), in_hbm(keys), in_hbm(values),
        out_shape=[
            *[pltpu.VMEM((rows, width), bf16)] * 3,
            pltpu.VMEM((2 * members, width), bf16),
            pltpu.VMEM((members, width), bf16),
            *[pltpu.VMEM((rows - members, c * HEAD_FEATURES), bf16) for c in CHUNKS],
            pltpu.VMEM((2, width), bf16),
        ],
        in_specs=[smem, smem, anywhere, anywhere, anywhere],
        out_specs=[vmem] * (6 + len(CHUNKS)),
        scratch_shapes=[orders, pltpu.SemaphoreType.DMA((3,))],
    )
    cross = partner(own_members, "inner", 2)
    near = gather_upper(stack(coarse, partner_elsewhere(coarse, 1)), "outer")
    near, own_vm = lax.optimization_barrier((near, own_vm))
    other_vm = partner(own_vm, "inner", 1)
    cross, own_vr = lax.optimization_barrier((cross, own_vr))
    other_vr = [partner(piece, "inner", 1) for piece in own_vr]
    other_km = call(
        pick_kernel,
        "pick",
        middle_head_shift, other_keys,
        out_shape=pltpu.VMEM((members, width), bf16),
        in_specs=[smem, vmem],
        out_specs=vmem,
    )
    diagonal_k = partner(other_km, "inner", 2)
    other_keys = lax.optimization_barrier((other_keys, other_km))[0]

    def first_part(first, query):
        return call(
            functools.partial(first_kernel, first),
            "first",
            middle_head_shift, query, k, v, other_keys,
            out_shape=[
                pltpu.VMEM((rows, half * HEAD_FEATURES), f32),
                pltpu.VMEM((half, rows, rows), bf16),
                pltpu.VMEM((rows, LANES), f32),
            ],
            in_specs=[smem] + [vmem] * 4,
            out_specs=[vmem] * 3,
            scratch_shapes=[orders],
        )

    own_a, weights_a, state_a = first_part(0, q)
    diagonal_v = partner(lax.optimization_barrier((other_vm, state_a))[0], "inner", 2)
    own_b, weights_b, state_b = first_part(half, lax.optimization_barrier((q, state_a, diagonal_k))[0])
    mine = jnp.concatenate([near, partner_elsewhere(near, 2)], axis=0)
    extra_sum, share = call(
        extra_kernel,
        "extra",
        middle_head_shift, coarse_head_shift, q, state_a, state_b, cross, diagonal_k, diagonal_v, mine,
        partner(mine, "outer", 1),
        out_shape=[pltpu.VMEM((rows, width), f32), pltpu.VMEM((rows, LANES), f32)],
        in_specs=[smem, smem] + [vmem] * 8,
        out_specs=[vmem] * 2,
    )

    out = []
    first = 0
    for chunk, vr in zip(CHUNKS, other_vr):
        heads = range(first, first + chunk)
        base, spread = call(
            functools.partial(base_kernel, heads),
            "base",
            extra_sum, share, own_a, own_b,
            out_shape=[pltpu.VMEM((rows, chunk * HEAD_FEATURES), f32)] * 2,
            in_specs=[vmem] * 4,
            out_specs=[vmem] * 2,
        )
        args = [base, spread, weights_a, weights_b, other_vm, vr]
        out = [
            call(
                functools.partial(finish_kernel, heads),
                "finish",
                *args, *out,
                out_shape=jax.ShapeDtypeStruct((rows, width), bf16),
                in_specs=[vmem] * len(args) + [anywhere] * len(out),
                out_specs=anywhere,
                input_output_aliases={len(args): 0} if out else {},
                scratch_shapes=[pltpu.VMEM((chunk, rows, HEAD_FEATURES), bf16), pltpu.SemaphoreType.DMA((chunk,))],
            )
        ]
        first += chunk
    return out[0]


def solution(mesh):
    placed = (
        P(("outer", "inner"), None),
        P(("outer", "inner"), None),
        P(("outer", "inner"), None),
        P(),
        P(),
    )
    return jax.shard_map(
        on_device,
        mesh=mesh,
        in_specs=placed,
        out_specs=P(("outer", "inner"), None),
        check_vma=False,
    )
```

```python
import functools

import jax
import jax.numpy as jnp
from jax import lax
from jax.experimental import pallas as pl
from jax.experimental.pallas import tpu as pltpu
from jax.sharding import PartitionSpec as P

HEAD_COUNT = 16
HEAD_FEATURES = 128
MIDDLE_DILATION = 4
CHUNKS = (11, 4, 1)
LANES = 128
SUBLANES = 16
EXP2_SCALE = HEAD_FEATURES ** (-0.5) * 1.4426950408889634
MASKED = -1e30


def partner(value, axis, mask):
    pairs = [(source, source ^ mask) for source in range(lax.axis_size(axis))]
    return lax.ppermute(value, axis, pairs)


def partner_elsewhere(value, inner_mask):
    outer = lax.axis_size("outer")
    outer_mask = 2 if outer > 2 else 0
    pairs = []
    for i in range(lax.axis_size("inner")):
        for o in range(outer):
            pairs.append((i * outer + o, (i ^ inner_mask) * outer + (o ^ outer_mask)))
    return lax.ppermute(value, ("inner", "outer"), pairs)


def one_hot(mask):
    return mask.astype(jnp.float32).astype(jnp.bfloat16)


def fill_orders(order_ref):
    rows = order_ref.shape[1]
    members = rows // MIDDLE_DILATION
    group = lax.broadcasted_iota(jnp.int32, (members, rows), 0)
    token = lax.broadcasted_iota(jnp.int32, (members, rows), 1)
    for place in range(MIDDLE_DILATION):
        block = one_hot(token == MIDDLE_DILATION * group + place)
        for shift in range(MIDDLE_DILATION):
            slot = (place - shift) % MIDDLE_DILATION
            order_ref[shift, slot * members : (slot + 1) * members] = block


def dot(a, b):
    return jnp.dot(a, b, preferred_element_type=jnp.float32)


def head_columns(head):
    return slice(head * HEAD_FEATURES, (head + 1) * HEAD_FEATURES)


def prepare_kernel(chunks, middle_ref, coarse_ref, q_hbm, k_hbm, v_hbm, *rest):
    q_ref, k_ref, v_ref, members_ref, vm_ref, *vr_refs, coarse_out_ref, order_ref, semaphores = rest
    pairs = ((k_hbm, k_ref), (v_hbm, v_ref), (q_hbm, q_ref))
    copies = [pltpu.make_async_copy(*pair, semaphores.at[i]) for i, pair in enumerate(pairs)]
    for copy in copies:
        copy.start()
    rows = k_ref.shape[0]
    members = rows // MIDDLE_DILATION
    fill_orders(order_ref)
    token = lax.broadcasted_iota(jnp.int32, (SUBLANES, rows), 1)
    first_row = lax.broadcasted_iota(jnp.int32, (SUBLANES, rows), 0) == 0
    second_row = lax.broadcasted_iota(jnp.int32, (SUBLANES, rows), 0) == 1
    copies[0].wait()
    copies[1].wait()
    head = 0
    for chunk, vr_ref in zip(chunks, vr_refs):
        for place in range(chunk):
            columns = head_columns(head)
            order = order_ref[middle_ref[head]]
            k, v = k_ref[:, columns], v_ref[:, columns]
            v_ordered = dot(order, v).astype(jnp.bfloat16)
            members_ref[:members, columns] = dot(order[:members], k).astype(jnp.bfloat16)
            members_ref[members:, columns] = v_ordered[:members]
            vm_ref[:, columns] = v_ordered[:members]
            vr_ref[:, head_columns(place)] = v_ordered[members:]
            chosen = token == coarse_ref[head]
            picked = dot(one_hot(chosen & first_row), k) + dot(one_hot(chosen & second_row), v)
            coarse_out_ref[:, columns] = picked[:2].astype(jnp.bfloat16)
            head += 1
    copies[2].wait()


def pick_kernel(middle_ref, k_ref, members_ref):
    rows = k_ref.shape[0]
    members = rows // MIDDLE_DILATION
    group = lax.broadcasted_iota(jnp.int32, (members, rows), 0)
    token = lax.broadcasted_iota(jnp.int32, (members, rows), 1)
    offset = token - MIDDLE_DILATION * group
    for head in range(HEAD_COUNT):
        columns = head_columns(head)
        chosen = one_hot(offset == middle_ref[head])
        members_ref[:, columns] = dot(chosen, k_ref[:, columns]).astype(jnp.bfloat16)


def dot_keys(q, keys):
    return lax.dot_general(q, keys, (((1,), (1,)), ((), ())), preferred_element_type=jnp.float32)


def dot_rows(a, b):
    return lax.dot_general(a, b, (((0,), (0,)), ((), ())), preferred_element_type=jnp.float32)


def side_by_side(columns):
    rows = columns[0].shape[0]
    lane = lax.broadcasted_iota(jnp.int32, (rows, LANES), 1)
    result = jnp.zeros((rows, LANES), jnp.float32)
    for place, column in enumerate(columns):
        result = jnp.where(lane == place, column, result)
    return result


def member_rows(rows, shift):
    row = lax.broadcasted_iota(jnp.int32, (rows, 1), 0)
    return (row & (MIDDLE_DILATION - 1)) == shift


def lane_tiles(part):
    return [part[:, i : i + LANES] for i in range(0, part.shape[1], LANES)]


def weights(part, top):
    return jnp.exp2((part - top) * EXP2_SCALE)


def own_kernel(middle_ref, q_ref, k_ref, v_ref, sum_ref, state_ref):
    rows = q_ref.shape[0]
    column = lax.broadcasted_iota(jnp.int32, (1, rows), 1)
    tops, totals = [], []
    for head in range(HEAD_COUNT):
        columns = head_columns(head)
        shift = middle_ref[head]
        own = dot_keys(q_ref[:, columns], k_ref[:, columns])
        top = jnp.max(functools.reduce(jnp.maximum, lane_tiles(own)), axis=1, keepdims=True)
        own = weights(own, top)
        twice = member_rows(rows, shift) & ((column & (MIDDLE_DILATION - 1)) == shift)
        own = jnp.where(twice, own + own, own)
        tops.append(top)
        totals.append(jnp.sum(functools.reduce(jnp.add, lane_tiles(own)), axis=1, keepdims=True))
        sum_ref[:, columns] = dot(own.astype(jnp.bfloat16), v_ref[:, columns])
    state_ref[...] = side_by_side(tops + totals)


def other_kernel(first, middle_ref, q_ref, kp_ref, other_ref, state_ref, order_ref):
    fill_orders(order_ref)
    rows = q_ref.shape[0]
    members = rows // MIDDLE_DILATION
    column = lax.broadcasted_iota(jnp.int32, (1, LANES), 1)
    tops, totals = [], []
    for place in range(other_ref.shape[0]):
        columns = head_columns(first + place)
        shift = middle_ref[first + place]
        other_keys = dot(order_ref[shift], kp_ref[:, columns]).astype(jnp.bfloat16)
        other = dot_keys(q_ref[:, columns], other_keys)
        top = jnp.max(functools.reduce(jnp.maximum, lane_tiles(other)), axis=1, keepdims=True)
        other = weights(other, top)
        twice = other[:, :LANES]
        twice = jnp.where(member_rows(rows, shift) & (column < members), twice + twice, twice)
        other = jnp.concatenate([twice, other[:, LANES:]], axis=1)
        tops.append(top)
        totals.append(jnp.sum(functools.reduce(jnp.add, lane_tiles(other)), axis=1, keepdims=True))
        other_ref[place] = other.astype(jnp.bfloat16)
    state_ref[...] = side_by_side(tops + totals)


def extra_kernel(
    middle_ref, coarse_ref, q_ref, own_state_ref, state_a_ref, state_b_ref, cross_ref, diagonal_k_ref, diagonal_v_ref, mine_ref,
    other_ref, sum_ref, share_ref,
):
    rows = q_ref.shape[0]
    members = rows // MIDDLE_DILATION
    half = HEAD_COUNT // 2
    far_rows, coarse_rows = 2 * members, 2 * mine_ref.shape[0]
    token = lax.broadcasted_iota(jnp.int32, (1, rows), 1)
    is_key = (lax.broadcasted_iota(jnp.int32, (coarse_rows, 1), 0) & 1) == 0
    own_state = own_state_ref[...].T
    states = [ref[...].T for ref in (state_a_ref, state_b_ref)]
    own_shares, other_shares = [], []
    for head in range(HEAD_COUNT):
        columns = head_columns(head)
        state, place = states[head // half], head % half
        pairs = [mine_ref[:, columns], other_ref[:, columns]]
        keys = jnp.concatenate([cross_ref[:members, columns], diagonal_k_ref[:, columns], *pairs], axis=0)
        values = jnp.concatenate([cross_ref[members:, columns], diagonal_v_ref[:, columns], *pairs], axis=0)
        scores = dot_keys(keys, q_ref[:, columns])
        far = jnp.where((token & (MIDDLE_DILATION - 1)) == middle_ref[head], scores[:far_rows], MASKED)
        coarse = jnp.where(is_key & (token == coarse_ref[head]), scores[far_rows:], MASKED)
        own_top, other_top = own_state[head : head + 1], state[place : place + 1]
        top = jnp.maximum(jnp.maximum(own_top, other_top), jnp.max(far, axis=0, keepdims=True))
        top = jnp.maximum(top, jnp.max(coarse, axis=0, keepdims=True))
        far, coarse = weights(far, top), weights(coarse, top)
        own_kept, other_kept = weights(own_top, top), weights(other_top, top)
        total = own_kept * own_state[HEAD_COUNT + head : HEAD_COUNT + head + 1]
        total += other_kept * state[half + place : half + place + 1]
        total += jnp.sum(far, axis=0, keepdims=True) + jnp.sum(coarse, axis=0, keepdims=True)
        inverse = 1.0 / total
        shifted = pltpu.roll(coarse, 1, 0)
        mixed = jnp.concatenate([(far * inverse).astype(jnp.bfloat16), (shifted * inverse).astype(jnp.bfloat16)], axis=0)
        sum_ref[:, columns] = dot_rows(mixed, values)
        own_shares.append(own_kept * inverse)
        other_shares.append(other_kept * inverse)
    share_ref[:, : 2 * HEAD_COUNT] = jnp.concatenate(own_shares + other_shares, axis=0).T


def base_kernel(heads, sum_ref, share_ref, own_ref, base_ref, spread_ref):
    shape = (sum_ref.shape[0], HEAD_FEATURES)
    for place, head in enumerate(heads):
        columns, place_columns = head_columns(head), head_columns(place)
        share = share_ref[:, head : head + 1]
        base_ref[:, place_columns] = sum_ref[:, columns] + share * own_ref[:, columns]
        other = HEAD_COUNT + head
        spread_ref[:, place_columns] = jnp.broadcast_to(share_ref[:, other : other + 1], shape)


def finish_kernel(heads, base_ref, spread_ref, other_a_ref, other_b_ref, vm_ref, vr_ref, *rest):
    out_ref, ready_ref, semaphores = rest[-3:]
    half = HEAD_COUNT // 2
    copies = []
    for place, head in enumerate(heads):
        columns = head_columns(place)
        other_ref = (other_a_ref, other_b_ref)[head // half]
        values = jnp.concatenate([vm_ref[:, head_columns(head)], vr_ref[:, columns]], axis=0)
        result = base_ref[:, columns] + spread_ref[:, columns] * dot(other_ref[head % half], values)
        ready_ref[place] = result.astype(jnp.bfloat16)
        target = out_ref.at[:, head_columns(head)]
        copies.append(pltpu.make_async_copy(ready_ref.at[place], target, semaphores.at[place]))
        copies[-1].start()
    for copy in copies:
        copy.wait()


def in_hbm(array):
    return pltpu.with_memory_space_constraint(array, pltpu.HBM)


def cost():
    return pl.CostEstimate(flops=0, bytes_accessed=0, transcendentals=0)


def stack_kernel(*refs):
    out_ref = refs[-1]
    out_ref[...] = jnp.concatenate([ref[...].astype(jnp.float32) for ref in refs[:-1]], axis=0).astype(out_ref.dtype)


def stack(*pieces):
    vmem = pl.BlockSpec(memory_space=pltpu.VMEM)
    rows = sum(piece.shape[0] for piece in pieces)
    return pl.pallas_call(
        stack_kernel,
        name="stack",
        out_shape=pltpu.VMEM((rows, pieces[0].shape[1]), pieces[0].dtype),
        in_specs=[vmem] * len(pieces),
        out_specs=vmem,
        compiler_params=pltpu.CompilerParams(vmem_limit_bytes=8 * 1024 * 1024),
        cost_estimate=cost(),
    )(*pieces)


def gather_upper(value, axis):
    size = lax.axis_size(axis)
    assert size & (size - 1) == 0
    bits = [2**j for j in range(1, size.bit_length() - 1)]
    for step in [bits[j : j + 2] for j in range(0, len(bits), 2)]:
        masks = step + [sum(step)] if len(step) == 2 else step
        value = stack(value, *[partner(value, axis, mask) for mask in masks])
    return value


def on_device(query, keys, values, middle_head_shift, coarse_head_shift):
    rows, width = query.shape
    members = rows // MIDDLE_DILATION
    half = HEAD_COUNT // 2
    bf16, f32 = jnp.bfloat16, jnp.float32
    smem = pl.BlockSpec(memory_space=pltpu.SMEM)
    vmem = pl.BlockSpec(memory_space=pltpu.VMEM)
    anywhere = pl.BlockSpec(memory_space=pl.ANY)
    params = pltpu.CompilerParams(vmem_limit_bytes=8 * 1024 * 1024)
    orders = pltpu.VMEM((MIDDLE_DILATION, rows, rows), bf16)

    def call(kernel, name, *args, **options):
        return pl.pallas_call(kernel, name=name, compiler_params=params, cost_estimate=cost(), **options)(*args)

    other_keys = partner(keys, "inner", 1)
    q, k, v, own_members, own_vm, *own_vr, coarse = call(
        functools.partial(prepare_kernel, CHUNKS),
        "prepare",
        middle_head_shift, coarse_head_shift, in_hbm(query), in_hbm(keys), in_hbm(values),
        out_shape=[
            *[pltpu.VMEM((rows, width), bf16)] * 3,
            pltpu.VMEM((2 * members, width), bf16),
            pltpu.VMEM((members, width), bf16),
            *[pltpu.VMEM((rows - members, c * HEAD_FEATURES), bf16) for c in CHUNKS],
            pltpu.VMEM((2, width), bf16),
        ],
        in_specs=[smem, smem, anywhere, anywhere, anywhere],
        out_specs=[vmem] * (6 + len(CHUNKS)),
        scratch_shapes=[orders, pltpu.SemaphoreType.DMA((3,))],
    )
    cross = partner(own_members, "inner", 2)
    near = gather_upper(stack(coarse, partner_elsewhere(coarse, 1)), "outer")
    own_sum, own_state = call(
        own_kernel,
        "own",
        middle_head_shift, q, k, v,
        out_shape=[pltpu.VMEM((rows, width), f32), pltpu.VMEM((rows, LANES), f32)],
        in_specs=[smem] + [vmem] * 3,
        out_specs=[vmem] * 2,
    )
    near, own_vm, own_state = lax.optimization_barrier((near, own_vm, own_state))
    other_vm = partner(own_vm, "inner", 1)
    cross, own_vr = lax.optimization_barrier((cross, own_vr))
    other_vr = [partner(piece, "inner", 1) for piece in own_vr]
    other_km = call(
        pick_kernel,
        "pick",
        middle_head_shift, other_keys,
        out_shape=pltpu.VMEM((members, width), bf16),
        in_specs=[smem, vmem],
        out_specs=vmem,
    )
    diagonal_k = partner(other_km, "inner", 2)
    other_keys = lax.optimization_barrier((other_keys, other_km))[0]

    def other_part(first, query):
        return call(
            functools.partial(other_kernel, first),
            "other",
            middle_head_shift, query, other_keys,
            out_shape=[pltpu.VMEM((half, rows, rows), bf16), pltpu.VMEM((rows, LANES), f32)],
            in_specs=[smem] + [vmem] * 2,
            out_specs=[vmem] * 2,
            scratch_shapes=[orders],
        )

    weights_a, state_a = other_part(0, q)
    diagonal_v = partner(lax.optimization_barrier((other_vm, state_a))[0], "inner", 2)
    weights_b, state_b = other_part(half, lax.optimization_barrier((q, state_a, diagonal_k))[0])
    mine = jnp.concatenate([near, partner_elsewhere(near, 2)], axis=0)
    extra_sum, share = call(
        extra_kernel,
        "extra",
        middle_head_shift, coarse_head_shift, q, own_state, state_a, state_b, cross, diagonal_k, diagonal_v, mine,
        partner(mine, "outer", 1),
        out_shape=[pltpu.VMEM((rows, width), f32), pltpu.VMEM((rows, LANES), f32)],
        in_specs=[smem, smem] + [vmem] * 9,
        out_specs=[vmem] * 2,
    )

    out = []
    first = 0
    for chunk, vr in zip(CHUNKS, other_vr):
        heads = range(first, first + chunk)
        base, spread = call(
            functools.partial(base_kernel, heads),
            "base",
            extra_sum, share, own_sum,
            out_shape=[pltpu.VMEM((rows, chunk * HEAD_FEATURES), f32)] * 2,
            in_specs=[vmem] * 3,
            out_specs=[vmem] * 2,
        )
        args = [base, spread, weights_a, weights_b, other_vm, vr]
        out = [
            call(
                functools.partial(finish_kernel, heads),
                "finish",
                *args, *out,
                out_shape=jax.ShapeDtypeStruct((rows, width), bf16),
                in_specs=[vmem] * len(args) + [anywhere] * len(out),
                out_specs=anywhere,
                input_output_aliases={len(args): 0} if out else {},
                scratch_shapes=[pltpu.VMEM((chunk, rows, HEAD_FEATURES), bf16), pltpu.SemaphoreType.DMA((chunk,))],
            )
        ]
        first += chunk
    return out[0]


def solution(mesh):
    placed = (
        P(("outer", "inner"), None),
        P(("outer", "inner"), None),
        P(("outer", "inner"), None),
        P(),
        P(),
    )
    return jax.shard_map(
        on_device,
        mesh=mesh,
        in_specs=placed,
        out_specs=P(("outer", "inner"), None),
        check_vma=False,
    )
```

```python
import functools

import jax
import jax.numpy as jnp
from jax import lax
from jax.experimental import pallas as pl
from jax.experimental.pallas import tpu as pltpu
from jax.sharding import PartitionSpec as P

HEAD_COUNT = 16
HEAD_FEATURES = 128
MIDDLE_DILATION = 4
CHUNKS = (11, 3, 2)
LANES = 128
SUBLANES = 16
EXP2_SCALE = HEAD_FEATURES ** (-0.5) * 1.4426950408889634
MASKED = -1e30


def partner(value, axis, mask):
    pairs = [(source, source ^ mask) for source in range(lax.axis_size(axis))]
    return lax.ppermute(value, axis, pairs)


def partner_elsewhere(value, inner_mask):
    outer = lax.axis_size("outer")
    outer_mask = 2 if outer > 2 else 0
    pairs = []
    for i in range(lax.axis_size("inner")):
        for o in range(outer):
            pairs.append((i * outer + o, (i ^ inner_mask) * outer + (o ^ outer_mask)))
    return lax.ppermute(value, ("inner", "outer"), pairs)


def one_hot(mask):
    return mask.astype(jnp.float32).astype(jnp.bfloat16)


def fill_orders(order_ref):
    rows = order_ref.shape[1]
    members = rows // MIDDLE_DILATION
    group = lax.broadcasted_iota(jnp.int32, (members, rows), 0)
    token = lax.broadcasted_iota(jnp.int32, (members, rows), 1)
    for place in range(MIDDLE_DILATION):
        block = one_hot(token == MIDDLE_DILATION * group + place)
        for shift in range(MIDDLE_DILATION):
            slot = (place - shift) % MIDDLE_DILATION
            order_ref[shift, slot * members : (slot + 1) * members] = block


def dot(a, b):
    return jnp.dot(a, b, preferred_element_type=jnp.float32)


def head_columns(head):
    return slice(head * HEAD_FEATURES, (head + 1) * HEAD_FEATURES)


def prepare_kernel(chunks, middle_ref, coarse_ref, q_hbm, k_hbm, v_hbm, *rest):
    q_ref, k_ref, v_ref, members_ref, vm_ref, *vr_refs, coarse_out_ref, order_ref, semaphores = rest
    pairs = ((k_hbm, k_ref), (v_hbm, v_ref), (q_hbm, q_ref))
    copies = [pltpu.make_async_copy(*pair, semaphores.at[i]) for i, pair in enumerate(pairs)]
    for copy in copies:
        copy.start()
    rows = k_ref.shape[0]
    members = rows // MIDDLE_DILATION
    fill_orders(order_ref)
    token = lax.broadcasted_iota(jnp.int32, (SUBLANES, rows), 1)
    first_row = lax.broadcasted_iota(jnp.int32, (SUBLANES, rows), 0) == 0
    second_row = lax.broadcasted_iota(jnp.int32, (SUBLANES, rows), 0) == 1
    copies[0].wait()
    copies[1].wait()
    head = 0
    for chunk, vr_ref in zip(chunks, vr_refs):
        for place in range(chunk):
            columns = head_columns(head)
            order = order_ref[middle_ref[head]]
            k, v = k_ref[:, columns], v_ref[:, columns]
            v_ordered = dot(order, v).astype(jnp.bfloat16)
            members_ref[:members, columns] = dot(order[:members], k).astype(jnp.bfloat16)
            members_ref[members:, columns] = v_ordered[:members]
            vm_ref[:, columns] = v_ordered[:members]
            vr_ref[:, head_columns(place)] = v_ordered[members:]
            chosen = token == coarse_ref[head]
            picked = dot(one_hot(chosen & first_row), k) + dot(one_hot(chosen & second_row), v)
            coarse_out_ref[:, columns] = picked[:2].astype(jnp.bfloat16)
            head += 1
    copies[2].wait()


def pick_kernel(middle_ref, k_ref, members_ref):
    rows = k_ref.shape[0]
    members = rows // MIDDLE_DILATION
    group = lax.broadcasted_iota(jnp.int32, (members, rows), 0)
    token = lax.broadcasted_iota(jnp.int32, (members, rows), 1)
    offset = token - MIDDLE_DILATION * group
    for head in range(HEAD_COUNT):
        columns = head_columns(head)
        chosen = one_hot(offset == middle_ref[head])
        members_ref[:, columns] = dot(chosen, k_ref[:, columns]).astype(jnp.bfloat16)


def dot_keys(q, keys):
    return lax.dot_general(q, keys, (((1,), (1,)), ((), ())), preferred_element_type=jnp.float32)


def dot_rows(a, b):
    return lax.dot_general(a, b, (((0,), (0,)), ((), ())), preferred_element_type=jnp.float32)


def side_by_side(columns):
    rows = columns[0].shape[0]
    lane = lax.broadcasted_iota(jnp.int32, (rows, LANES), 1)
    result = jnp.zeros((rows, LANES), jnp.float32)
    for place, column in enumerate(columns):
        result = jnp.where(lane == place, column, result)
    return result


def member_rows(rows, shift):
    row = lax.broadcasted_iota(jnp.int32, (rows, 1), 0)
    return (row & (MIDDLE_DILATION - 1)) == shift


def lane_tiles(part):
    return [part[:, i : i + LANES] for i in range(0, part.shape[1], LANES)]


def weights(part, top):
    return jnp.exp2((part - top) * EXP2_SCALE)


def own_kernel(q_ref, k_ref, scores_ref, top_ref):
    tops = []
    for head in range(HEAD_COUNT):
        columns = head_columns(head)
        own = dot_keys(q_ref[:, columns], k_ref[:, columns])
        tops.append(jnp.max(functools.reduce(jnp.maximum, lane_tiles(own)), axis=1, keepdims=True))
        scores_ref[head] = own
    top_ref[...] = side_by_side(tops)


def first_kernel(
    first, middle_ref, q_ref, scores_ref, top_ref, v_ref, kp_ref, own_ref, other_ref, state_ref, order_ref
):
    fill_orders(order_ref)
    rows = q_ref.shape[0]
    members = rows // MIDDLE_DILATION
    column = lax.broadcasted_iota(jnp.int32, (1, rows), 1)
    tops, totals = [], []
    for place in range(other_ref.shape[0]):
        head = first + place
        columns = head_columns(head)
        shift = middle_ref[head]
        row_is_member = member_rows(rows, shift)
        other_keys = dot(order_ref[shift], kp_ref[:, columns]).astype(jnp.bfloat16)
        other = dot_keys(q_ref[:, columns], other_keys)
        top = jnp.max(functools.reduce(jnp.maximum, lane_tiles(other)), axis=1, keepdims=True)
        top = jnp.maximum(top, top_ref[:, head : head + 1])
        other = weights(other, top)
        twice = other[:, :LANES]
        twice = jnp.where(row_is_member & (column[:, :LANES] < members), twice + twice, twice)
        other = jnp.concatenate([twice, other[:, LANES:]], axis=1)
        total = functools.reduce(jnp.add, lane_tiles(other))
        other_ref[place] = other.astype(jnp.bfloat16)
        own = weights(scores_ref[head], top)
        own_member = row_is_member & ((column & (MIDDLE_DILATION - 1)) == shift)
        own = jnp.where(own_member, own + own, own)
        total = functools.reduce(jnp.add, lane_tiles(own), total)
        tops.append(top)
        totals.append(jnp.sum(total, axis=1, keepdims=True))
        own_ref[:, head_columns(place)] = dot(own.astype(jnp.bfloat16), v_ref[:, columns])
    state_ref[...] = side_by_side(tops + totals)


def extra_kernel(
    middle_ref, coarse_ref, q_ref, state_a_ref, state_b_ref, cross_ref, diagonal_k_ref, diagonal_v_ref, mine_ref,
    other_ref, sum_ref, share_ref,
):
    rows = q_ref.shape[0]
    members = rows // MIDDLE_DILATION
    half = HEAD_COUNT // 2
    far_rows, coarse_rows = 2 * members, 2 * mine_ref.shape[0]
    token = lax.broadcasted_iota(jnp.int32, (1, rows), 1)
    is_key = (lax.broadcasted_iota(jnp.int32, (coarse_rows, 1), 0) & 1) == 0
    states = [ref[...].T for ref in (state_a_ref, state_b_ref)]
    shares = []
    for head in range(HEAD_COUNT):
        columns = head_columns(head)
        state, place = states[head // half], head % half
        pairs = [mine_ref[:, columns], other_ref[:, columns]]
        keys = jnp.concatenate([cross_ref[:members, columns], diagonal_k_ref[:, columns], *pairs], axis=0)
        values = jnp.concatenate([cross_ref[members:, columns], diagonal_v_ref[:, columns], *pairs], axis=0)
        scores = dot_keys(keys, q_ref[:, columns])
        far = jnp.where((token & (MIDDLE_DILATION - 1)) == middle_ref[head], scores[:far_rows], MASKED)
        coarse = jnp.where(is_key & (token == coarse_ref[head]), scores[far_rows:], MASKED)
        before = state[place : place + 1]
        top = jnp.maximum(before, jnp.max(far, axis=0, keepdims=True))
        top = jnp.maximum(top, jnp.max(coarse, axis=0, keepdims=True))
        far, coarse = weights(far, top), weights(coarse, top)
        kept = weights(before, top)
        total = kept * state[half + place : half + place + 1]
        total += jnp.sum(far, axis=0, keepdims=True) + jnp.sum(coarse, axis=0, keepdims=True)
        inverse = 1.0 / total
        shifted = pltpu.roll(coarse, 1, 0)
        mixed = jnp.concatenate([(far * inverse).astype(jnp.bfloat16), (shifted * inverse).astype(jnp.bfloat16)], axis=0)
        sum_ref[:, columns] = dot_rows(mixed, values)
        shares.append(kept * inverse)
    share_ref[:, :HEAD_COUNT] = jnp.concatenate(shares, axis=0).T


def base_kernel(heads, sum_ref, share_ref, own_a_ref, own_b_ref, base_ref, spread_ref):
    half = HEAD_COUNT // 2
    rows = sum_ref.shape[0]
    for place, head in enumerate(heads):
        own_ref = (own_a_ref, own_b_ref)[head // half]
        share = jnp.broadcast_to(share_ref[:, head : head + 1], (rows, HEAD_FEATURES))
        columns = head_columns(place)
        base_ref[:, columns] = sum_ref[:, head_columns(head)] + share * own_ref[:, head_columns(head % half)]
        spread_ref[:, columns] = share


def finish_kernel(heads, base_ref, spread_ref, other_a_ref, other_b_ref, vm_ref, vr_ref, *rest):
    out_ref, ready_ref, semaphores = rest[-3:]
    half = HEAD_COUNT // 2
    copies = []
    for place, head in enumerate(heads):
        columns = head_columns(place)
        other_ref = (other_a_ref, other_b_ref)[head // half]
        values = jnp.concatenate([vm_ref[:, head_columns(head)], vr_ref[:, columns]], axis=0)
        result = base_ref[:, columns] + spread_ref[:, columns] * dot(other_ref[head % half], values)
        ready_ref[place] = result.astype(jnp.bfloat16)
        target = out_ref.at[:, head_columns(head)]
        copies.append(pltpu.make_async_copy(ready_ref.at[place], target, semaphores.at[place]))
        copies[-1].start()
    for copy in copies:
        copy.wait()


def in_hbm(array):
    return pltpu.with_memory_space_constraint(array, pltpu.HBM)


def cost():
    return pl.CostEstimate(flops=0, bytes_accessed=0, transcendentals=0)


def stack_kernel(*refs):
    out_ref = refs[-1]
    out_ref[...] = jnp.concatenate([ref[...].astype(jnp.float32) for ref in refs[:-1]], axis=0).astype(out_ref.dtype)


def stack(*pieces):
    vmem = pl.BlockSpec(memory_space=pltpu.VMEM)
    rows = sum(piece.shape[0] for piece in pieces)
    return pl.pallas_call(
        stack_kernel,
        name="stack",
        out_shape=pltpu.VMEM((rows, pieces[0].shape[1]), pieces[0].dtype),
        in_specs=[vmem] * len(pieces),
        out_specs=vmem,
        compiler_params=pltpu.CompilerParams(vmem_limit_bytes=8 * 1024 * 1024),
        cost_estimate=cost(),
    )(*pieces)


def gather_upper(value, axis):
    size = lax.axis_size(axis)
    assert size & (size - 1) == 0
    bits = [2**j for j in range(1, size.bit_length() - 1)]
    for step in [bits[j : j + 2] for j in range(0, len(bits), 2)]:
        masks = step + [sum(step)] if len(step) == 2 else step
        value = stack(value, *[partner(value, axis, mask) for mask in masks])
    return value


def on_device(query, keys, values, middle_head_shift, coarse_head_shift):
    rows, width = query.shape
    members = rows // MIDDLE_DILATION
    half = HEAD_COUNT // 2
    bf16, f32 = jnp.bfloat16, jnp.float32
    smem = pl.BlockSpec(memory_space=pltpu.SMEM)
    vmem = pl.BlockSpec(memory_space=pltpu.VMEM)
    anywhere = pl.BlockSpec(memory_space=pl.ANY)
    params = pltpu.CompilerParams(vmem_limit_bytes=8 * 1024 * 1024)
    orders = pltpu.VMEM((MIDDLE_DILATION, rows, rows), bf16)

    def call(kernel, name, *args, **options):
        return pl.pallas_call(kernel, name=name, compiler_params=params, cost_estimate=cost(), **options)(*args)

    other_keys = partner(keys, "inner", 1)
    q, k, v, own_members, own_vm, *own_vr, coarse = call(
        functools.partial(prepare_kernel, CHUNKS),
        "prepare",
        middle_head_shift, coarse_head_shift, in_hbm(query), in_hbm(keys), in_hbm(values),
        out_shape=[
            *[pltpu.VMEM((rows, width), bf16)] * 3,
            pltpu.VMEM((2 * members, width), bf16),
            pltpu.VMEM((members, width), bf16),
            *[pltpu.VMEM((rows - members, c * HEAD_FEATURES), bf16) for c in CHUNKS],
            pltpu.VMEM((2, width), bf16),
        ],
        in_specs=[smem, smem, anywhere, anywhere, anywhere],
        out_specs=[vmem] * (6 + len(CHUNKS)),
        scratch_shapes=[orders, pltpu.SemaphoreType.DMA((3,))],
    )
    cross = partner(own_members, "inner", 2)
    near = gather_upper(stack(coarse, partner_elsewhere(coarse, 1)), "outer")
    own_scores, own_top = call(
        own_kernel,
        "own",
        q, k,
        out_shape=[pltpu.VMEM((HEAD_COUNT, rows, rows), f32), pltpu.VMEM((rows, LANES), f32)],
        in_specs=[vmem] * 2,
        out_specs=[vmem] * 2,
    )
    near, own_vm, own_top = lax.optimization_barrier((near, own_vm, own_top))
    other_vm = partner(own_vm, "inner", 1)
    cross, own_vr = lax.optimization_barrier((cross, own_vr))
    other_vr = [partner(piece, "inner", 1) for piece in own_vr]
    other_km = call(
        pick_kernel,
        "pick",
        middle_head_shift, other_keys,
        out_shape=pltpu.VMEM((members, width), bf16),
        in_specs=[smem, vmem],
        out_specs=vmem,
    )
    diagonal_k = partner(other_km, "inner", 2)
    other_keys = lax.optimization_barrier((other_keys, other_km))[0]

    def first_part(first, query):
        return call(
            functools.partial(first_kernel, first),
            "first",
            middle_head_shift, query, own_scores, own_top, v, other_keys,
            out_shape=[
                pltpu.VMEM((rows, half * HEAD_FEATURES), f32),
                pltpu.VMEM((half, rows, rows), bf16),
                pltpu.VMEM((rows, LANES), f32),
            ],
            in_specs=[smem] + [vmem] * 5,
            out_specs=[vmem] * 3,
            scratch_shapes=[orders],
        )

    own_a, weights_a, state_a = first_part(0, q)
    diagonal_v = partner(lax.optimization_barrier((other_vm, state_a))[0], "inner", 2)
    own_b, weights_b, state_b = first_part(half, lax.optimization_barrier((q, state_a, diagonal_k))[0])
    mine = jnp.concatenate([near, partner_elsewhere(near, 2)], axis=0)
    extra_sum, share = call(
        extra_kernel,
        "extra",
        middle_head_shift, coarse_head_shift, q, state_a, state_b, cross, diagonal_k, diagonal_v, mine,
        partner(mine, "outer", 1),
        out_shape=[pltpu.VMEM((rows, width), f32), pltpu.VMEM((rows, LANES), f32)],
        in_specs=[smem, smem] + [vmem] * 8,
        out_specs=[vmem] * 2,
    )

    out = []
    first = 0
    for chunk, vr in zip(CHUNKS, other_vr):
        heads = range(first, first + chunk)
        base, spread = call(
            functools.partial(base_kernel, heads),
            "base",
            extra_sum, share, own_a, own_b,
            out_shape=[pltpu.VMEM((rows, chunk * HEAD_FEATURES), f32)] * 2,
            in_specs=[vmem] * 4,
            out_specs=[vmem] * 2,
        )
        args = [base, spread, weights_a, weights_b, other_vm, vr]
        out = [
            call(
                functools.partial(finish_kernel, heads),
                "finish",
                *args, *out,
                out_shape=jax.ShapeDtypeStruct((rows, width), bf16),
                in_specs=[vmem] * len(args) + [anywhere] * len(out),
                out_specs=anywhere,
                input_output_aliases={len(args): 0} if out else {},
                scratch_shapes=[pltpu.VMEM((chunk, rows, HEAD_FEATURES), bf16), pltpu.SemaphoreType.DMA((chunk,))],
            )
        ]
        first += chunk
    return out[0]


def solution(mesh):
    placed = (
        P(("outer", "inner"), None),
        P(("outer", "inner"), None),
        P(("outer", "inner"), None),
        P(),
        P(),
    )
    return jax.shard_map(
        on_device,
        mesh=mesh,
        in_specs=placed,
        out_specs=P(("outer", "inner"), None),
        check_vma=False,
    )
```

```python
import functools

import jax
import jax.numpy as jnp
from jax import lax
from jax.experimental import pallas as pl
from jax.experimental.pallas import tpu as pltpu
from jax.sharding import PartitionSpec as P

HEAD_COUNT = 16
HEAD_FEATURES = 128
MIDDLE_DILATION = 4
CHUNKS = (12, 3, 1)
LANES = 128
SUBLANES = 16
EXP2_SCALE = HEAD_FEATURES ** (-0.5) * 1.4426950408889634
MASKED = -1e30


def partner(value, axis, mask):
    pairs = [(source, source ^ mask) for source in range(lax.axis_size(axis))]
    return lax.ppermute(value, axis, pairs)


def partner_elsewhere(value, inner_mask):
    outer = lax.axis_size("outer")
    outer_mask = 2 if outer > 2 else 0
    pairs = []
    for i in range(lax.axis_size("inner")):
        for o in range(outer):
            pairs.append((i * outer + o, (i ^ inner_mask) * outer + (o ^ outer_mask)))
    return lax.ppermute(value, ("inner", "outer"), pairs)


def one_hot(mask):
    return mask.astype(jnp.float32).astype(jnp.bfloat16)


def fill_orders(order_ref):
    rows = order_ref.shape[1]
    members = rows // MIDDLE_DILATION
    group = lax.broadcasted_iota(jnp.int32, (members, rows), 0)
    token = lax.broadcasted_iota(jnp.int32, (members, rows), 1)
    for place in range(MIDDLE_DILATION):
        block = one_hot(token == MIDDLE_DILATION * group + place)
        for shift in range(MIDDLE_DILATION):
            slot = (place - shift) % MIDDLE_DILATION
            order_ref[shift, slot * members : (slot + 1) * members] = block


def dot(a, b):
    return jnp.dot(a, b, preferred_element_type=jnp.float32)


def head_columns(head):
    return slice(head * HEAD_FEATURES, (head + 1) * HEAD_FEATURES)


def prepare_kernel(chunks, middle_ref, coarse_ref, q_hbm, k_hbm, v_hbm, *rest):
    q_ref, k_ref, v_ref, members_ref, vm_ref, *vr_refs, coarse_out_ref, order_ref, semaphores = rest
    pairs = ((k_hbm, k_ref), (v_hbm, v_ref), (q_hbm, q_ref))
    copies = [pltpu.make_async_copy(*pair, semaphores.at[i]) for i, pair in enumerate(pairs)]
    for copy in copies:
        copy.start()
    rows = k_ref.shape[0]
    members = rows // MIDDLE_DILATION
    fill_orders(order_ref)
    token = lax.broadcasted_iota(jnp.int32, (SUBLANES, rows), 1)
    first_row = lax.broadcasted_iota(jnp.int32, (SUBLANES, rows), 0) == 0
    second_row = lax.broadcasted_iota(jnp.int32, (SUBLANES, rows), 0) == 1
    copies[0].wait()
    copies[1].wait()
    head = 0
    for chunk, vr_ref in zip(chunks, vr_refs):
        for place in range(chunk):
            columns = head_columns(head)
            order = order_ref[middle_ref[head]]
            k, v = k_ref[:, columns], v_ref[:, columns]
            v_ordered = dot(order, v).astype(jnp.bfloat16)
            members_ref[:members, columns] = dot(order[:members], k).astype(jnp.bfloat16)
            members_ref[members:, columns] = v_ordered[:members]
            vm_ref[:, columns] = v_ordered[:members]
            vr_ref[:, head_columns(place)] = v_ordered[members:]
            chosen = token == coarse_ref[head]
            picked = dot(one_hot(chosen & first_row), k) + dot(one_hot(chosen & second_row), v)
            coarse_out_ref[:, columns] = picked[:2].astype(jnp.bfloat16)
            head += 1
    copies[2].wait()


def pick_kernel(middle_ref, k_ref, members_ref):
    rows = k_ref.shape[0]
    members = rows // MIDDLE_DILATION
    group = lax.broadcasted_iota(jnp.int32, (members, rows), 0)
    token = lax.broadcasted_iota(jnp.int32, (members, rows), 1)
    offset = token - MIDDLE_DILATION * group
    for head in range(HEAD_COUNT):
        columns = head_columns(head)
        chosen = one_hot(offset == middle_ref[head])
        members_ref[:, columns] = dot(chosen, k_ref[:, columns]).astype(jnp.bfloat16)


def dot_keys(q, keys):
    return lax.dot_general(q, keys, (((1,), (1,)), ((), ())), preferred_element_type=jnp.float32)


def dot_rows(a, b):
    return lax.dot_general(a, b, (((0,), (0,)), ((), ())), preferred_element_type=jnp.float32)


def side_by_side(columns):
    rows = columns[0].shape[0]
    lane = lax.broadcasted_iota(jnp.int32, (rows, LANES), 1)
    result = jnp.zeros((rows, LANES), jnp.float32)
    for place, column in enumerate(columns):
        result = jnp.where(lane == place, column, result)
    return result


def member_rows(rows, shift):
    row = lax.broadcasted_iota(jnp.int32, (rows, 1), 0)
    return (row & (MIDDLE_DILATION - 1)) == shift


def lane_tiles(part):
    return [part[:, i : i + LANES] for i in range(0, part.shape[1], LANES)]


def weights(part, top):
    return jnp.exp2((part - top) * EXP2_SCALE)


def score_kernel(q_ref, k_ref, scores_ref, top_ref):
    tops = []
    for head in range(HEAD_COUNT):
        columns = head_columns(head)
        own = dot_keys(q_ref[:, columns], k_ref[:, columns])
        tops.append(jnp.max(functools.reduce(jnp.maximum, lane_tiles(own)), axis=1, keepdims=True))
        scores_ref[head] = own
    top_ref[...] = side_by_side(tops)


def other_kernel(first, middle_ref, q_ref, own_top_ref, kp_ref, other_ref, state_ref, order_ref):
    fill_orders(order_ref)
    rows = q_ref.shape[0]
    members = rows // MIDDLE_DILATION
    column = lax.broadcasted_iota(jnp.int32, (1, LANES), 1)
    tops, totals = [], []
    for place in range(other_ref.shape[0]):
        head = first + place
        columns = head_columns(head)
        shift = middle_ref[head]
        other_keys = dot(order_ref[shift], kp_ref[:, columns]).astype(jnp.bfloat16)
        other = dot_keys(q_ref[:, columns], other_keys)
        top = jnp.max(functools.reduce(jnp.maximum, lane_tiles(other)), axis=1, keepdims=True)
        top = jnp.maximum(top, own_top_ref[:, head : head + 1])
        other = weights(other, top)
        twice = other[:, :LANES]
        twice = jnp.where(member_rows(rows, shift) & (column < members), twice + twice, twice)
        other = jnp.concatenate([twice, other[:, LANES:]], axis=1)
        tops.append(top)
        totals.append(jnp.sum(functools.reduce(jnp.add, lane_tiles(other)), axis=1, keepdims=True))
        other_ref[place] = other.astype(jnp.bfloat16)
    state_ref[...] = side_by_side(tops + totals)


def own_kernel(middle_ref, scores_ref, state_a_ref, state_b_ref, v_ref, sum_ref, total_ref):
    rows = v_ref.shape[0]
    half = HEAD_COUNT // 2
    column = lax.broadcasted_iota(jnp.int32, (1, rows), 1)
    totals = []
    for head in range(HEAD_COUNT):
        columns = head_columns(head)
        shift = middle_ref[head]
        place = head % half
        own = weights(scores_ref[head], (state_a_ref, state_b_ref)[head // half][:, place : place + 1])
        twice = member_rows(rows, shift) & ((column & (MIDDLE_DILATION - 1)) == shift)
        own = jnp.where(twice, own + own, own)
        totals.append(jnp.sum(functools.reduce(jnp.add, lane_tiles(own)), axis=1, keepdims=True))
        sum_ref[:, columns] = dot(own.astype(jnp.bfloat16), v_ref[:, columns])
    total_ref[...] = side_by_side(totals)


def extra_kernel(
    middle_ref, coarse_ref, q_ref, own_total_ref, state_a_ref, state_b_ref, cross_ref, diagonal_k_ref, diagonal_v_ref, mine_ref,
    other_ref, sum_ref, share_ref,
):
    rows = q_ref.shape[0]
    members = rows // MIDDLE_DILATION
    half = HEAD_COUNT // 2
    far_rows, coarse_rows = 2 * members, 2 * mine_ref.shape[0]
    token = lax.broadcasted_iota(jnp.int32, (1, rows), 1)
    is_key = (lax.broadcasted_iota(jnp.int32, (coarse_rows, 1), 0) & 1) == 0
    own_totals = own_total_ref[...].T
    states = [ref[...].T for ref in (state_a_ref, state_b_ref)]
    shares = []
    for head in range(HEAD_COUNT):
        columns = head_columns(head)
        state, place = states[head // half], head % half
        pairs = [mine_ref[:, columns], other_ref[:, columns]]
        keys = jnp.concatenate([cross_ref[:members, columns], diagonal_k_ref[:, columns], *pairs], axis=0)
        values = jnp.concatenate([cross_ref[members:, columns], diagonal_v_ref[:, columns], *pairs], axis=0)
        scores = dot_keys(keys, q_ref[:, columns])
        far = jnp.where((token & (MIDDLE_DILATION - 1)) == middle_ref[head], scores[:far_rows], MASKED)
        coarse = jnp.where(is_key & (token == coarse_ref[head]), scores[far_rows:], MASKED)
        before = state[place : place + 1]
        top = jnp.maximum(before, jnp.max(far, axis=0, keepdims=True))
        top = jnp.maximum(top, jnp.max(coarse, axis=0, keepdims=True))
        far, coarse = weights(far, top), weights(coarse, top)
        kept = weights(before, top)
        total = kept * (state[half + place : half + place + 1] + own_totals[head : head + 1])
        total += jnp.sum(far, axis=0, keepdims=True) + jnp.sum(coarse, axis=0, keepdims=True)
        inverse = 1.0 / total
        shifted = pltpu.roll(coarse, 1, 0)
        mixed = jnp.concatenate([(far * inverse).astype(jnp.bfloat16), (shifted * inverse).astype(jnp.bfloat16)], axis=0)
        sum_ref[:, columns] = dot_rows(mixed, values)
        shares.append(kept * inverse)
    share_ref[:, :HEAD_COUNT] = jnp.concatenate(shares, axis=0).T


def base_kernel(heads, sum_ref, share_ref, own_ref, base_ref, spread_ref):
    shape = (sum_ref.shape[0], HEAD_FEATURES)
    for place, head in enumerate(heads):
        columns, place_columns = head_columns(head), head_columns(place)
        share = jnp.broadcast_to(share_ref[:, head : head + 1], shape)
        base_ref[:, place_columns] = sum_ref[:, columns] + share * own_ref[:, columns]
        spread_ref[:, place_columns] = share


def finish_kernel(heads, base_ref, spread_ref, other_a_ref, other_b_ref, vm_ref, vr_ref, *rest):
    out_ref, ready_ref, semaphores = rest[-3:]
    half = HEAD_COUNT // 2
    copies = []
    for place, head in enumerate(heads):
        columns = head_columns(place)
        other_ref = (other_a_ref, other_b_ref)[head // half]
        values = jnp.concatenate([vm_ref[:, head_columns(head)], vr_ref[:, columns]], axis=0)
        result = base_ref[:, columns] + spread_ref[:, columns] * dot(other_ref[head % half], values)
        ready_ref[place] = result.astype(jnp.bfloat16)
        target = out_ref.at[:, head_columns(head)]
        copies.append(pltpu.make_async_copy(ready_ref.at[place], target, semaphores.at[place]))
        copies[-1].start()
    for copy in copies:
        copy.wait()


def in_hbm(array):
    return pltpu.with_memory_space_constraint(array, pltpu.HBM)


def cost():
    return pl.CostEstimate(flops=0, bytes_accessed=0, transcendentals=0)


def stack_kernel(*refs):
    out_ref = refs[-1]
    out_ref[...] = jnp.concatenate([ref[...].astype(jnp.float32) for ref in refs[:-1]], axis=0).astype(out_ref.dtype)


def stack(*pieces):
    vmem = pl.BlockSpec(memory_space=pltpu.VMEM)
    rows = sum(piece.shape[0] for piece in pieces)
    return pl.pallas_call(
        stack_kernel,
        name="stack",
        out_shape=pltpu.VMEM((rows, pieces[0].shape[1]), pieces[0].dtype),
        in_specs=[vmem] * len(pieces),
        out_specs=vmem,
        compiler_params=pltpu.CompilerParams(vmem_limit_bytes=8 * 1024 * 1024),
        cost_estimate=cost(),
    )(*pieces)


def gather_upper(value, axis):
    size = lax.axis_size(axis)
    assert size & (size - 1) == 0
    bits = [2**j for j in range(1, size.bit_length() - 1)]
    for step in [bits[j : j + 2] for j in range(0, len(bits), 2)]:
        masks = step + [sum(step)] if len(step) == 2 else step
        value = stack(value, *[partner(value, axis, mask) for mask in masks])
    return value


def on_device(query, keys, values, middle_head_shift, coarse_head_shift):
    rows, width = query.shape
    members = rows // MIDDLE_DILATION
    half = HEAD_COUNT // 2
    bf16, f32 = jnp.bfloat16, jnp.float32
    smem = pl.BlockSpec(memory_space=pltpu.SMEM)
    vmem = pl.BlockSpec(memory_space=pltpu.VMEM)
    anywhere = pl.BlockSpec(memory_space=pl.ANY)
    params = pltpu.CompilerParams(vmem_limit_bytes=8 * 1024 * 1024)
    orders = pltpu.VMEM((MIDDLE_DILATION, rows, rows), bf16)

    def call(kernel, name, *args, **options):
        return pl.pallas_call(kernel, name=name, compiler_params=params, cost_estimate=cost(), **options)(*args)

    other_keys = partner(keys, "inner", 1)
    q, k, v, own_members, own_vm, *own_vr, coarse = call(
        functools.partial(prepare_kernel, CHUNKS),
        "prepare",
        middle_head_shift, coarse_head_shift, in_hbm(query), in_hbm(keys), in_hbm(values),
        out_shape=[
            *[pltpu.VMEM((rows, width), bf16)] * 3,
            pltpu.VMEM((2 * members, width), bf16),
            pltpu.VMEM((members, width), bf16),
            *[pltpu.VMEM((rows - members, c * HEAD_FEATURES), bf16) for c in CHUNKS],
            pltpu.VMEM((2, width), bf16),
        ],
        in_specs=[smem, smem, anywhere, anywhere, anywhere],
        out_specs=[vmem] * (6 + len(CHUNKS)),
        scratch_shapes=[orders, pltpu.SemaphoreType.DMA((3,))],
    )
    cross = partner(own_members, "inner", 2)
    near = gather_upper(stack(coarse, partner_elsewhere(coarse, 1)), "outer")
    own_scores, own_top = call(
        score_kernel,
        "score",
        q, k,
        out_shape=[pltpu.VMEM((HEAD_COUNT, rows, rows), f32), pltpu.VMEM((rows, LANES), f32)],
        in_specs=[vmem] * 2,
        out_specs=[vmem] * 2,
    )
    near, own_vm, own_top = lax.optimization_barrier((near, own_vm, own_top))
    other_vm = partner(own_vm, "inner", 1)
    cross, own_vr = lax.optimization_barrier((cross, own_vr))
    other_vr = [partner(piece, "inner", 1) for piece in own_vr]
    other_km = call(
        pick_kernel,
        "pick",
        middle_head_shift, other_keys,
        out_shape=pltpu.VMEM((members, width), bf16),
        in_specs=[smem, vmem],
        out_specs=vmem,
    )
    diagonal_k = partner(other_km, "inner", 2)
    other_keys = lax.optimization_barrier((other_keys, other_km))[0]

    def other_part(first, query):
        return call(
            functools.partial(other_kernel, first),
            "other",
            middle_head_shift, query, own_top, other_keys,
            out_shape=[pltpu.VMEM((half, rows, rows), bf16), pltpu.VMEM((rows, LANES), f32)],
            in_specs=[smem] + [vmem] * 3,
            out_specs=[vmem] * 2,
            scratch_shapes=[orders],
        )

    weights_a, state_a = other_part(0, q)
    diagonal_v = partner(lax.optimization_barrier((other_vm, state_a))[0], "inner", 2)
    weights_b, state_b = other_part(half, lax.optimization_barrier((q, state_a, diagonal_k))[0])
    own_sum, own_total = call(
        own_kernel,
        "own",
        middle_head_shift, own_scores, state_a, state_b, v,
        out_shape=[pltpu.VMEM((rows, width), f32), pltpu.VMEM((rows, LANES), f32)],
        in_specs=[smem] + [vmem] * 4,
        out_specs=[vmem] * 2,
    )
    mine = jnp.concatenate([near, partner_elsewhere(near, 2)], axis=0)
    extra_sum, share = call(
        extra_kernel,
        "extra",
        middle_head_shift, coarse_head_shift, q, own_total, state_a, state_b, cross, diagonal_k, diagonal_v, mine,
        partner(mine, "outer", 1),
        out_shape=[pltpu.VMEM((rows, width), f32), pltpu.VMEM((rows, LANES), f32)],
        in_specs=[smem, smem] + [vmem] * 9,
        out_specs=[vmem] * 2,
    )

    out = []
    first = 0
    for chunk, vr in zip(CHUNKS, other_vr):
        heads = range(first, first + chunk)
        base, spread = call(
            functools.partial(base_kernel, heads),
            "base",
            extra_sum, share, own_sum,
            out_shape=[pltpu.VMEM((rows, chunk * HEAD_FEATURES), f32)] * 2,
            in_specs=[vmem] * 3,
            out_specs=[vmem] * 2,
        )
        args = [base, spread, weights_a, weights_b, other_vm, vr]
        out = [
            call(
                functools.partial(finish_kernel, heads),
                "finish",
                *args, *out,
                out_shape=jax.ShapeDtypeStruct((rows, width), bf16),
                in_specs=[vmem] * len(args) + [anywhere] * len(out),
                out_specs=anywhere,
                input_output_aliases={len(args): 0} if out else {},
                scratch_shapes=[pltpu.VMEM((chunk, rows, HEAD_FEATURES), bf16), pltpu.SemaphoreType.DMA((chunk,))],
            )
        ]
        first += chunk
    return out[0]


def solution(mesh):
    placed = (
        P(("outer", "inner"), None),
        P(("outer", "inner"), None),
        P(("outer", "inner"), None),
        P(),
        P(),
    )
    return jax.shard_map(
        on_device,
        mesh=mesh,
        in_specs=placed,
        out_specs=P(("outer", "inner"), None),
        check_vma=False,
    )
```

```python
import functools

import jax
import jax.numpy as jnp
from jax import lax
from jax.experimental import pallas as pl
from jax.experimental.pallas import tpu as pltpu
from jax.sharding import PartitionSpec as P

HEAD_COUNT = 16
HEAD_FEATURES = 128
MIDDLE_DILATION = 4
CHUNKS = (12, 3, 1)
LANES = 128
SUBLANES = 16
EXP2_SCALE = HEAD_FEATURES ** (-0.5) * 1.4426950408889634
MASKED = -1e30


def partner(value, axis, mask):
    pairs = [(source, source ^ mask) for source in range(lax.axis_size(axis))]
    return lax.ppermute(value, axis, pairs)


def partner_elsewhere(value, inner_mask):
    outer = lax.axis_size("outer")
    outer_mask = 2 if outer > 2 else 0
    pairs = []
    for i in range(lax.axis_size("inner")):
        for o in range(outer):
            pairs.append((i * outer + o, (i ^ inner_mask) * outer + (o ^ outer_mask)))
    return lax.ppermute(value, ("inner", "outer"), pairs)


def one_hot(mask):
    return mask.astype(jnp.float32).astype(jnp.bfloat16)


def fill_orders(order_ref):
    rows = order_ref.shape[1]
    members = rows // MIDDLE_DILATION
    group = lax.broadcasted_iota(jnp.int32, (members, rows), 0)
    token = lax.broadcasted_iota(jnp.int32, (members, rows), 1)
    for place in range(MIDDLE_DILATION):
        block = one_hot(token == MIDDLE_DILATION * group + place)
        for shift in range(MIDDLE_DILATION):
            slot = (place - shift) % MIDDLE_DILATION
            order_ref[shift, slot * members : (slot + 1) * members] = block


def dot(a, b):
    return jnp.dot(a, b, preferred_element_type=jnp.float32)


def head_columns(head):
    return slice(head * HEAD_FEATURES, (head + 1) * HEAD_FEATURES)


def prepare_kernel(chunks, middle_ref, coarse_ref, q_hbm, k_hbm, v_hbm, *rest):
    q_ref, k_ref, v_ref, members_ref, vm_ref, *vr_refs, coarse_out_ref, order_ref, semaphores = rest
    pairs = ((k_hbm, k_ref), (v_hbm, v_ref), (q_hbm, q_ref))
    copies = [pltpu.make_async_copy(*pair, semaphores.at[i]) for i, pair in enumerate(pairs)]
    for copy in copies:
        copy.start()
    rows = k_ref.shape[0]
    members = rows // MIDDLE_DILATION
    fill_orders(order_ref)
    token = lax.broadcasted_iota(jnp.int32, (SUBLANES, rows), 1)
    first_row = lax.broadcasted_iota(jnp.int32, (SUBLANES, rows), 0) == 0
    second_row = lax.broadcasted_iota(jnp.int32, (SUBLANES, rows), 0) == 1
    copies[0].wait()
    copies[1].wait()
    head = 0
    for chunk, vr_ref in zip(chunks, vr_refs):
        for place in range(chunk):
            columns = head_columns(head)
            order = order_ref[middle_ref[head]]
            k, v = k_ref[:, columns], v_ref[:, columns]
            v_ordered = dot(order, v).astype(jnp.bfloat16)
            members_ref[:members, columns] = dot(order[:members], k).astype(jnp.bfloat16)
            members_ref[members:, columns] = v_ordered[:members]
            vm_ref[:, columns] = v_ordered[:members]
            vr_ref[:, head_columns(place)] = v_ordered[members:]
            chosen = token == coarse_ref[head]
            picked = dot(one_hot(chosen & first_row), k) + dot(one_hot(chosen & second_row), v)
            coarse_out_ref[:, columns] = picked[:2].astype(jnp.bfloat16)
            head += 1
    copies[2].wait()


def pick_kernel(middle_ref, k_ref, members_ref):
    rows = k_ref.shape[0]
    members = rows // MIDDLE_DILATION
    group = lax.broadcasted_iota(jnp.int32, (members, rows), 0)
    token = lax.broadcasted_iota(jnp.int32, (members, rows), 1)
    offset = token - MIDDLE_DILATION * group
    for head in range(HEAD_COUNT):
        columns = head_columns(head)
        chosen = one_hot(offset == middle_ref[head])
        members_ref[:, columns] = dot(chosen, k_ref[:, columns]).astype(jnp.bfloat16)


def dot_keys(q, keys):
    return lax.dot_general(q, keys, (((1,), (1,)), ((), ())), preferred_element_type=jnp.float32)


def dot_rows(a, b):
    return lax.dot_general(a, b, (((0,), (0,)), ((), ())), preferred_element_type=jnp.float32)


def side_by_side(columns):
    rows = columns[0].shape[0]
    lane = lax.broadcasted_iota(jnp.int32, (rows, LANES), 1)
    result = jnp.zeros((rows, LANES), jnp.float32)
    for place, column in enumerate(columns):
        result = jnp.where(lane == place, column, result)
    return result


def member_rows(rows, shift):
    row = lax.broadcasted_iota(jnp.int32, (rows, 1), 0)
    return (row & (MIDDLE_DILATION - 1)) == shift


def lane_tiles(part):
    return [part[:, i : i + LANES] for i in range(0, part.shape[1], LANES)]


def weights(part, top):
    return jnp.exp2((part - top) * EXP2_SCALE)


def score_kernel(q_ref, k_ref, scores_ref, top_ref):
    for head in range(HEAD_COUNT):
        columns = head_columns(head)
        own = dot_keys(q_ref[:, columns], k_ref[:, columns])
        top = jnp.max(functools.reduce(jnp.maximum, lane_tiles(own)), axis=1, keepdims=True)
        top_ref[head] = jnp.broadcast_to(top, top_ref.shape[1:])
        scores_ref[head] = own


def other_kernel(first, middle_ref, q_ref, own_top_ref, kp_ref, other_ref, top_ref, state_ref, order_ref):
    fill_orders(order_ref)
    rows = q_ref.shape[0]
    members = rows // MIDDLE_DILATION
    column = lax.broadcasted_iota(jnp.int32, (1, LANES), 1)
    tops, totals = [], []
    for place in range(other_ref.shape[0]):
        head = first + place
        columns = head_columns(head)
        shift = middle_ref[head]
        other_keys = dot(order_ref[shift], kp_ref[:, columns]).astype(jnp.bfloat16)
        other = dot_keys(q_ref[:, columns], other_keys)
        top = jnp.max(functools.reduce(jnp.maximum, lane_tiles(other)), axis=1, keepdims=True)
        top = jnp.maximum(top, own_top_ref[head])
        top_ref[place] = top
        tiles = [weights(tile, top) for tile in lane_tiles(other)]
        twice = member_rows(rows, shift) & (column < members)
        tiles[0] = jnp.where(twice, tiles[0] + tiles[0], tiles[0])
        tops.append(top)
        totals.append(jnp.sum(functools.reduce(jnp.add, tiles), axis=1, keepdims=True))
        other_ref[place] = jnp.concatenate(tiles, axis=1).astype(jnp.bfloat16)
    state_ref[...] = side_by_side(tops + totals)


def own_kernel(middle_ref, scores_ref, top_a_ref, top_b_ref, v_ref, sum_ref, total_ref):
    rows = v_ref.shape[0]
    half = HEAD_COUNT // 2
    lane = lax.broadcasted_iota(jnp.int32, (1, LANES), 1)
    totals = []
    for head in range(HEAD_COUNT):
        columns = head_columns(head)
        shift = middle_ref[head]
        top = (top_a_ref, top_b_ref)[head // half][head % half]
        twice = member_rows(rows, shift) & ((lane & (MIDDLE_DILATION - 1)) == shift)
        tiles = [weights(tile, top) for tile in lane_tiles(scores_ref[head])]
        tiles = [jnp.where(twice, tile + tile, tile) for tile in tiles]
        totals.append(jnp.sum(functools.reduce(jnp.add, tiles), axis=1, keepdims=True))
        sum_ref[:, columns] = dot(jnp.concatenate(tiles, axis=1).astype(jnp.bfloat16), v_ref[:, columns])
    total_ref[...] = side_by_side(totals)


def extra_kernel(
    middle_ref, coarse_ref, q_ref, own_total_ref, state_a_ref, state_b_ref, cross_ref, diagonal_k_ref, diagonal_v_ref, mine_ref,
    other_ref, sum_ref, share_ref,
):
    rows = q_ref.shape[0]
    members = rows // MIDDLE_DILATION
    half = HEAD_COUNT // 2
    far_rows, coarse_rows = 2 * members, 2 * mine_ref.shape[0]
    token = lax.broadcasted_iota(jnp.int32, (1, rows), 1)
    is_key = (lax.broadcasted_iota(jnp.int32, (coarse_rows, 1), 0) & 1) == 0
    own_totals = own_total_ref[...].T
    states = [ref[...].T for ref in (state_a_ref, state_b_ref)]
    shares = []
    for head in range(HEAD_COUNT):
        columns = head_columns(head)
        state, place = states[head // half], head % half
        pairs = [mine_ref[:, columns], other_ref[:, columns]]
        keys = jnp.concatenate([cross_ref[:members, columns], diagonal_k_ref[:, columns], *pairs], axis=0)
        values = jnp.concatenate([cross_ref[members:, columns], diagonal_v_ref[:, columns], *pairs], axis=0)
        scores = dot_keys(keys, q_ref[:, columns])
        far = jnp.where((token & (MIDDLE_DILATION - 1)) == middle_ref[head], scores[:far_rows], MASKED)
        coarse = jnp.where(is_key & (token == coarse_ref[head]), scores[far_rows:], MASKED)
        before = state[place : place + 1]
        top = jnp.maximum(before, jnp.max(far, axis=0, keepdims=True))
        top = jnp.maximum(top, jnp.max(coarse, axis=0, keepdims=True))
        far, coarse = weights(far, top), weights(coarse, top)
        kept = weights(before, top)
        total = kept * (state[half + place : half + place + 1] + own_totals[head : head + 1])
        total += jnp.sum(far, axis=0, keepdims=True) + jnp.sum(coarse, axis=0, keepdims=True)
        inverse = 1.0 / total
        shifted = pltpu.roll(coarse, 1, 0)
        mixed = jnp.concatenate([(far * inverse).astype(jnp.bfloat16), (shifted * inverse).astype(jnp.bfloat16)], axis=0)
        sum_ref[:, columns] = dot_rows(mixed, values)
        shares.append(kept * inverse)
    share_ref[:, :HEAD_COUNT] = jnp.concatenate(shares, axis=0).T


def base_kernel(heads, sum_ref, share_ref, own_ref, base_ref, spread_ref):
    shape = (sum_ref.shape[0], HEAD_FEATURES)
    for place, head in enumerate(heads):
        columns, place_columns = head_columns(head), head_columns(place)
        share = jnp.broadcast_to(share_ref[:, head : head + 1], shape)
        base_ref[:, place_columns] = sum_ref[:, columns] + share * own_ref[:, columns]
        spread_ref[:, place_columns] = share


def finish_kernel(heads, base_ref, spread_ref, other_a_ref, other_b_ref, vm_ref, vr_ref, *rest):
    out_ref, ready_ref, semaphores = rest[-3:]
    half = HEAD_COUNT // 2
    copies = []
    for place, head in enumerate(heads):
        columns = head_columns(place)
        other_ref = (other_a_ref, other_b_ref)[head // half]
        values = jnp.concatenate([vm_ref[:, head_columns(head)], vr_ref[:, columns]], axis=0)
        result = base_ref[:, columns] + spread_ref[:, columns] * dot(other_ref[head % half], values)
        ready_ref[place] = result.astype(jnp.bfloat16)
        target = out_ref.at[:, head_columns(head)]
        copies.append(pltpu.make_async_copy(ready_ref.at[place], target, semaphores.at[place]))
        copies[-1].start()
    for copy in copies:
        copy.wait()


def in_hbm(array):
    return pltpu.with_memory_space_constraint(array, pltpu.HBM)


def cost():
    return pl.CostEstimate(flops=0, bytes_accessed=0, transcendentals=0)


def stack_kernel(*refs):
    out_ref = refs[-1]
    out_ref[...] = jnp.concatenate([ref[...].astype(jnp.float32) for ref in refs[:-1]], axis=0).astype(out_ref.dtype)


def stack(*pieces):
    vmem = pl.BlockSpec(memory_space=pltpu.VMEM)
    rows = sum(piece.shape[0] for piece in pieces)
    return pl.pallas_call(
        stack_kernel,
        name="stack",
        out_shape=pltpu.VMEM((rows, pieces[0].shape[1]), pieces[0].dtype),
        in_specs=[vmem] * len(pieces),
        out_specs=vmem,
        compiler_params=pltpu.CompilerParams(vmem_limit_bytes=8 * 1024 * 1024),
        cost_estimate=cost(),
    )(*pieces)


def gather_upper(value, axis):
    size = lax.axis_size(axis)
    assert size & (size - 1) == 0
    bits = [2**j for j in range(1, size.bit_length() - 1)]
    for step in [bits[j : j + 2] for j in range(0, len(bits), 2)]:
        masks = step + [sum(step)] if len(step) == 2 else step
        value = stack(value, *[partner(value, axis, mask) for mask in masks])
    return value


def on_device(query, keys, values, middle_head_shift, coarse_head_shift):
    rows, width = query.shape
    members = rows // MIDDLE_DILATION
    half = HEAD_COUNT // 2
    bf16, f32 = jnp.bfloat16, jnp.float32
    smem = pl.BlockSpec(memory_space=pltpu.SMEM)
    vmem = pl.BlockSpec(memory_space=pltpu.VMEM)
    anywhere = pl.BlockSpec(memory_space=pl.ANY)
    params = pltpu.CompilerParams(vmem_limit_bytes=8 * 1024 * 1024)
    orders = pltpu.VMEM((MIDDLE_DILATION, rows, rows), bf16)

    def call(kernel, name, *args, **options):
        return pl.pallas_call(kernel, name=name, compiler_params=params, cost_estimate=cost(), **options)(*args)

    other_keys = partner(keys, "inner", 1)
    q, k, v, own_members, own_vm, *own_vr, coarse = call(
        functools.partial(prepare_kernel, CHUNKS),
        "prepare",
        middle_head_shift, coarse_head_shift, in_hbm(query), in_hbm(keys), in_hbm(values),
        out_shape=[
            *[pltpu.VMEM((rows, width), bf16)] * 3,
            pltpu.VMEM((2 * members, width), bf16),
            pltpu.VMEM((members, width), bf16),
            *[pltpu.VMEM((rows - members, c * HEAD_FEATURES), bf16) for c in CHUNKS],
            pltpu.VMEM((2, width), bf16),
        ],
        in_specs=[smem, smem, anywhere, anywhere, anywhere],
        out_specs=[vmem] * (6 + len(CHUNKS)),
        scratch_shapes=[orders, pltpu.SemaphoreType.DMA((3,))],
    )
    cross = partner(own_members, "inner", 2)
    near = gather_upper(stack(coarse, partner_elsewhere(coarse, 1)), "outer")
    own_scores, own_top = call(
        score_kernel,
        "score",
        q, k,
        out_shape=[pltpu.VMEM((HEAD_COUNT, rows, rows), f32), pltpu.VMEM((HEAD_COUNT, rows, LANES), f32)],
        in_specs=[vmem] * 2,
        out_specs=[vmem] * 2,
    )
    near, own_vm, own_top = lax.optimization_barrier((near, own_vm, own_top))
    other_vm = partner(own_vm, "inner", 1)
    cross, own_vr = lax.optimization_barrier((cross, own_vr))
    other_vr = [partner(piece, "inner", 1) for piece in own_vr]
    other_km = call(
        pick_kernel,
        "pick",
        middle_head_shift, other_keys,
        out_shape=pltpu.VMEM((members, width), bf16),
        in_specs=[smem, vmem],
        out_specs=vmem,
    )
    diagonal_k = partner(other_km, "inner", 2)
    other_keys = lax.optimization_barrier((other_keys, other_km))[0]

    def other_part(first, query):
        return call(
            functools.partial(other_kernel, first),
            "other",
            middle_head_shift, query, own_top, other_keys,
            out_shape=[
                pltpu.VMEM((half, rows, rows), bf16),
                pltpu.VMEM((half, rows, LANES), f32),
                pltpu.VMEM((rows, LANES), f32),
            ],
            in_specs=[smem] + [vmem] * 3,
            out_specs=[vmem] * 3,
            scratch_shapes=[orders],
        )

    weights_a, top_a, state_a = other_part(0, q)
    diagonal_v = partner(lax.optimization_barrier((other_vm, state_a))[0], "inner", 2)
    weights_b, top_b, state_b = other_part(half, lax.optimization_barrier((q, state_a, diagonal_k))[0])
    own_sum, own_total = call(
        own_kernel,
        "own",
        middle_head_shift, own_scores, top_a, top_b, v,
        out_shape=[pltpu.VMEM((rows, width), f32), pltpu.VMEM((rows, LANES), f32)],
        in_specs=[smem] + [vmem] * 4,
        out_specs=[vmem] * 2,
    )
    mine = jnp.concatenate([near, partner_elsewhere(near, 2)], axis=0)
    extra_sum, share = call(
        extra_kernel,
        "extra",
        middle_head_shift, coarse_head_shift, q, own_total, state_a, state_b, cross, diagonal_k, diagonal_v, mine,
        partner(mine, "outer", 1),
        out_shape=[pltpu.VMEM((rows, width), f32), pltpu.VMEM((rows, LANES), f32)],
        in_specs=[smem, smem] + [vmem] * 9,
        out_specs=[vmem] * 2,
    )

    out = []
    first = 0
    for chunk, vr in zip(CHUNKS, other_vr):
        heads = range(first, first + chunk)
        base, spread = call(
            functools.partial(base_kernel, heads),
            "base",
            extra_sum, share, own_sum,
            out_shape=[pltpu.VMEM((rows, chunk * HEAD_FEATURES), f32)] * 2,
            in_specs=[vmem] * 3,
            out_specs=[vmem] * 2,
        )
        args = [base, spread, weights_a, weights_b, other_vm, vr]
        out = [
            call(
                functools.partial(finish_kernel, heads),
                "finish",
                *args, *out,
                out_shape=jax.ShapeDtypeStruct((rows, width), bf16),
                in_specs=[vmem] * len(args) + [anywhere] * len(out),
                out_specs=anywhere,
                input_output_aliases={len(args): 0} if out else {},
                scratch_shapes=[pltpu.VMEM((chunk, rows, HEAD_FEATURES), bf16), pltpu.SemaphoreType.DMA((chunk,))],
            )
        ]
        first += chunk
    return out[0]


def solution(mesh):
    placed = (
        P(("outer", "inner"), None),
        P(("outer", "inner"), None),
        P(("outer", "inner"), None),
        P(),
        P(),
    )
    return jax.shard_map(
        on_device,
        mesh=mesh,
        in_specs=placed,
        out_specs=P(("outer", "inner"), None),
        check_vma=False,
    )
```

```python
import functools

import jax
import jax.numpy as jnp
from jax import lax
from jax.experimental import pallas as pl
from jax.experimental.pallas import tpu as pltpu
from jax.sharding import PartitionSpec as P

HEAD_COUNT = 16
HEAD_FEATURES = 128
MIDDLE_DILATION = 4
CHUNKS = (12, 4)
LANES = 128
SUBLANES = 16
EXP2_SCALE = HEAD_FEATURES ** (-0.5) * 1.4426950408889634
MASKED = -1e30


def partner(value, axis, mask):
    pairs = [(source, source ^ mask) for source in range(lax.axis_size(axis))]
    return lax.ppermute(value, axis, pairs)


def partner_elsewhere(value, inner_mask):
    outer = lax.axis_size("outer")
    outer_mask = 2 if outer > 2 else 0
    pairs = []
    for i in range(lax.axis_size("inner")):
        for o in range(outer):
            pairs.append((i * outer + o, (i ^ inner_mask) * outer + (o ^ outer_mask)))
    return lax.ppermute(value, ("inner", "outer"), pairs)


def one_hot(mask):
    return mask.astype(jnp.float32).astype(jnp.bfloat16)


def fill_orders(order_ref):
    rows = order_ref.shape[1]
    members = rows // MIDDLE_DILATION
    group = lax.broadcasted_iota(jnp.int32, (members, rows), 0)
    token = lax.broadcasted_iota(jnp.int32, (members, rows), 1)
    for place in range(MIDDLE_DILATION):
        block = one_hot(token == MIDDLE_DILATION * group + place)
        for shift in range(MIDDLE_DILATION):
            slot = (place - shift) % MIDDLE_DILATION
            order_ref[shift, slot * members : (slot + 1) * members] = block


def dot(a, b):
    return jnp.dot(a, b, preferred_element_type=jnp.float32)


def head_columns(head):
    return slice(head * HEAD_FEATURES, (head + 1) * HEAD_FEATURES)


def prepare_kernel(chunks, middle_ref, coarse_ref, q_hbm, k_hbm, v_hbm, *rest):
    q_ref, k_ref, v_ref, members_ref, vm_ref, *vr_refs, coarse_out_ref, order_ref, semaphores = rest
    pairs = ((k_hbm, k_ref), (v_hbm, v_ref), (q_hbm, q_ref))
    copies = [pltpu.make_async_copy(*pair, semaphores.at[i]) for i, pair in enumerate(pairs)]
    for copy in copies:
        copy.start()
    rows = k_ref.shape[0]
    members = rows // MIDDLE_DILATION
    fill_orders(order_ref)
    token = lax.broadcasted_iota(jnp.int32, (SUBLANES, rows), 1)
    first_row = lax.broadcasted_iota(jnp.int32, (SUBLANES, rows), 0) == 0
    second_row = lax.broadcasted_iota(jnp.int32, (SUBLANES, rows), 0) == 1
    copies[0].wait()
    copies[1].wait()
    head = 0
    for chunk, vr_ref in zip(chunks, vr_refs):
        for place in range(chunk):
            columns = head_columns(head)
            order = order_ref[middle_ref[head]]
            k, v = k_ref[:, columns], v_ref[:, columns]
            v_ordered = dot(order, v).astype(jnp.bfloat16)
            members_ref[:members, columns] = dot(order[:members], k).astype(jnp.bfloat16)
            members_ref[members:, columns] = v_ordered[:members]
            vm_ref[:, columns] = v_ordered[:members]
            vr_ref[:, head_columns(place)] = v_ordered[members:]
            chosen = token == coarse_ref[head]
            picked = dot(one_hot(chosen & first_row), k) + dot(one_hot(chosen & second_row), v)
            coarse_out_ref[:, columns] = picked[:2].astype(jnp.bfloat16)
            head += 1
    copies[2].wait()


def pick_kernel(middle_ref, k_ref, members_ref):
    rows = k_ref.shape[0]
    members = rows // MIDDLE_DILATION
    group = lax.broadcasted_iota(jnp.int32, (members, rows), 0)
    token = lax.broadcasted_iota(jnp.int32, (members, rows), 1)
    offset = token - MIDDLE_DILATION * group
    for head in range(HEAD_COUNT):
        columns = head_columns(head)
        chosen = one_hot(offset == middle_ref[head])
        members_ref[:, columns] = dot(chosen, k_ref[:, columns]).astype(jnp.bfloat16)


def dot_keys(q, keys):
    return lax.dot_general(q, keys, (((1,), (1,)), ((), ())), preferred_element_type=jnp.float32)


def dot_rows(a, b):
    return lax.dot_general(a, b, (((0,), (0,)), ((), ())), preferred_element_type=jnp.float32)


def side_by_side(columns):
    rows = columns[0].shape[0]
    lane = lax.broadcasted_iota(jnp.int32, (rows, LANES), 1)
    result = jnp.zeros((rows, LANES), jnp.float32)
    for place, column in enumerate(columns):
        result = jnp.where(lane == place, column, result)
    return result


def member_rows(rows, shift):
    row = lax.broadcasted_iota(jnp.int32, (rows, 1), 0)
    return (row & (MIDDLE_DILATION - 1)) == shift


def lane_tiles(part):
    return [part[:, i : i + LANES] for i in range(0, part.shape[1], LANES)]


def weights(part, top):
    return jnp.exp2((part - top) * EXP2_SCALE)


def score_kernel(q_ref, k_ref, scores_ref, top_ref):
    for head in range(HEAD_COUNT):
        columns = head_columns(head)
        own = dot_keys(q_ref[:, columns], k_ref[:, columns])
        top = jnp.max(functools.reduce(jnp.maximum, lane_tiles(own)), axis=1, keepdims=True)
        top_ref[head] = jnp.broadcast_to(top, top_ref.shape[1:])
        scores_ref[head] = own


def other_kernel(first, middle_ref, q_ref, own_top_ref, kp_ref, other_ref, top_ref, state_ref, order_ref):
    fill_orders(order_ref)
    rows = q_ref.shape[0]
    members = rows // MIDDLE_DILATION
    column = lax.broadcasted_iota(jnp.int32, (1, LANES), 1)
    tops, totals = [], []
    for place in range(other_ref.shape[0]):
        head = first + place
        columns = head_columns(head)
        shift = middle_ref[head]
        other_keys = dot(order_ref[shift], kp_ref[:, columns]).astype(jnp.bfloat16)
        other = dot_keys(q_ref[:, columns], other_keys)
        top = jnp.max(functools.reduce(jnp.maximum, lane_tiles(other)), axis=1, keepdims=True)
        top = jnp.maximum(top, own_top_ref[head])
        top_ref[place] = top
        tiles = [weights(tile, top) for tile in lane_tiles(other)]
        twice = member_rows(rows, shift) & (column < members)
        tiles[0] = jnp.where(twice, tiles[0] + tiles[0], tiles[0])
        tops.append(top)
        totals.append(jnp.sum(functools.reduce(jnp.add, tiles), axis=1, keepdims=True))
        other_ref[place] = jnp.concatenate(tiles, axis=1).astype(jnp.bfloat16)
    state_ref[...] = side_by_side(tops + totals)


def own_kernel(middle_ref, scores_ref, top_a_ref, top_b_ref, v_ref, sum_ref, total_ref):
    rows = v_ref.shape[0]
    half = HEAD_COUNT // 2
    lane = lax.broadcasted_iota(jnp.int32, (1, LANES), 1)
    totals = []
    for head in range(HEAD_COUNT):
        columns = head_columns(head)
        shift = middle_ref[head]
        top = (top_a_ref, top_b_ref)[head // half][head % half]
        twice = member_rows(rows, shift) & ((lane & (MIDDLE_DILATION - 1)) == shift)
        tiles = [weights(tile, top) for tile in lane_tiles(scores_ref[head])]
        tiles = [jnp.where(twice, tile + tile, tile) for tile in tiles]
        totals.append(jnp.sum(functools.reduce(jnp.add, tiles), axis=1, keepdims=True))
        sum_ref[:, columns] = dot(jnp.concatenate(tiles, axis=1).astype(jnp.bfloat16), v_ref[:, columns])
    total_ref[...] = side_by_side(totals)


def extra_kernel(
    middle_ref, coarse_ref, q_ref, own_total_ref, state_a_ref, state_b_ref, cross_ref, diagonal_k_ref, diagonal_v_ref, mine_ref,
    other_ref, sum_ref, share_ref,
):
    rows = q_ref.shape[0]
    members = rows // MIDDLE_DILATION
    half = HEAD_COUNT // 2
    far_rows, coarse_rows = 2 * members, 2 * mine_ref.shape[0]
    token = lax.broadcasted_iota(jnp.int32, (1, rows), 1)
    is_key = (lax.broadcasted_iota(jnp.int32, (coarse_rows, 1), 0) & 1) == 0
    own_totals = own_total_ref[...].T
    states = [ref[...].T for ref in (state_a_ref, state_b_ref)]
    shares = []
    for head in range(HEAD_COUNT):
        columns = head_columns(head)
        state, place = states[head // half], head % half
        pairs = [mine_ref[:, columns], other_ref[:, columns]]
        keys = jnp.concatenate([cross_ref[:members, columns], diagonal_k_ref[:, columns], *pairs], axis=0)
        values = jnp.concatenate([cross_ref[members:, columns], diagonal_v_ref[:, columns], *pairs], axis=0)
        scores = dot_keys(keys, q_ref[:, columns])
        far = jnp.where((token & (MIDDLE_DILATION - 1)) == middle_ref[head], scores[:far_rows], MASKED)
        coarse = jnp.where(is_key & (token == coarse_ref[head]), scores[far_rows:], MASKED)
        before = state[place : place + 1]
        top = jnp.maximum(before, jnp.max(far, axis=0, keepdims=True))
        top = jnp.maximum(top, jnp.max(coarse, axis=0, keepdims=True))
        far, coarse = weights(far, top), weights(coarse, top)
        kept = weights(before, top)
        total = kept * (state[half + place : half + place + 1] + own_totals[head : head + 1])
        total += jnp.sum(far, axis=0, keepdims=True) + jnp.sum(coarse, axis=0, keepdims=True)
        inverse = 1.0 / total
        shifted = pltpu.roll(coarse, 1, 0)
        mixed = jnp.concatenate([(far * inverse).astype(jnp.bfloat16), (shifted * inverse).astype(jnp.bfloat16)], axis=0)
        sum_ref[:, columns] = dot_rows(mixed, values)
        shares.append(kept * inverse)
    share_ref[:, :HEAD_COUNT] = jnp.concatenate(shares, axis=0).T


def base_kernel(heads, sum_ref, share_ref, own_ref, base_ref, spread_ref):
    shape = (sum_ref.shape[0], HEAD_FEATURES)
    for place, head in enumerate(heads):
        columns, place_columns = head_columns(head), head_columns(place)
        share = jnp.broadcast_to(share_ref[:, head : head + 1], shape)
        base_ref[:, place_columns] = sum_ref[:, columns] + share * own_ref[:, columns]
        spread_ref[:, place_columns] = share


def finish_kernel(heads, base_ref, spread_ref, other_a_ref, other_b_ref, vm_ref, vr_ref, *rest):
    out_ref, ready_ref, semaphores = rest[-3:]
    half = HEAD_COUNT // 2
    copies = []
    for place, head in enumerate(heads):
        columns = head_columns(place)
        other_ref = (other_a_ref, other_b_ref)[head // half]
        values = jnp.concatenate([vm_ref[:, head_columns(head)], vr_ref[:, columns]], axis=0)
        result = base_ref[:, columns] + spread_ref[:, columns] * dot(other_ref[head % half], values)
        ready_ref[place] = result.astype(jnp.bfloat16)
        target = out_ref.at[:, head_columns(head)]
        copies.append(pltpu.make_async_copy(ready_ref.at[place], target, semaphores.at[place]))
        copies[-1].start()
    for copy in copies:
        copy.wait()


def in_hbm(array):
    return pltpu.with_memory_space_constraint(array, pltpu.HBM)


def cost():
    return pl.CostEstimate(flops=0, bytes_accessed=0, transcendentals=0)


def stack_kernel(*refs):
    out_ref = refs[-1]
    out_ref[...] = jnp.concatenate([ref[...].astype(jnp.float32) for ref in refs[:-1]], axis=0).astype(out_ref.dtype)


def stack(*pieces):
    vmem = pl.BlockSpec(memory_space=pltpu.VMEM)
    rows = sum(piece.shape[0] for piece in pieces)
    return pl.pallas_call(
        stack_kernel,
        name="stack",
        out_shape=pltpu.VMEM((rows, pieces[0].shape[1]), pieces[0].dtype),
        in_specs=[vmem] * len(pieces),
        out_specs=vmem,
        compiler_params=pltpu.CompilerParams(vmem_limit_bytes=8 * 1024 * 1024),
        cost_estimate=cost(),
    )(*pieces)


def gather_upper(value, axis):
    size = lax.axis_size(axis)
    assert size & (size - 1) == 0
    bits = [2**j for j in range(1, size.bit_length() - 1)]
    for step in [bits[j : j + 2] for j in range(0, len(bits), 2)]:
        masks = step + [sum(step)] if len(step) == 2 else step
        value = stack(value, *[partner(value, axis, mask) for mask in masks])
    return value


def on_device(query, keys, values, middle_head_shift, coarse_head_shift):
    rows, width = query.shape
    members = rows // MIDDLE_DILATION
    half = HEAD_COUNT // 2
    bf16, f32 = jnp.bfloat16, jnp.float32
    smem = pl.BlockSpec(memory_space=pltpu.SMEM)
    vmem = pl.BlockSpec(memory_space=pltpu.VMEM)
    anywhere = pl.BlockSpec(memory_space=pl.ANY)
    params = pltpu.CompilerParams(vmem_limit_bytes=8 * 1024 * 1024)
    orders = pltpu.VMEM((MIDDLE_DILATION, rows, rows), bf16)

    def call(kernel, name, *args, **options):
        return pl.pallas_call(kernel, name=name, compiler_params=params, cost_estimate=cost(), **options)(*args)

    other_keys = partner(keys, "inner", 1)
    q, k, v, own_members, own_vm, *own_vr, coarse = call(
        functools.partial(prepare_kernel, CHUNKS),
        "prepare",
        middle_head_shift, coarse_head_shift, in_hbm(query), in_hbm(keys), in_hbm(values),
        out_shape=[
            *[pltpu.VMEM((rows, width), bf16)] * 3,
            pltpu.VMEM((2 * members, width), bf16),
            pltpu.VMEM((members, width), bf16),
            *[pltpu.VMEM((rows - members, c * HEAD_FEATURES), bf16) for c in CHUNKS],
            pltpu.VMEM((2, width), bf16),
        ],
        in_specs=[smem, smem, anywhere, anywhere, anywhere],
        out_specs=[vmem] * (6 + len(CHUNKS)),
        scratch_shapes=[orders, pltpu.SemaphoreType.DMA((3,))],
    )
    cross = partner(own_members, "inner", 2)
    near = gather_upper(stack(coarse, partner_elsewhere(coarse, 1)), "outer")
    own_scores, own_top = call(
        score_kernel,
        "score",
        q, k,
        out_shape=[pltpu.VMEM((HEAD_COUNT, rows, rows), f32), pltpu.VMEM((HEAD_COUNT, rows, LANES), f32)],
        in_specs=[vmem] * 2,
        out_specs=[vmem] * 2,
    )
    near, own_vm, own_top = lax.optimization_barrier((near, own_vm, own_top))
    other_vm = partner(own_vm, "inner", 1)
    cross, own_vr = lax.optimization_barrier((cross, own_vr))
    other_vr = [partner(piece, "inner", 1) for piece in own_vr]
    other_km = call(
        pick_kernel,
        "pick",
        middle_head_shift, other_keys,
        out_shape=pltpu.VMEM((members, width), bf16),
        in_specs=[smem, vmem],
        out_specs=vmem,
    )
    diagonal_k = partner(other_km, "inner", 2)
    other_keys = lax.optimization_barrier((other_keys, other_km))[0]

    def other_part(first, query):
        return call(
            functools.partial(other_kernel, first),
            "other",
            middle_head_shift, query, own_top, other_keys,
            out_shape=[
                pltpu.VMEM((half, rows, rows), bf16),
                pltpu.VMEM((half, rows, LANES), f32),
                pltpu.VMEM((rows, LANES), f32),
            ],
            in_specs=[smem] + [vmem] * 3,
            out_specs=[vmem] * 3,
            scratch_shapes=[orders],
        )

    weights_a, top_a, state_a = other_part(0, q)
    diagonal_v = partner(lax.optimization_barrier((other_vm, state_a))[0], "inner", 2)
    weights_b, top_b, state_b = other_part(half, lax.optimization_barrier((q, state_a, diagonal_k))[0])
    own_sum, own_total = call(
        own_kernel,
        "own",
        middle_head_shift, own_scores, top_a, top_b, v,
        out_shape=[pltpu.VMEM((rows, width), f32), pltpu.VMEM((rows, LANES), f32)],
        in_specs=[smem] + [vmem] * 4,
        out_specs=[vmem] * 2,
    )
    mine = jnp.concatenate([near, partner_elsewhere(near, 2)], axis=0)
    extra_sum, share = call(
        extra_kernel,
        "extra",
        middle_head_shift, coarse_head_shift, q, own_total, state_a, state_b, cross, diagonal_k, diagonal_v, mine,
        partner(mine, "outer", 1),
        out_shape=[pltpu.VMEM((rows, width), f32), pltpu.VMEM((rows, LANES), f32)],
        in_specs=[smem, smem] + [vmem] * 9,
        out_specs=[vmem] * 2,
    )

    out = []
    first = 0
    for chunk, vr in zip(CHUNKS, other_vr):
        heads = range(first, first + chunk)
        base, spread = call(
            functools.partial(base_kernel, heads),
            "base",
            extra_sum, share, own_sum,
            out_shape=[pltpu.VMEM((rows, chunk * HEAD_FEATURES), f32)] * 2,
            in_specs=[vmem] * 3,
            out_specs=[vmem] * 2,
        )
        args = [base, spread, weights_a, weights_b, other_vm, vr]
        out = [
            call(
                functools.partial(finish_kernel, heads),
                "finish",
                *args, *out,
                out_shape=jax.ShapeDtypeStruct((rows, width), bf16),
                in_specs=[vmem] * len(args) + [anywhere] * len(out),
                out_specs=anywhere,
                input_output_aliases={len(args): 0} if out else {},
                scratch_shapes=[pltpu.VMEM((chunk, rows, HEAD_FEATURES), bf16), pltpu.SemaphoreType.DMA((chunk,))],
            )
        ]
        first += chunk
    return out[0]


def solution(mesh):
    placed = (
        P(("outer", "inner"), None),
        P(("outer", "inner"), None),
        P(("outer", "inner"), None),
        P(),
        P(),
    )
    return jax.shard_map(
        on_device,
        mesh=mesh,
        in_specs=placed,
        out_specs=P(("outer", "inner"), None),
        check_vma=False,
    )
```

```python
import functools

import jax
import jax.numpy as jnp
from jax import lax
from jax.experimental import pallas as pl
from jax.experimental.pallas import tpu as pltpu
from jax.sharding import PartitionSpec as P

HEAD_COUNT = 16
HEAD_FEATURES = 128
MIDDLE_DILATION = 4
CHUNKS = (14, 2)
LANES = 128
SUBLANES = 16
EXP2_SCALE = HEAD_FEATURES ** (-0.5) * 1.4426950408889634
MASKED = -1e30


def partner(value, axis, mask):
    pairs = [(source, source ^ mask) for source in range(lax.axis_size(axis))]
    return lax.ppermute(value, axis, pairs)


def partner_elsewhere(value, inner_mask):
    outer = lax.axis_size("outer")
    outer_mask = 2 if outer > 2 else 0
    pairs = []
    for i in range(lax.axis_size("inner")):
        for o in range(outer):
            pairs.append((i * outer + o, (i ^ inner_mask) * outer + (o ^ outer_mask)))
    return lax.ppermute(value, ("inner", "outer"), pairs)


def one_hot(mask):
    return mask.astype(jnp.float32).astype(jnp.bfloat16)


def fill_orders(order_ref):
    rows = order_ref.shape[1]
    members = rows // MIDDLE_DILATION
    group = lax.broadcasted_iota(jnp.int32, (members, rows), 0)
    token = lax.broadcasted_iota(jnp.int32, (members, rows), 1)
    for place in range(MIDDLE_DILATION):
        block = one_hot(token == MIDDLE_DILATION * group + place)
        for shift in range(MIDDLE_DILATION):
            slot = (place - shift) % MIDDLE_DILATION
            order_ref[shift, slot * members : (slot + 1) * members] = block


def dot(a, b):
    return jnp.dot(a, b, preferred_element_type=jnp.float32)


def head_columns(head):
    return slice(head * HEAD_FEATURES, (head + 1) * HEAD_FEATURES)


def prepare_kernel(chunks, middle_ref, coarse_ref, q_hbm, k_hbm, v_hbm, *rest):
    q_ref, k_ref, v_ref, members_ref, vm_ref, *vr_refs, coarse_out_ref, order_ref, semaphores = rest
    pairs = ((k_hbm, k_ref), (v_hbm, v_ref), (q_hbm, q_ref))
    copies = [pltpu.make_async_copy(*pair, semaphores.at[i]) for i, pair in enumerate(pairs)]
    for copy in copies:
        copy.start()
    rows = k_ref.shape[0]
    members = rows // MIDDLE_DILATION
    fill_orders(order_ref)
    token = lax.broadcasted_iota(jnp.int32, (SUBLANES, rows), 1)
    first_row = lax.broadcasted_iota(jnp.int32, (SUBLANES, rows), 0) == 0
    second_row = lax.broadcasted_iota(jnp.int32, (SUBLANES, rows), 0) == 1
    copies[0].wait()
    copies[1].wait()
    head = 0
    for chunk, vr_ref in zip(chunks, vr_refs):
        for place in range(chunk):
            columns = head_columns(head)
            order = order_ref[middle_ref[head]]
            k, v = k_ref[:, columns], v_ref[:, columns]
            v_ordered = dot(order, v).astype(jnp.bfloat16)
            members_ref[:members, columns] = dot(order[:members], k).astype(jnp.bfloat16)
            members_ref[members:, columns] = v_ordered[:members]
            vm_ref[:, columns] = v_ordered[:members]
            vr_ref[:, head_columns(place)] = v_ordered[members:]
            chosen = token == coarse_ref[head]
            picked = dot(one_hot(chosen & first_row), k) + dot(one_hot(chosen & second_row), v)
            coarse_out_ref[:, columns] = picked[:2].astype(jnp.bfloat16)
            head += 1
    copies[2].wait()


def pick_kernel(middle_ref, k_ref, members_ref):
    rows = k_ref.shape[0]
    members = rows // MIDDLE_DILATION
    group = lax.broadcasted_iota(jnp.int32, (members, rows), 0)
    token = lax.broadcasted_iota(jnp.int32, (members, rows), 1)
    offset = token - MIDDLE_DILATION * group
    for head in range(HEAD_COUNT):
        columns = head_columns(head)
        chosen = one_hot(offset == middle_ref[head])
        members_ref[:, columns] = dot(chosen, k_ref[:, columns]).astype(jnp.bfloat16)


def dot_keys(q, keys):
    return lax.dot_general(q, keys, (((1,), (1,)), ((), ())), preferred_element_type=jnp.float32)


def dot_rows(a, b):
    return lax.dot_general(a, b, (((0,), (0,)), ((), ())), preferred_element_type=jnp.float32)


def side_by_side(columns):
    rows = columns[0].shape[0]
    lane = lax.broadcasted_iota(jnp.int32, (rows, LANES), 1)
    result = jnp.zeros((rows, LANES), jnp.float32)
    for place, column in enumerate(columns):
        result = jnp.where(lane == place, column, result)
    return result


def member_rows(rows, shift):
    row = lax.broadcasted_iota(jnp.int32, (rows, 1), 0)
    return (row & (MIDDLE_DILATION - 1)) == shift


def lane_tiles(part):
    return [part[:, i : i + LANES] for i in range(0, part.shape[1], LANES)]


def weights(part, top):
    return jnp.exp2((part - top) * EXP2_SCALE)


def score_kernel(q_ref, k_ref, scores_ref, top_ref):
    for head in range(HEAD_COUNT):
        columns = head_columns(head)
        own = dot_keys(q_ref[:, columns], k_ref[:, columns])
        top = jnp.max(functools.reduce(jnp.maximum, lane_tiles(own)), axis=1, keepdims=True)
        top_ref[head] = jnp.broadcast_to(top, top_ref.shape[1:])
        scores_ref[head] = own


def other_kernel(first, middle_ref, q_ref, own_top_ref, kp_ref, other_ref, top_ref, state_ref, order_ref):
    fill_orders(order_ref)
    rows = q_ref.shape[0]
    members = rows // MIDDLE_DILATION
    column = lax.broadcasted_iota(jnp.int32, (1, LANES), 1)
    tops, totals = [], []
    for place in range(other_ref.shape[0]):
        head = first + place
        columns = head_columns(head)
        shift = middle_ref[head]
        other_keys = dot(order_ref[shift], kp_ref[:, columns]).astype(jnp.bfloat16)
        other = dot_keys(q_ref[:, columns], other_keys)
        top = jnp.max(functools.reduce(jnp.maximum, lane_tiles(other)), axis=1, keepdims=True)
        top = jnp.maximum(top, own_top_ref[head])
        top_ref[place] = top
        tiles = [weights(tile, top) for tile in lane_tiles(other)]
        twice = member_rows(rows, shift) & (column < members)
        tiles[0] = jnp.where(twice, tiles[0] + tiles[0], tiles[0])
        tops.append(top)
        totals.append(jnp.sum(functools.reduce(jnp.add, tiles), axis=1, keepdims=True))
        other_ref[place] = jnp.concatenate(tiles, axis=1).astype(jnp.bfloat16)
    state_ref[...] = side_by_side(tops + totals)


def own_kernel(middle_ref, scores_ref, top_a_ref, top_b_ref, v_ref, sum_ref, total_ref):
    rows = v_ref.shape[0]
    half = HEAD_COUNT // 2
    lane = lax.broadcasted_iota(jnp.int32, (1, LANES), 1)
    totals = []
    for head in range(HEAD_COUNT):
        columns = head_columns(head)
        shift = middle_ref[head]
        top = (top_a_ref, top_b_ref)[head // half][head % half]
        twice = member_rows(rows, shift) & ((lane & (MIDDLE_DILATION - 1)) == shift)
        tiles = [weights(tile, top) for tile in lane_tiles(scores_ref[head])]
        tiles = [jnp.where(twice, tile + tile, tile) for tile in tiles]
        totals.append(jnp.sum(functools.reduce(jnp.add, tiles), axis=1, keepdims=True))
        sum_ref[:, columns] = dot(jnp.concatenate(tiles, axis=1).astype(jnp.bfloat16), v_ref[:, columns])
    total_ref[...] = side_by_side(totals)


def extra_kernel(
    middle_ref, coarse_ref, q_ref, own_total_ref, state_a_ref, state_b_ref, cross_ref, diagonal_k_ref, diagonal_v_ref, mine_ref,
    other_ref, sum_ref, share_ref,
):
    rows = q_ref.shape[0]
    members = rows // MIDDLE_DILATION
    half = HEAD_COUNT // 2
    far_rows, coarse_rows = 2 * members, 2 * mine_ref.shape[0]
    token = lax.broadcasted_iota(jnp.int32, (1, rows), 1)
    is_key = (lax.broadcasted_iota(jnp.int32, (coarse_rows, 1), 0) & 1) == 0
    own_totals = own_total_ref[...].T
    states = [ref[...].T for ref in (state_a_ref, state_b_ref)]
    shares = []
    for head in range(HEAD_COUNT):
        columns = head_columns(head)
        state, place = states[head // half], head % half
        pairs = [mine_ref[:, columns], other_ref[:, columns]]
        keys = jnp.concatenate([cross_ref[:members, columns], diagonal_k_ref[:, columns], *pairs], axis=0)
        values = jnp.concatenate([cross_ref[members:, columns], diagonal_v_ref[:, columns], *pairs], axis=0)
        scores = dot_keys(keys, q_ref[:, columns])
        far = jnp.where((token & (MIDDLE_DILATION - 1)) == middle_ref[head], scores[:far_rows], MASKED)
        coarse = jnp.where(is_key & (token == coarse_ref[head]), scores[far_rows:], MASKED)
        before = state[place : place + 1]
        top = jnp.maximum(before, jnp.max(far, axis=0, keepdims=True))
        top = jnp.maximum(top, jnp.max(coarse, axis=0, keepdims=True))
        far, coarse = weights(far, top), weights(coarse, top)
        kept = weights(before, top)
        total = kept * (state[half + place : half + place + 1] + own_totals[head : head + 1])
        total += jnp.sum(far, axis=0, keepdims=True) + jnp.sum(coarse, axis=0, keepdims=True)
        inverse = 1.0 / total
        shifted = pltpu.roll(coarse, 1, 0)
        mixed = jnp.concatenate([(far * inverse).astype(jnp.bfloat16), (shifted * inverse).astype(jnp.bfloat16)], axis=0)
        sum_ref[:, columns] = dot_rows(mixed, values)
        shares.append(kept * inverse)
    share_ref[:, :HEAD_COUNT] = jnp.concatenate(shares, axis=0).T


def base_kernel(heads, sum_ref, share_ref, own_ref, base_ref, spread_ref):
    shape = (sum_ref.shape[0], HEAD_FEATURES)
    for place, head in enumerate(heads):
        columns, place_columns = head_columns(head), head_columns(place)
        share = jnp.broadcast_to(share_ref[:, head : head + 1], shape)
        base_ref[:, place_columns] = sum_ref[:, columns] + share * own_ref[:, columns]
        spread_ref[:, place_columns] = share


def finish_kernel(heads, base_ref, spread_ref, other_a_ref, other_b_ref, vm_ref, vr_ref, *rest):
    out_ref, ready_ref, semaphores = rest[-3:]
    half = HEAD_COUNT // 2
    copies = []
    for place, head in enumerate(heads):
        columns = head_columns(place)
        other_ref = (other_a_ref, other_b_ref)[head // half]
        values = jnp.concatenate([vm_ref[:, head_columns(head)], vr_ref[:, columns]], axis=0)
        result = base_ref[:, columns] + spread_ref[:, columns] * dot(other_ref[head % half], values)
        ready_ref[place] = result.astype(jnp.bfloat16)
        target = out_ref.at[:, head_columns(head)]
        copies.append(pltpu.make_async_copy(ready_ref.at[place], target, semaphores.at[place]))
        copies[-1].start()
    for copy in copies:
        copy.wait()


def in_hbm(array):
    return pltpu.with_memory_space_constraint(array, pltpu.HBM)


def cost():
    return pl.CostEstimate(flops=0, bytes_accessed=0, transcendentals=0)


def stack_kernel(*refs):
    out_ref = refs[-1]
    out_ref[...] = jnp.concatenate([ref[...].astype(jnp.float32) for ref in refs[:-1]], axis=0).astype(out_ref.dtype)


def stack(*pieces):
    vmem = pl.BlockSpec(memory_space=pltpu.VMEM)
    rows = sum(piece.shape[0] for piece in pieces)
    return pl.pallas_call(
        stack_kernel,
        name="stack",
        out_shape=pltpu.VMEM((rows, pieces[0].shape[1]), pieces[0].dtype),
        in_specs=[vmem] * len(pieces),
        out_specs=vmem,
        compiler_params=pltpu.CompilerParams(vmem_limit_bytes=8 * 1024 * 1024),
        cost_estimate=cost(),
    )(*pieces)


def gather_upper(value, axis):
    size = lax.axis_size(axis)
    assert size & (size - 1) == 0
    bits = [2**j for j in range(1, size.bit_length() - 1)]
    for step in [bits[j : j + 2] for j in range(0, len(bits), 2)]:
        masks = step + [sum(step)] if len(step) == 2 else step
        value = stack(value, *[partner(value, axis, mask) for mask in masks])
    return value


def on_device(query, keys, values, middle_head_shift, coarse_head_shift):
    rows, width = query.shape
    members = rows // MIDDLE_DILATION
    half = HEAD_COUNT // 2
    bf16, f32 = jnp.bfloat16, jnp.float32
    smem = pl.BlockSpec(memory_space=pltpu.SMEM)
    vmem = pl.BlockSpec(memory_space=pltpu.VMEM)
    anywhere = pl.BlockSpec(memory_space=pl.ANY)
    params = pltpu.CompilerParams(vmem_limit_bytes=8 * 1024 * 1024)
    orders = pltpu.VMEM((MIDDLE_DILATION, rows, rows), bf16)

    def call(kernel, name, *args, **options):
        return pl.pallas_call(kernel, name=name, compiler_params=params, cost_estimate=cost(), **options)(*args)

    other_keys = partner(keys, "inner", 1)
    q, k, v, own_members, own_vm, *own_vr, coarse = call(
        functools.partial(prepare_kernel, CHUNKS),
        "prepare",
        middle_head_shift, coarse_head_shift, in_hbm(query), in_hbm(keys), in_hbm(values),
        out_shape=[
            *[pltpu.VMEM((rows, width), bf16)] * 3,
            pltpu.VMEM((2 * members, width), bf16),
            pltpu.VMEM((members, width), bf16),
            *[pltpu.VMEM((rows - members, c * HEAD_FEATURES), bf16) for c in CHUNKS],
            pltpu.VMEM((2, width), bf16),
        ],
        in_specs=[smem, smem, anywhere, anywhere, anywhere],
        out_specs=[vmem] * (6 + len(CHUNKS)),
        scratch_shapes=[orders, pltpu.SemaphoreType.DMA((3,))],
    )
    cross = partner(own_members, "inner", 2)
    near = gather_upper(stack(coarse, partner_elsewhere(coarse, 1)), "outer")
    own_scores, own_top = call(
        score_kernel,
        "score",
        q, k,
        out_shape=[pltpu.VMEM((HEAD_COUNT, rows, rows), f32), pltpu.VMEM((HEAD_COUNT, rows, LANES), f32)],
        in_specs=[vmem] * 2,
        out_specs=[vmem] * 2,
    )
    near, own_vm, own_top = lax.optimization_barrier((near, own_vm, own_top))
    other_vm = partner(own_vm, "inner", 1)
    cross, own_vr = lax.optimization_barrier((cross, own_vr))
    other_vr = [partner(piece, "inner", 1) for piece in own_vr]
    other_km = call(
        pick_kernel,
        "pick",
        middle_head_shift, other_keys,
        out_shape=pltpu.VMEM((members, width), bf16),
        in_specs=[smem, vmem],
        out_specs=vmem,
    )
    diagonal_k = partner(other_km, "inner", 2)
    other_keys = lax.optimization_barrier((other_keys, other_km))[0]

    def other_part(first, query):
        return call(
            functools.partial(other_kernel, first),
            "other",
            middle_head_shift, query, own_top, other_keys,
            out_shape=[
                pltpu.VMEM((half, rows, rows), bf16),
                pltpu.VMEM((half, rows, LANES), f32),
                pltpu.VMEM((rows, LANES), f32),
            ],
            in_specs=[smem] + [vmem] * 3,
            out_specs=[vmem] * 3,
            scratch_shapes=[orders],
        )

    weights_a, top_a, state_a = other_part(0, q)
    diagonal_v = partner(lax.optimization_barrier((other_vm, state_a))[0], "inner", 2)
    weights_b, top_b, state_b = other_part(half, lax.optimization_barrier((q, state_a, diagonal_k))[0])
    own_sum, own_total = call(
        own_kernel,
        "own",
        middle_head_shift, own_scores, top_a, top_b, v,
        out_shape=[pltpu.VMEM((rows, width), f32), pltpu.VMEM((rows, LANES), f32)],
        in_specs=[smem] + [vmem] * 4,
        out_specs=[vmem] * 2,
    )
    mine = jnp.concatenate([near, partner_elsewhere(near, 2)], axis=0)
    extra_sum, share = call(
        extra_kernel,
        "extra",
        middle_head_shift, coarse_head_shift, q, own_total, state_a, state_b, cross, diagonal_k, diagonal_v, mine,
        partner(mine, "outer", 1),
        out_shape=[pltpu.VMEM((rows, width), f32), pltpu.VMEM((rows, LANES), f32)],
        in_specs=[smem, smem] + [vmem] * 9,
        out_specs=[vmem] * 2,
    )

    out = []
    first = 0
    for chunk, vr in zip(CHUNKS, other_vr):
        heads = range(first, first + chunk)
        if not out:
            base, spread = call(
                functools.partial(base_kernel, heads),
                "base",
                extra_sum, share, own_sum,
                out_shape=[pltpu.VMEM((rows, chunk * HEAD_FEATURES), f32)] * 2,
                in_specs=[vmem] * 3,
                out_specs=[vmem] * 2,
            )
        else:
            chosen = slice(first * HEAD_FEATURES, None)
            spread = jnp.repeat(share[:, first:HEAD_COUNT], HEAD_FEATURES, axis=1)
            base = extra_sum[:, chosen] + spread * own_sum[:, chosen]
        args = [base, spread, weights_a, weights_b, other_vm, vr]
        out = [
            call(
                functools.partial(finish_kernel, heads),
                "finish",
                *args, *out,
                out_shape=jax.ShapeDtypeStruct((rows, width), bf16),
                in_specs=[vmem] * len(args) + [anywhere] * len(out),
                out_specs=anywhere,
                input_output_aliases={len(args): 0} if out else {},
                scratch_shapes=[pltpu.VMEM((chunk, rows, HEAD_FEATURES), bf16), pltpu.SemaphoreType.DMA((chunk,))],
            )
        ]
        first += chunk
    return out[0]


def solution(mesh):
    placed = (
        P(("outer", "inner"), None),
        P(("outer", "inner"), None),
        P(("outer", "inner"), None),
        P(),
        P(),
    )
    return jax.shard_map(
        on_device,
        mesh=mesh,
        in_specs=placed,
        out_specs=P(("outer", "inner"), None),
        check_vma=False,
    )
```

```python
import functools

import jax
import jax.numpy as jnp
from jax import lax
from jax.experimental import pallas as pl
from jax.experimental.pallas import tpu as pltpu
from jax.sharding import PartitionSpec as P

HEAD_COUNT = 16
HEAD_FEATURES = 128
MIDDLE_DILATION = 4
CHUNKS = (13, 3)
LATE = 10
LANES = 128
SUBLANES = 16
EXP2_SCALE = HEAD_FEATURES ** (-0.5) * 1.4426950408889634
MASKED = -1e30


def partner(value, axis, mask):
    pairs = [(source, source ^ mask) for source in range(lax.axis_size(axis))]
    return lax.ppermute(value, axis, pairs)


def partner_elsewhere(value, inner_mask):
    outer = lax.axis_size("outer")
    outer_mask = 2 if outer > 2 else 0
    pairs = []
    for i in range(lax.axis_size("inner")):
        for o in range(outer):
            pairs.append((i * outer + o, (i ^ inner_mask) * outer + (o ^ outer_mask)))
    return lax.ppermute(value, ("inner", "outer"), pairs)


def one_hot(mask):
    return mask.astype(jnp.float32).astype(jnp.bfloat16)


def fill_orders(order_ref):
    rows = order_ref.shape[1]
    members = rows // MIDDLE_DILATION
    group = lax.broadcasted_iota(jnp.int32, (members, rows), 0)
    token = lax.broadcasted_iota(jnp.int32, (members, rows), 1)
    for place in range(MIDDLE_DILATION):
        block = one_hot(token == MIDDLE_DILATION * group + place)
        for shift in range(MIDDLE_DILATION):
            slot = (place - shift) % MIDDLE_DILATION
            order_ref[shift, slot * members : (slot + 1) * members] = block


def dot(a, b):
    return jnp.dot(a, b, preferred_element_type=jnp.float32)


def head_columns(head):
    return slice(head * HEAD_FEATURES, (head + 1) * HEAD_FEATURES)


def prepare_kernel(chunks, middle_ref, coarse_ref, q_hbm, k_hbm, v_hbm, *rest):
    q_ref, k_ref, v_ref, members_ref, vm_ref, *vr_refs, coarse_out_ref, order_ref, semaphores = rest
    pairs = ((k_hbm, k_ref), (v_hbm, v_ref), (q_hbm, q_ref))
    copies = [pltpu.make_async_copy(*pair, semaphores.at[i]) for i, pair in enumerate(pairs)]
    for copy in copies:
        copy.start()
    rows = k_ref.shape[0]
    members = rows // MIDDLE_DILATION
    fill_orders(order_ref)
    token = lax.broadcasted_iota(jnp.int32, (SUBLANES, rows), 1)
    first_row = lax.broadcasted_iota(jnp.int32, (SUBLANES, rows), 0) == 0
    second_row = lax.broadcasted_iota(jnp.int32, (SUBLANES, rows), 0) == 1
    copies[0].wait()
    copies[1].wait()
    head = 0
    for chunk, vr_ref in zip(chunks, vr_refs):
        for place in range(chunk):
            columns = head_columns(head)
            order = order_ref[middle_ref[head]]
            k, v = k_ref[:, columns], v_ref[:, columns]
            v_ordered = dot(order, v).astype(jnp.bfloat16)
            members_ref[:members, columns] = dot(order[:members], k).astype(jnp.bfloat16)
            members_ref[members:, columns] = v_ordered[:members]
            vm_ref[:, columns] = v_ordered[:members]
            vr_ref[:, head_columns(place)] = v_ordered[members:]
            chosen = token == coarse_ref[head]
            picked = dot(one_hot(chosen & first_row), k) + dot(one_hot(chosen & second_row), v)
            coarse_out_ref[:, columns] = picked[:2].astype(jnp.bfloat16)
            head += 1
    copies[2].wait()


def pick_kernel(middle_ref, k_ref, members_ref):
    rows = k_ref.shape[0]
    members = rows // MIDDLE_DILATION
    group = lax.broadcasted_iota(jnp.int32, (members, rows), 0)
    token = lax.broadcasted_iota(jnp.int32, (members, rows), 1)
    offset = token - MIDDLE_DILATION * group
    for head in range(HEAD_COUNT):
        columns = head_columns(head)
        chosen = one_hot(offset == middle_ref[head])
        members_ref[:, columns] = dot(chosen, k_ref[:, columns]).astype(jnp.bfloat16)


def dot_keys(q, keys):
    return lax.dot_general(q, keys, (((1,), (1,)), ((), ())), preferred_element_type=jnp.float32)


def dot_rows(a, b):
    return lax.dot_general(a, b, (((0,), (0,)), ((), ())), preferred_element_type=jnp.float32)


def side_by_side(columns):
    rows = columns[0].shape[0]
    lane = lax.broadcasted_iota(jnp.int32, (rows, LANES), 1)
    result = jnp.zeros((rows, LANES), jnp.float32)
    for place, column in enumerate(columns):
        result = jnp.where(lane == place, column, result)
    return result


def member_rows(rows, shift):
    row = lax.broadcasted_iota(jnp.int32, (rows, 1), 0)
    return (row & (MIDDLE_DILATION - 1)) == shift


def lane_tiles(part):
    return [part[:, i : i + LANES] for i in range(0, part.shape[1], LANES)]


def weights(part, top):
    return jnp.exp2((part - top) * EXP2_SCALE)


def score_kernel(q_ref, k_ref, scores_ref, top_ref):
    for head in range(HEAD_COUNT):
        columns = head_columns(head)
        own = dot_keys(q_ref[:, columns], k_ref[:, columns])
        top = jnp.max(functools.reduce(jnp.maximum, lane_tiles(own)), axis=1, keepdims=True)
        top_ref[head] = jnp.broadcast_to(top, top_ref.shape[1:])
        scores_ref[head] = own


def other_kernel(first, middle_ref, q_ref, own_top_ref, kp_ref, other_ref, top_ref, state_ref, order_ref):
    fill_orders(order_ref)
    rows = q_ref.shape[0]
    members = rows // MIDDLE_DILATION
    column = lax.broadcasted_iota(jnp.int32, (1, LANES), 1)
    tops, totals = [], []
    for place in range(other_ref.shape[0]):
        head = first + place
        columns = head_columns(head)
        shift = middle_ref[head]
        other_keys = dot(order_ref[shift], kp_ref[:, columns]).astype(jnp.bfloat16)
        other = dot_keys(q_ref[:, columns], other_keys)
        top = jnp.max(functools.reduce(jnp.maximum, lane_tiles(other)), axis=1, keepdims=True)
        top = jnp.maximum(top, own_top_ref[head])
        top_ref[place] = top
        tiles = [weights(tile, top) for tile in lane_tiles(other)]
        twice = member_rows(rows, shift) & (column < members)
        tiles[0] = jnp.where(twice, tiles[0] + tiles[0], tiles[0])
        tops.append(top)
        totals.append(jnp.sum(functools.reduce(jnp.add, tiles), axis=1, keepdims=True))
        other_ref[place] = jnp.concatenate(tiles, axis=1).astype(jnp.bfloat16)
    state_ref[...] = side_by_side(tops + totals)


def own_kernel(middle_ref, scores_ref, top_a_ref, top_b_ref, v_ref, sum_ref, total_ref):
    rows = v_ref.shape[0]
    half = HEAD_COUNT // 2
    lane = lax.broadcasted_iota(jnp.int32, (1, LANES), 1)
    totals = []
    for head in range(HEAD_COUNT):
        columns = head_columns(head)
        shift = middle_ref[head]
        top = (top_a_ref, top_b_ref)[head // half][head % half]
        twice = member_rows(rows, shift) & ((lane & (MIDDLE_DILATION - 1)) == shift)
        tiles = [weights(tile, top) for tile in lane_tiles(scores_ref[head])]
        tiles = [jnp.where(twice, tile + tile, tile) for tile in tiles]
        totals.append(jnp.sum(functools.reduce(jnp.add, tiles), axis=1, keepdims=True))
        sum_ref[:, columns] = dot(jnp.concatenate(tiles, axis=1).astype(jnp.bfloat16), v_ref[:, columns])
    total_ref[...] = side_by_side(totals)


def extra_kernel(
    middle_ref, coarse_ref, q_ref, own_total_ref, state_a_ref, state_b_ref, cross_ref, diagonal_k_ref, diagonal_v_ref, mine_ref,
    other_ref, sum_ref, share_ref,
):
    rows = q_ref.shape[0]
    members = rows // MIDDLE_DILATION
    half = HEAD_COUNT // 2
    far_rows, coarse_rows = 2 * members, 2 * mine_ref.shape[0]
    token = lax.broadcasted_iota(jnp.int32, (1, rows), 1)
    is_key = (lax.broadcasted_iota(jnp.int32, (coarse_rows, 1), 0) & 1) == 0
    own_totals = own_total_ref[...].T
    states = [ref[...].T for ref in (state_a_ref, state_b_ref)]
    shares = []
    for head in range(HEAD_COUNT):
        columns = head_columns(head)
        state, place = states[head // half], head % half
        pairs = [mine_ref[:, columns], other_ref[:, columns]]
        keys = jnp.concatenate([cross_ref[:members, columns], diagonal_k_ref[:, columns], *pairs], axis=0)
        values = jnp.concatenate([cross_ref[members:, columns], diagonal_v_ref[:, columns], *pairs], axis=0)
        scores = dot_keys(keys, q_ref[:, columns])
        far = jnp.where((token & (MIDDLE_DILATION - 1)) == middle_ref[head], scores[:far_rows], MASKED)
        coarse = jnp.where(is_key & (token == coarse_ref[head]), scores[far_rows:], MASKED)
        before = state[place : place + 1]
        top = jnp.maximum(before, jnp.max(far, axis=0, keepdims=True))
        top = jnp.maximum(top, jnp.max(coarse, axis=0, keepdims=True))
        far, coarse = weights(far, top), weights(coarse, top)
        kept = weights(before, top)
        total = kept * (state[half + place : half + place + 1] + own_totals[head : head + 1])
        total += jnp.sum(far, axis=0, keepdims=True) + jnp.sum(coarse, axis=0, keepdims=True)
        inverse = 1.0 / total
        shifted = pltpu.roll(coarse, 1, 0)
        mixed = jnp.concatenate([(far * inverse).astype(jnp.bfloat16), (shifted * inverse).astype(jnp.bfloat16)], axis=0)
        sum_ref[:, columns] = dot_rows(mixed, values)
        shares.append(kept * inverse)
    share_ref[:, :HEAD_COUNT] = jnp.concatenate(shares, axis=0).T


def base_kernel(heads, sum_ref, share_ref, own_ref, base_ref, spread_ref):
    shape = (sum_ref.shape[0], HEAD_FEATURES)
    for place, head in enumerate(heads):
        columns, place_columns = head_columns(head), head_columns(place)
        share = jnp.broadcast_to(share_ref[:, head : head + 1], shape)
        base_ref[:, place_columns] = sum_ref[:, columns] + share * own_ref[:, columns]
        spread_ref[:, place_columns] = share


def finish_kernel(
    heads, base_ref, spread_ref, late_base_ref, late_spread_ref, other_a_ref, other_b_ref, vm_ref, vr_ref, *rest
):
    out_ref, ready_ref, semaphores = rest[-3:]
    half = HEAD_COUNT // 2
    copies = []
    for place, head in enumerate(heads):
        columns = head_columns(place)
        other_ref = (other_a_ref, other_b_ref)[head // half]
        values = jnp.concatenate([vm_ref[:, head_columns(head)], vr_ref[:, columns]], axis=0)
        result = dot(other_ref[head % half], values)
        if head < LATE:
            result = base_ref[:, head_columns(head)] + spread_ref[:, head_columns(head)] * result
        else:
            late = head_columns(head - LATE)
            result = late_base_ref[:, late] + late_spread_ref[:, late] * result
        ready_ref[place] = result.astype(jnp.bfloat16)
        target = out_ref.at[:, head_columns(head)]
        copies.append(pltpu.make_async_copy(ready_ref.at[place], target, semaphores.at[place]))
        copies[-1].start()
    for copy in copies:
        copy.wait()


def in_hbm(array):
    return pltpu.with_memory_space_constraint(array, pltpu.HBM)


def cost():
    return pl.CostEstimate(flops=0, bytes_accessed=0, transcendentals=0)


def stack_kernel(*refs):
    out_ref = refs[-1]
    out_ref[...] = jnp.concatenate([ref[...].astype(jnp.float32) for ref in refs[:-1]], axis=0).astype(out_ref.dtype)


def stack(*pieces):
    vmem = pl.BlockSpec(memory_space=pltpu.VMEM)
    rows = sum(piece.shape[0] for piece in pieces)
    return pl.pallas_call(
        stack_kernel,
        name="stack",
        out_shape=pltpu.VMEM((rows, pieces[0].shape[1]), pieces[0].dtype),
        in_specs=[vmem] * len(pieces),
        out_specs=vmem,
        compiler_params=pltpu.CompilerParams(vmem_limit_bytes=8 * 1024 * 1024),
        cost_estimate=cost(),
    )(*pieces)


def gather_upper(value, axis):
    size = lax.axis_size(axis)
    assert size & (size - 1) == 0
    bits = [2**j for j in range(1, size.bit_length() - 1)]
    for step in [bits[j : j + 2] for j in range(0, len(bits), 2)]:
        masks = step + [sum(step)] if len(step) == 2 else step
        value = stack(value, *[partner(value, axis, mask) for mask in masks])
    return value


def on_device(query, keys, values, middle_head_shift, coarse_head_shift):
    rows, width = query.shape
    members = rows // MIDDLE_DILATION
    half = HEAD_COUNT // 2
    bf16, f32 = jnp.bfloat16, jnp.float32
    smem = pl.BlockSpec(memory_space=pltpu.SMEM)
    vmem = pl.BlockSpec(memory_space=pltpu.VMEM)
    anywhere = pl.BlockSpec(memory_space=pl.ANY)
    params = pltpu.CompilerParams(vmem_limit_bytes=8 * 1024 * 1024)
    orders = pltpu.VMEM((MIDDLE_DILATION, rows, rows), bf16)

    def call(kernel, name, *args, **options):
        return pl.pallas_call(kernel, name=name, compiler_params=params, cost_estimate=cost(), **options)(*args)

    other_keys = partner(keys, "inner", 1)
    q, k, v, own_members, own_vm, *own_vr, coarse = call(
        functools.partial(prepare_kernel, CHUNKS),
        "prepare",
        middle_head_shift, coarse_head_shift, in_hbm(query), in_hbm(keys), in_hbm(values),
        out_shape=[
            *[pltpu.VMEM((rows, width), bf16)] * 3,
            pltpu.VMEM((2 * members, width), bf16),
            pltpu.VMEM((members, width), bf16),
            *[pltpu.VMEM((rows - members, c * HEAD_FEATURES), bf16) for c in CHUNKS],
            pltpu.VMEM((2, width), bf16),
        ],
        in_specs=[smem, smem, anywhere, anywhere, anywhere],
        out_specs=[vmem] * (6 + len(CHUNKS)),
        scratch_shapes=[orders, pltpu.SemaphoreType.DMA((3,))],
    )
    cross = partner(own_members, "inner", 2)
    near = gather_upper(stack(coarse, partner_elsewhere(coarse, 1)), "outer")
    own_scores, own_top = call(
        score_kernel,
        "score",
        q, k,
        out_shape=[pltpu.VMEM((HEAD_COUNT, rows, rows), f32), pltpu.VMEM((HEAD_COUNT, rows, LANES), f32)],
        in_specs=[vmem] * 2,
        out_specs=[vmem] * 2,
    )
    near, own_vm, own_top = lax.optimization_barrier((near, own_vm, own_top))
    other_vm = partner(own_vm, "inner", 1)
    cross, own_vr = lax.optimization_barrier((cross, own_vr))
    other_vr = [partner(piece, "inner", 1) for piece in own_vr]
    other_km = call(
        pick_kernel,
        "pick",
        middle_head_shift, other_keys,
        out_shape=pltpu.VMEM((members, width), bf16),
        in_specs=[smem, vmem],
        out_specs=vmem,
    )
    diagonal_k = partner(other_km, "inner", 2)
    other_keys = lax.optimization_barrier((other_keys, other_km))[0]

    def other_part(first, query):
        return call(
            functools.partial(other_kernel, first),
            "other",
            middle_head_shift, query, own_top, other_keys,
            out_shape=[
                pltpu.VMEM((half, rows, rows), bf16),
                pltpu.VMEM((half, rows, LANES), f32),
                pltpu.VMEM((rows, LANES), f32),
            ],
            in_specs=[smem] + [vmem] * 3,
            out_specs=[vmem] * 3,
            scratch_shapes=[orders],
        )

    weights_a, top_a, state_a = other_part(0, q)
    diagonal_v = partner(lax.optimization_barrier((other_vm, state_a))[0], "inner", 2)
    weights_b, top_b, state_b = other_part(half, lax.optimization_barrier((q, state_a, diagonal_k))[0])
    own_sum, own_total = call(
        own_kernel,
        "own",
        middle_head_shift, own_scores, top_a, top_b, v,
        out_shape=[pltpu.VMEM((rows, width), f32), pltpu.VMEM((rows, LANES), f32)],
        in_specs=[smem] + [vmem] * 4,
        out_specs=[vmem] * 2,
    )
    mine = jnp.concatenate([near, partner_elsewhere(near, 2)], axis=0)
    extra_sum, share = call(
        extra_kernel,
        "extra",
        middle_head_shift, coarse_head_shift, q, own_total, state_a, state_b, cross, diagonal_k, diagonal_v, mine,
        partner(mine, "outer", 1),
        out_shape=[pltpu.VMEM((rows, width), f32), pltpu.VMEM((rows, LANES), f32)],
        in_specs=[smem, smem] + [vmem] * 9,
        out_specs=[vmem] * 2,
    )

    base, spread = call(
        functools.partial(base_kernel, range(LATE)),
        "base",
        extra_sum, share, own_sum,
        out_shape=[pltpu.VMEM((rows, LATE * HEAD_FEATURES), f32)] * 2,
        in_specs=[vmem] * 3,
        out_specs=[vmem] * 2,
    )
    late = slice(LATE * HEAD_FEATURES, None)
    late_spread = jnp.repeat(share[:, LATE:HEAD_COUNT], HEAD_FEATURES, axis=1)
    late_base = extra_sum[:, late] + late_spread * own_sum[:, late]
    out = []
    first = 0
    for chunk, vr in zip(CHUNKS, other_vr):
        heads = range(first, first + chunk)
        args = [base, spread, late_base, late_spread, weights_a, weights_b, other_vm, vr]
        out = [
            call(
                functools.partial(finish_kernel, heads),
                "finish",
                *args, *out,
                out_shape=jax.ShapeDtypeStruct((rows, width), bf16),
                in_specs=[vmem] * len(args) + [anywhere] * len(out),
                out_specs=anywhere,
                input_output_aliases={len(args): 0} if out else {},
                scratch_shapes=[pltpu.VMEM((chunk, rows, HEAD_FEATURES), bf16), pltpu.SemaphoreType.DMA((chunk,))],
            )
        ]
        first += chunk
    return out[0]


def solution(mesh):
    placed = (
        P(("outer", "inner"), None),
        P(("outer", "inner"), None),
        P(("outer", "inner"), None),
        P(),
        P(),
    )
    return jax.shard_map(
        on_device,
        mesh=mesh,
        in_specs=placed,
        out_specs=P(("outer", "inner"), None),
        check_vma=False,
    )
```

```python
import functools

import jax
import jax.numpy as jnp
from jax import lax
from jax.experimental import pallas as pl
from jax.experimental.pallas import tpu as pltpu
from jax.sharding import PartitionSpec as P

HEAD_COUNT = 16
HEAD_FEATURES = 128
MIDDLE_DILATION = 4
CHUNKS = (14, 2)
LANES = 128
SUBLANES = 16
EXP2_SCALE = HEAD_FEATURES ** (-0.5) * 1.4426950408889634
MASKED = -1e30


def partner(value, axis, mask):
    pairs = [(source, source ^ mask) for source in range(lax.axis_size(axis))]
    return lax.ppermute(value, axis, pairs)


def partner_elsewhere(value, inner_mask):
    outer = lax.axis_size("outer")
    outer_mask = 2 if outer > 2 else 0
    pairs = []
    for i in range(lax.axis_size("inner")):
        for o in range(outer):
            pairs.append((i * outer + o, (i ^ inner_mask) * outer + (o ^ outer_mask)))
    return lax.ppermute(value, ("inner", "outer"), pairs)


def one_hot(mask):
    return mask.astype(jnp.float32).astype(jnp.bfloat16)


def fill_orders(order_ref):
    rows = order_ref.shape[1]
    members = rows // MIDDLE_DILATION
    group = lax.broadcasted_iota(jnp.int32, (members, rows), 0)
    token = lax.broadcasted_iota(jnp.int32, (members, rows), 1)
    for place in range(MIDDLE_DILATION):
        block = one_hot(token == MIDDLE_DILATION * group + place)
        for shift in range(MIDDLE_DILATION):
            slot = (place - shift) % MIDDLE_DILATION
            order_ref[shift, slot * members : (slot + 1) * members] = block


def dot(a, b):
    return jnp.dot(a, b, preferred_element_type=jnp.float32)


def head_columns(head):
    return slice(head * HEAD_FEATURES, (head + 1) * HEAD_FEATURES)


def prepare_kernel(chunks, middle_ref, coarse_ref, q_hbm, k_hbm, v_hbm, *rest):
    q_ref, k_ref, v_ref, members_ref, vm_ref, *vr_refs, coarse_out_ref, order_ref, semaphores = rest
    pairs = ((k_hbm, k_ref), (v_hbm, v_ref), (q_hbm, q_ref))
    copies = [pltpu.make_async_copy(*pair, semaphores.at[i]) for i, pair in enumerate(pairs)]
    for copy in copies:
        copy.start()
    rows = k_ref.shape[0]
    members = rows // MIDDLE_DILATION
    fill_orders(order_ref)
    token = lax.broadcasted_iota(jnp.int32, (SUBLANES, rows), 1)
    first_row = lax.broadcasted_iota(jnp.int32, (SUBLANES, rows), 0) == 0
    second_row = lax.broadcasted_iota(jnp.int32, (SUBLANES, rows), 0) == 1
    copies[0].wait()
    copies[1].wait()
    head = 0
    for chunk, vr_ref in zip(chunks, vr_refs):
        for place in range(chunk):
            columns = head_columns(head)
            order = order_ref[middle_ref[head]]
            k, v = k_ref[:, columns], v_ref[:, columns]
            v_ordered = dot(order, v).astype(jnp.bfloat16)
            members_ref[:members, columns] = dot(order[:members], k).astype(jnp.bfloat16)
            members_ref[members:, columns] = v_ordered[:members]
            vm_ref[:, columns] = v_ordered[:members]
            vr_ref[:, head_columns(place)] = v_ordered[members:]
            chosen = token == coarse_ref[head]
            picked = dot(one_hot(chosen & first_row), k) + dot(one_hot(chosen & second_row), v)
            coarse_out_ref[:, columns] = picked[:2].astype(jnp.bfloat16)
            head += 1
    copies[2].wait()


def pick_kernel(middle_ref, k_ref, members_ref):
    rows = k_ref.shape[0]
    members = rows // MIDDLE_DILATION
    group = lax.broadcasted_iota(jnp.int32, (members, rows), 0)
    token = lax.broadcasted_iota(jnp.int32, (members, rows), 1)
    offset = token - MIDDLE_DILATION * group
    for head in range(HEAD_COUNT):
        columns = head_columns(head)
        chosen = one_hot(offset == middle_ref[head])
        members_ref[:, columns] = dot(chosen, k_ref[:, columns]).astype(jnp.bfloat16)


def dot_keys(q, keys):
    return lax.dot_general(q, keys, (((1,), (1,)), ((), ())), preferred_element_type=jnp.float32)


def dot_rows(a, b):
    return lax.dot_general(a, b, (((0,), (0,)), ((), ())), preferred_element_type=jnp.float32)


def side_by_side(columns):
    rows = columns[0].shape[0]
    lane = lax.broadcasted_iota(jnp.int32, (rows, LANES), 1)
    result = jnp.zeros((rows, LANES), jnp.float32)
    for place, column in enumerate(columns):
        result = jnp.where(lane == place, column, result)
    return result


def member_rows(rows, shift):
    row = lax.broadcasted_iota(jnp.int32, (rows, 1), 0)
    return (row & (MIDDLE_DILATION - 1)) == shift


def lane_tiles(part):
    return [part[:, i : i + LANES] for i in range(0, part.shape[1], LANES)]


def weights(part, top):
    return jnp.exp2((part - top) * EXP2_SCALE)


def score_kernel(q_ref, k_ref, scores_ref, top_ref):
    for head in range(HEAD_COUNT):
        columns = head_columns(head)
        own = dot_keys(q_ref[:, columns], k_ref[:, columns])
        top = jnp.max(functools.reduce(jnp.maximum, lane_tiles(own)), axis=1, keepdims=True)
        top_ref[head] = jnp.broadcast_to(top, top_ref.shape[1:])
        scores_ref[head] = own


def other_kernel(first, middle_ref, q_ref, own_top_ref, kp_ref, other_ref, top_ref, state_ref, order_ref):
    fill_orders(order_ref)
    rows = q_ref.shape[0]
    members = rows // MIDDLE_DILATION
    column = lax.broadcasted_iota(jnp.int32, (1, LANES), 1)
    tops, totals = [], []
    for place in range(other_ref.shape[0]):
        head = first + place
        columns = head_columns(head)
        shift = middle_ref[head]
        other_keys = dot(order_ref[shift], kp_ref[:, columns]).astype(jnp.bfloat16)
        other = dot_keys(q_ref[:, columns], other_keys)
        top = jnp.max(functools.reduce(jnp.maximum, lane_tiles(other)), axis=1, keepdims=True)
        top = jnp.maximum(top, own_top_ref[head])
        top_ref[place] = top
        tiles = [weights(tile, top) for tile in lane_tiles(other)]
        twice = member_rows(rows, shift) & (column < members)
        tiles[0] = jnp.where(twice, tiles[0] + tiles[0], tiles[0])
        tops.append(top)
        totals.append(jnp.sum(functools.reduce(jnp.add, tiles), axis=1, keepdims=True))
        other_ref[place] = jnp.concatenate(tiles, axis=1).astype(jnp.bfloat16)
    state_ref[...] = side_by_side(tops + totals)


def own_kernel(middle_ref, scores_ref, top_a_ref, top_b_ref, v_ref, sum_ref, total_ref):
    rows = v_ref.shape[0]
    half = HEAD_COUNT // 2
    lane = lax.broadcasted_iota(jnp.int32, (1, LANES), 1)
    totals = []
    for head in range(HEAD_COUNT):
        columns = head_columns(head)
        shift = middle_ref[head]
        top = (top_a_ref, top_b_ref)[head // half][head % half]
        twice = member_rows(rows, shift) & ((lane & (MIDDLE_DILATION - 1)) == shift)
        tiles = [weights(tile, top) for tile in lane_tiles(scores_ref[head])]
        tiles = [jnp.where(twice, tile + tile, tile) for tile in tiles]
        totals.append(jnp.sum(functools.reduce(jnp.add, tiles), axis=1, keepdims=True))
        sum_ref[:, columns] = dot(jnp.concatenate(tiles, axis=1).astype(jnp.bfloat16), v_ref[:, columns])
    total_ref[...] = side_by_side(totals)


def extra_kernel(
    middle_ref, coarse_ref, q_ref, own_total_ref, state_a_ref, state_b_ref, cross_ref, diagonal_k_ref, diagonal_v_ref, mine_ref,
    other_ref, sum_ref, share_ref,
):
    rows = q_ref.shape[0]
    members = rows // MIDDLE_DILATION
    half = HEAD_COUNT // 2
    far_rows, coarse_rows = 2 * members, 2 * mine_ref.shape[0]
    token = lax.broadcasted_iota(jnp.int32, (1, rows), 1)
    is_key = (lax.broadcasted_iota(jnp.int32, (coarse_rows, 1), 0) & 1) == 0
    own_totals = own_total_ref[...].T
    states = [ref[...].T for ref in (state_a_ref, state_b_ref)]
    shares = []
    for head in range(HEAD_COUNT):
        columns = head_columns(head)
        state, place = states[head // half], head % half
        pairs = [mine_ref[:, columns], other_ref[:, columns]]
        keys = jnp.concatenate([cross_ref[:members, columns], diagonal_k_ref[:, columns], *pairs], axis=0)
        values = jnp.concatenate([cross_ref[members:, columns], diagonal_v_ref[:, columns], *pairs], axis=0)
        scores = dot_keys(keys, q_ref[:, columns])
        far = jnp.where((token & (MIDDLE_DILATION - 1)) == middle_ref[head], scores[:far_rows], MASKED)
        coarse = jnp.where(is_key & (token == coarse_ref[head]), scores[far_rows:], MASKED)
        before = state[place : place + 1]
        top = jnp.maximum(before, jnp.max(far, axis=0, keepdims=True))
        top = jnp.maximum(top, jnp.max(coarse, axis=0, keepdims=True))
        far, coarse = weights(far, top), weights(coarse, top)
        kept = weights(before, top)
        total = kept * (state[half + place : half + place + 1] + own_totals[head : head + 1])
        total += jnp.sum(far, axis=0, keepdims=True) + jnp.sum(coarse, axis=0, keepdims=True)
        inverse = 1.0 / total
        shifted = pltpu.roll(coarse, 1, 0)
        mixed = jnp.concatenate([(far * inverse).astype(jnp.bfloat16), (shifted * inverse).astype(jnp.bfloat16)], axis=0)
        sum_ref[:, columns] = dot_rows(mixed, values)
        shares.append(kept * inverse)
    share_ref[:, :HEAD_COUNT] = jnp.concatenate(shares, axis=0).T


def base_kernel(heads, sum_ref, share_ref, own_ref, base_ref, spread_ref):
    shape = (sum_ref.shape[0], HEAD_FEATURES)
    for place, head in enumerate(heads):
        columns, place_columns = head_columns(head), head_columns(place)
        share = jnp.broadcast_to(share_ref[:, head : head + 1], shape)
        base_ref[:, place_columns] = sum_ref[:, columns] + share * own_ref[:, columns]
        spread_ref[:, place_columns] = share


def finish_kernel(heads, base_ref, spread_ref, other_a_ref, other_b_ref, vm_ref, vr_ref, *rest):
    out_ref, ready_ref, semaphores = rest[-3:]
    half = HEAD_COUNT // 2
    copies = []
    for place, head in enumerate(heads):
        columns = head_columns(place)
        other_ref = (other_a_ref, other_b_ref)[head // half]
        values = jnp.concatenate([vm_ref[:, head_columns(head)], vr_ref[:, columns]], axis=0)
        result = base_ref[:, columns] + spread_ref[:, columns] * dot(other_ref[head % half], values)
        ready_ref[:, columns] = result.astype(jnp.bfloat16)
        target = out_ref.at[:, head_columns(head)]
        copies.append(pltpu.make_async_copy(ready_ref.at[:, columns], target, semaphores.at[place]))
        copies[-1].start()
    for copy in copies:
        copy.wait()


def in_hbm(array):
    return pltpu.with_memory_space_constraint(array, pltpu.HBM)


def cost():
    return pl.CostEstimate(flops=0, bytes_accessed=0, transcendentals=0)


def stack_kernel(*refs):
    out_ref = refs[-1]
    out_ref[...] = jnp.concatenate([ref[...].astype(jnp.float32) for ref in refs[:-1]], axis=0).astype(out_ref.dtype)


def stack(*pieces):
    vmem = pl.BlockSpec(memory_space=pltpu.VMEM)
    rows = sum(piece.shape[0] for piece in pieces)
    return pl.pallas_call(
        stack_kernel,
        name="stack",
        out_shape=pltpu.VMEM((rows, pieces[0].shape[1]), pieces[0].dtype),
        in_specs=[vmem] * len(pieces),
        out_specs=vmem,
        compiler_params=pltpu.CompilerParams(vmem_limit_bytes=8 * 1024 * 1024),
        cost_estimate=cost(),
    )(*pieces)


def gather_upper(value, axis):
    size = lax.axis_size(axis)
    assert size & (size - 1) == 0
    bits = [2**j for j in range(1, size.bit_length() - 1)]
    for step in [bits[j : j + 2] for j in range(0, len(bits), 2)]:
        masks = step + [sum(step)] if len(step) == 2 else step
        value = stack(value, *[partner(value, axis, mask) for mask in masks])
    return value


def on_device(query, keys, values, middle_head_shift, coarse_head_shift):
    rows, width = query.shape
    members = rows // MIDDLE_DILATION
    half = HEAD_COUNT // 2
    bf16, f32 = jnp.bfloat16, jnp.float32
    smem = pl.BlockSpec(memory_space=pltpu.SMEM)
    vmem = pl.BlockSpec(memory_space=pltpu.VMEM)
    anywhere = pl.BlockSpec(memory_space=pl.ANY)
    params = pltpu.CompilerParams(vmem_limit_bytes=8 * 1024 * 1024)
    orders = pltpu.VMEM((MIDDLE_DILATION, rows, rows), bf16)

    def call(kernel, name, *args, **options):
        return pl.pallas_call(kernel, name=name, compiler_params=params, cost_estimate=cost(), **options)(*args)

    other_keys = partner(keys, "inner", 1)
    q, k, v, own_members, own_vm, *own_vr, coarse = call(
        functools.partial(prepare_kernel, CHUNKS),
        "prepare",
        middle_head_shift, coarse_head_shift, in_hbm(query), in_hbm(keys), in_hbm(values),
        out_shape=[
            *[pltpu.VMEM((rows, width), bf16)] * 3,
            pltpu.VMEM((2 * members, width), bf16),
            pltpu.VMEM((members, width), bf16),
            *[pltpu.VMEM((rows - members, c * HEAD_FEATURES), bf16) for c in CHUNKS],
            pltpu.VMEM((2, width), bf16),
        ],
        in_specs=[smem, smem, anywhere, anywhere, anywhere],
        out_specs=[vmem] * (6 + len(CHUNKS)),
        scratch_shapes=[orders, pltpu.SemaphoreType.DMA((3,))],
    )
    cross = partner(own_members, "inner", 2)
    near = gather_upper(stack(coarse, partner_elsewhere(coarse, 1)), "outer")
    own_scores, own_top = call(
        score_kernel,
        "score",
        q, k,
        out_shape=[pltpu.VMEM((HEAD_COUNT, rows, rows), f32), pltpu.VMEM((HEAD_COUNT, rows, LANES), f32)],
        in_specs=[vmem] * 2,
        out_specs=[vmem] * 2,
    )
    near, own_vm, own_top = lax.optimization_barrier((near, own_vm, own_top))
    other_vm = partner(own_vm, "inner", 1)
    cross, own_vr = lax.optimization_barrier((cross, own_vr))
    other_vr = [partner(piece, "inner", 1) for piece in own_vr]
    other_km = call(
        pick_kernel,
        "pick",
        middle_head_shift, other_keys,
        out_shape=pltpu.VMEM((members, width), bf16),
        in_specs=[smem, vmem],
        out_specs=vmem,
    )
    diagonal_k = partner(other_km, "inner", 2)
    other_keys = lax.optimization_barrier((other_keys, other_km))[0]

    def other_part(first, query):
        return call(
            functools.partial(other_kernel, first),
            "other",
            middle_head_shift, query, own_top, other_keys,
            out_shape=[
                pltpu.VMEM((half, rows, rows), bf16),
                pltpu.VMEM((half, rows, LANES), f32),
                pltpu.VMEM((rows, LANES), f32),
            ],
            in_specs=[smem] + [vmem] * 3,
            out_specs=[vmem] * 3,
            scratch_shapes=[orders],
        )

    weights_a, top_a, state_a = other_part(0, q)
    diagonal_v = partner(lax.optimization_barrier((other_vm, state_a))[0], "inner", 2)
    weights_b, top_b, state_b = other_part(half, lax.optimization_barrier((q, state_a, diagonal_k))[0])
    own_sum, own_total = call(
        own_kernel,
        "own",
        middle_head_shift, own_scores, top_a, top_b, v,
        out_shape=[pltpu.VMEM((rows, width), f32), pltpu.VMEM((rows, LANES), f32)],
        in_specs=[smem] + [vmem] * 4,
        out_specs=[vmem] * 2,
    )
    mine = jnp.concatenate([near, partner_elsewhere(near, 2)], axis=0)
    extra_sum, share = call(
        extra_kernel,
        "extra",
        middle_head_shift, coarse_head_shift, q, own_total, state_a, state_b, cross, diagonal_k, diagonal_v, mine,
        partner(mine, "outer", 1),
        out_shape=[pltpu.VMEM((rows, width), f32), pltpu.VMEM((rows, LANES), f32)],
        in_specs=[smem, smem] + [vmem] * 9,
        out_specs=[vmem] * 2,
    )

    out = []
    first = 0
    for chunk, vr in zip(CHUNKS, other_vr):
        heads = range(first, first + chunk)
        if not out:
            base, spread = call(
                functools.partial(base_kernel, heads),
                "base",
                extra_sum, share, own_sum,
                out_shape=[pltpu.VMEM((rows, chunk * HEAD_FEATURES), f32)] * 2,
                in_specs=[vmem] * 3,
                out_specs=[vmem] * 2,
            )
        else:
            chosen = slice(first * HEAD_FEATURES, None)
            spread = jnp.repeat(share[:, first:HEAD_COUNT], HEAD_FEATURES, axis=1)
            base = extra_sum[:, chosen] + spread * own_sum[:, chosen]
        args = [base, spread, weights_a, weights_b, other_vm, vr]
        out = [
            call(
                functools.partial(finish_kernel, heads),
                "finish",
                *args, *out,
                out_shape=jax.ShapeDtypeStruct((rows, width), bf16),
                in_specs=[vmem] * len(args) + [anywhere] * len(out),
                out_specs=anywhere,
                input_output_aliases={len(args): 0} if out else {},
                scratch_shapes=[pltpu.VMEM((rows, chunk * HEAD_FEATURES), bf16), pltpu.SemaphoreType.DMA((chunk,))],
            )
        ]
        first += chunk
    return out[0]


def solution(mesh):
    placed = (
        P(("outer", "inner"), None),
        P(("outer", "inner"), None),
        P(("outer", "inner"), None),
        P(),
        P(),
    )
    return jax.shard_map(
        on_device,
        mesh=mesh,
        in_specs=placed,
        out_specs=P(("outer", "inner"), None),
        check_vma=False,
    )
```

```python
import functools

import jax
import jax.numpy as jnp
from jax import lax
from jax.experimental import pallas as pl
from jax.experimental.pallas import tpu as pltpu
from jax.sharding import PartitionSpec as P

HEAD_COUNT = 16
HEAD_FEATURES = 128
MIDDLE_DILATION = 4
CHUNKS = (13, 3)
LATE = 14
LANES = 128
SUBLANES = 16
EXP2_SCALE = HEAD_FEATURES ** (-0.5) * 1.4426950408889634
MASKED = -1e30


def partner(value, axis, mask):
    pairs = [(source, source ^ mask) for source in range(lax.axis_size(axis))]
    return lax.ppermute(value, axis, pairs)


def partner_elsewhere(value, inner_mask):
    outer = lax.axis_size("outer")
    outer_mask = 2 if outer > 2 else 0
    pairs = []
    for i in range(lax.axis_size("inner")):
        for o in range(outer):
            pairs.append((i * outer + o, (i ^ inner_mask) * outer + (o ^ outer_mask)))
    return lax.ppermute(value, ("inner", "outer"), pairs)


def one_hot(mask):
    return mask.astype(jnp.float32).astype(jnp.bfloat16)


def fill_orders(order_ref):
    rows = order_ref.shape[1]
    members = rows // MIDDLE_DILATION
    group = lax.broadcasted_iota(jnp.int32, (members, rows), 0)
    token = lax.broadcasted_iota(jnp.int32, (members, rows), 1)
    for place in range(MIDDLE_DILATION):
        block = one_hot(token == MIDDLE_DILATION * group + place)
        for shift in range(MIDDLE_DILATION):
            slot = (place - shift) % MIDDLE_DILATION
            order_ref[shift, slot * members : (slot + 1) * members] = block


def dot(a, b):
    return jnp.dot(a, b, preferred_element_type=jnp.float32)


def head_columns(head):
    return slice(head * HEAD_FEATURES, (head + 1) * HEAD_FEATURES)


def prepare_kernel(chunks, middle_ref, coarse_ref, q_hbm, k_hbm, v_hbm, *rest):
    q_ref, k_ref, v_ref, members_ref, vm_ref, *vr_refs, coarse_out_ref, order_ref, semaphores = rest
    pairs = ((k_hbm, k_ref), (v_hbm, v_ref), (q_hbm, q_ref))
    copies = [pltpu.make_async_copy(*pair, semaphores.at[i]) for i, pair in enumerate(pairs)]
    for copy in copies:
        copy.start()
    rows = k_ref.shape[0]
    members = rows // MIDDLE_DILATION
    fill_orders(order_ref)
    token = lax.broadcasted_iota(jnp.int32, (SUBLANES, rows), 1)
    first_row = lax.broadcasted_iota(jnp.int32, (SUBLANES, rows), 0) == 0
    second_row = lax.broadcasted_iota(jnp.int32, (SUBLANES, rows), 0) == 1
    copies[0].wait()
    copies[1].wait()
    head = 0
    for chunk, vr_ref in zip(chunks, vr_refs):
        for place in range(chunk):
            columns = head_columns(head)
            order = order_ref[middle_ref[head]]
            k, v = k_ref[:, columns], v_ref[:, columns]
            v_ordered = dot(order, v).astype(jnp.bfloat16)
            members_ref[:members, columns] = dot(order[:members], k).astype(jnp.bfloat16)
            members_ref[members:, columns] = v_ordered[:members]
            vm_ref[:, columns] = v_ordered[:members]
            vr_ref[:, head_columns(place)] = v_ordered[members:]
            chosen = token == coarse_ref[head]
            picked = dot(one_hot(chosen & first_row), k) + dot(one_hot(chosen & second_row), v)
            coarse_out_ref[:, columns] = picked[:2].astype(jnp.bfloat16)
            head += 1
    copies[2].wait()


def pick_kernel(middle_ref, k_ref, members_ref):
    rows = k_ref.shape[0]
    members = rows // MIDDLE_DILATION
    group = lax.broadcasted_iota(jnp.int32, (members, rows), 0)
    token = lax.broadcasted_iota(jnp.int32, (members, rows), 1)
    offset = token - MIDDLE_DILATION * group
    for head in range(HEAD_COUNT):
        columns = head_columns(head)
        chosen = one_hot(offset == middle_ref[head])
        members_ref[:, columns] = dot(chosen, k_ref[:, columns]).astype(jnp.bfloat16)


def dot_keys(q, keys):
    return lax.dot_general(q, keys, (((1,), (1,)), ((), ())), preferred_element_type=jnp.float32)


def dot_rows(a, b):
    return lax.dot_general(a, b, (((0,), (0,)), ((), ())), preferred_element_type=jnp.float32)


def side_by_side(columns):
    rows = columns[0].shape[0]
    lane = lax.broadcasted_iota(jnp.int32, (rows, LANES), 1)
    result = jnp.zeros((rows, LANES), jnp.float32)
    for place, column in enumerate(columns):
        result = jnp.where(lane == place, column, result)
    return result


def member_rows(rows, shift):
    row = lax.broadcasted_iota(jnp.int32, (rows, 1), 0)
    return (row & (MIDDLE_DILATION - 1)) == shift


def lane_tiles(part):
    return [part[:, i : i + LANES] for i in range(0, part.shape[1], LANES)]


def weights(part, top):
    return jnp.exp2((part - top) * EXP2_SCALE)


def score_kernel(q_ref, k_ref, scores_ref, top_ref):
    for head in range(HEAD_COUNT):
        columns = head_columns(head)
        own = dot_keys(q_ref[:, columns], k_ref[:, columns])
        top = jnp.max(functools.reduce(jnp.maximum, lane_tiles(own)), axis=1, keepdims=True)
        top_ref[head] = jnp.broadcast_to(top, top_ref.shape[1:])
        scores_ref[head] = own


def other_kernel(first, middle_ref, q_ref, own_top_ref, kp_ref, other_ref, top_ref, state_ref, order_ref):
    fill_orders(order_ref)
    rows = q_ref.shape[0]
    members = rows // MIDDLE_DILATION
    column = lax.broadcasted_iota(jnp.int32, (1, LANES), 1)
    tops, totals = [], []
    for place in range(other_ref.shape[0]):
        head = first + place
        columns = head_columns(head)
        shift = middle_ref[head]
        other_keys = dot(order_ref[shift], kp_ref[:, columns]).astype(jnp.bfloat16)
        other = dot_keys(q_ref[:, columns], other_keys)
        top = jnp.max(functools.reduce(jnp.maximum, lane_tiles(other)), axis=1, keepdims=True)
        top = jnp.maximum(top, own_top_ref[head])
        top_ref[place] = top
        tiles = [weights(tile, top) for tile in lane_tiles(other)]
        twice = member_rows(rows, shift) & (column < members)
        tiles[0] = jnp.where(twice, tiles[0] + tiles[0], tiles[0])
        tops.append(top)
        totals.append(jnp.sum(functools.reduce(jnp.add, tiles), axis=1, keepdims=True))
        other_ref[place] = jnp.concatenate(tiles, axis=1).astype(jnp.bfloat16)
    state_ref[...] = side_by_side(tops + totals)


def own_kernel(middle_ref, scores_ref, top_a_ref, top_b_ref, v_ref, sum_ref, total_ref):
    rows = v_ref.shape[0]
    half = HEAD_COUNT // 2
    lane = lax.broadcasted_iota(jnp.int32, (1, LANES), 1)
    totals = []
    for head in range(HEAD_COUNT):
        columns = head_columns(head)
        shift = middle_ref[head]
        top = (top_a_ref, top_b_ref)[head // half][head % half]
        twice = member_rows(rows, shift) & ((lane & (MIDDLE_DILATION - 1)) == shift)
        tiles = [weights(tile, top) for tile in lane_tiles(scores_ref[head])]
        tiles = [jnp.where(twice, tile + tile, tile) for tile in tiles]
        totals.append(jnp.sum(functools.reduce(jnp.add, tiles), axis=1, keepdims=True))
        sum_ref[:, columns] = dot(jnp.concatenate(tiles, axis=1).astype(jnp.bfloat16), v_ref[:, columns])
    total_ref[...] = side_by_side(totals)


def extra_kernel(
    middle_ref, coarse_ref, q_ref, own_total_ref, state_a_ref, state_b_ref, cross_ref, diagonal_k_ref, diagonal_v_ref, mine_ref,
    other_ref, sum_ref, share_ref,
):
    rows = q_ref.shape[0]
    members = rows // MIDDLE_DILATION
    half = HEAD_COUNT // 2
    far_rows, coarse_rows = 2 * members, 2 * mine_ref.shape[0]
    token = lax.broadcasted_iota(jnp.int32, (1, rows), 1)
    is_key = (lax.broadcasted_iota(jnp.int32, (coarse_rows, 1), 0) & 1) == 0
    own_totals = own_total_ref[...].T
    states = [ref[...].T for ref in (state_a_ref, state_b_ref)]
    shares = []
    for head in range(HEAD_COUNT):
        columns = head_columns(head)
        state, place = states[head // half], head % half
        pairs = [mine_ref[:, columns], other_ref[:, columns]]
        keys = jnp.concatenate([cross_ref[:members, columns], diagonal_k_ref[:, columns], *pairs], axis=0)
        values = jnp.concatenate([cross_ref[members:, columns], diagonal_v_ref[:, columns], *pairs], axis=0)
        scores = dot_keys(keys, q_ref[:, columns])
        far = jnp.where((token & (MIDDLE_DILATION - 1)) == middle_ref[head], scores[:far_rows], MASKED)
        coarse = jnp.where(is_key & (token == coarse_ref[head]), scores[far_rows:], MASKED)
        before = state[place : place + 1]
        top = jnp.maximum(before, jnp.max(far, axis=0, keepdims=True))
        top = jnp.maximum(top, jnp.max(coarse, axis=0, keepdims=True))
        far, coarse = weights(far, top), weights(coarse, top)
        kept = weights(before, top)
        total = kept * (state[half + place : half + place + 1] + own_totals[head : head + 1])
        total += jnp.sum(far, axis=0, keepdims=True) + jnp.sum(coarse, axis=0, keepdims=True)
        inverse = 1.0 / total
        shifted = pltpu.roll(coarse, 1, 0)
        mixed = jnp.concatenate([(far * inverse).astype(jnp.bfloat16), (shifted * inverse).astype(jnp.bfloat16)], axis=0)
        sum_ref[:, columns] = dot_rows(mixed, values)
        shares.append(kept * inverse)
    share_ref[:, :HEAD_COUNT] = jnp.concatenate(shares, axis=0).T


def base_kernel(heads, sum_ref, share_ref, own_ref, base_ref, spread_ref):
    shape = (sum_ref.shape[0], HEAD_FEATURES)
    for place, head in enumerate(heads):
        columns, place_columns = head_columns(head), head_columns(place)
        share = jnp.broadcast_to(share_ref[:, head : head + 1], shape)
        base_ref[:, place_columns] = sum_ref[:, columns] + share * own_ref[:, columns]
        spread_ref[:, place_columns] = share


def finish_kernel(
    heads, base_ref, spread_ref, late_base_ref, late_spread_ref, other_a_ref, other_b_ref, vm_ref, vr_ref, *rest
):
    out_ref, ready_ref, semaphores = rest[-3:]
    half = HEAD_COUNT // 2
    copies = []
    for place, head in enumerate(heads):
        columns = head_columns(place)
        other_ref = (other_a_ref, other_b_ref)[head // half]
        values = jnp.concatenate([vm_ref[:, head_columns(head)], vr_ref[:, columns]], axis=0)
        result = dot(other_ref[head % half], values)
        if head < LATE:
            result = base_ref[:, head_columns(head)] + spread_ref[:, head_columns(head)] * result
        else:
            late = head_columns(head - LATE)
            result = late_base_ref[:, late] + late_spread_ref[:, late] * result
        ready_ref[:, columns] = result.astype(jnp.bfloat16)
        target = out_ref.at[:, head_columns(head)]
        copies.append(pltpu.make_async_copy(ready_ref.at[:, columns], target, semaphores.at[place]))
        copies[-1].start()
    for copy in copies:
        copy.wait()


def in_hbm(array):
    return pltpu.with_memory_space_constraint(array, pltpu.HBM)


def cost():
    return pl.CostEstimate(flops=0, bytes_accessed=0, transcendentals=0)


def stack_kernel(*refs):
    out_ref = refs[-1]
    out_ref[...] = jnp.concatenate([ref[...].astype(jnp.float32) for ref in refs[:-1]], axis=0).astype(out_ref.dtype)


def stack(*pieces):
    vmem = pl.BlockSpec(memory_space=pltpu.VMEM)
    rows = sum(piece.shape[0] for piece in pieces)
    return pl.pallas_call(
        stack_kernel,
        name="stack",
        out_shape=pltpu.VMEM((rows, pieces[0].shape[1]), pieces[0].dtype),
        in_specs=[vmem] * len(pieces),
        out_specs=vmem,
        compiler_params=pltpu.CompilerParams(vmem_limit_bytes=8 * 1024 * 1024),
        cost_estimate=cost(),
    )(*pieces)


def gather_upper(value, axis):
    size = lax.axis_size(axis)
    assert size & (size - 1) == 0
    bits = [2**j for j in range(1, size.bit_length() - 1)]
    for step in [bits[j : j + 2] for j in range(0, len(bits), 2)]:
        masks = step + [sum(step)] if len(step) == 2 else step
        value = stack(value, *[partner(value, axis, mask) for mask in masks])
    return value


def on_device(query, keys, values, middle_head_shift, coarse_head_shift):
    rows, width = query.shape
    members = rows // MIDDLE_DILATION
    half = HEAD_COUNT // 2
    bf16, f32 = jnp.bfloat16, jnp.float32
    smem = pl.BlockSpec(memory_space=pltpu.SMEM)
    vmem = pl.BlockSpec(memory_space=pltpu.VMEM)
    anywhere = pl.BlockSpec(memory_space=pl.ANY)
    params = pltpu.CompilerParams(vmem_limit_bytes=8 * 1024 * 1024)
    orders = pltpu.VMEM((MIDDLE_DILATION, rows, rows), bf16)

    def call(kernel, name, *args, **options):
        return pl.pallas_call(kernel, name=name, compiler_params=params, cost_estimate=cost(), **options)(*args)

    other_keys = partner(keys, "inner", 1)
    q, k, v, own_members, own_vm, *own_vr, coarse = call(
        functools.partial(prepare_kernel, CHUNKS),
        "prepare",
        middle_head_shift, coarse_head_shift, in_hbm(query), in_hbm(keys), in_hbm(values),
        out_shape=[
            *[pltpu.VMEM((rows, width), bf16)] * 3,
            pltpu.VMEM((2 * members, width), bf16),
            pltpu.VMEM((members, width), bf16),
            *[pltpu.VMEM((rows - members, c * HEAD_FEATURES), bf16) for c in CHUNKS],
            pltpu.VMEM((2, width), bf16),
        ],
        in_specs=[smem, smem, anywhere, anywhere, anywhere],
        out_specs=[vmem] * (6 + len(CHUNKS)),
        scratch_shapes=[orders, pltpu.SemaphoreType.DMA((3,))],
    )
    cross = partner(own_members, "inner", 2)
    near = gather_upper(stack(coarse, partner_elsewhere(coarse, 1)), "outer")
    own_scores, own_top = call(
        score_kernel,
        "score",
        q, k,
        out_shape=[pltpu.VMEM((HEAD_COUNT, rows, rows), f32), pltpu.VMEM((HEAD_COUNT, rows, LANES), f32)],
        in_specs=[vmem] * 2,
        out_specs=[vmem] * 2,
    )
    near, own_vm, own_top = lax.optimization_barrier((near, own_vm, own_top))
    other_vm = partner(own_vm, "inner", 1)
    cross, own_vr = lax.optimization_barrier((cross, own_vr))
    other_vr = [partner(piece, "inner", 1) for piece in own_vr]
    other_km = call(
        pick_kernel,
        "pick",
        middle_head_shift, other_keys,
        out_shape=pltpu.VMEM((members, width), bf16),
        in_specs=[smem, vmem],
        out_specs=vmem,
    )
    diagonal_k = partner(other_km, "inner", 2)
    other_keys = lax.optimization_barrier((other_keys, other_km))[0]

    def other_part(first, query):
        return call(
            functools.partial(other_kernel, first),
            "other",
            middle_head_shift, query, own_top, other_keys,
            out_shape=[
                pltpu.VMEM((half, rows, rows), bf16),
                pltpu.VMEM((half, rows, LANES), f32),
                pltpu.VMEM((rows, LANES), f32),
            ],
            in_specs=[smem] + [vmem] * 3,
            out_specs=[vmem] * 3,
            scratch_shapes=[orders],
        )

    weights_a, top_a, state_a = other_part(0, q)
    diagonal_v = partner(lax.optimization_barrier((other_vm, state_a))[0], "inner", 2)
    weights_b, top_b, state_b = other_part(half, lax.optimization_barrier((q, state_a, diagonal_k))[0])
    own_sum, own_total = call(
        own_kernel,
        "own",
        middle_head_shift, own_scores, top_a, top_b, v,
        out_shape=[pltpu.VMEM((rows, width), f32), pltpu.VMEM((rows, LANES), f32)],
        in_specs=[smem] + [vmem] * 4,
        out_specs=[vmem] * 2,
    )
    mine = jnp.concatenate([near, partner_elsewhere(near, 2)], axis=0)
    extra_sum, share = call(
        extra_kernel,
        "extra",
        middle_head_shift, coarse_head_shift, q, own_total, state_a, state_b, cross, diagonal_k, diagonal_v, mine,
        partner(mine, "outer", 1),
        out_shape=[pltpu.VMEM((rows, width), f32), pltpu.VMEM((rows, LANES), f32)],
        in_specs=[smem, smem] + [vmem] * 9,
        out_specs=[vmem] * 2,
    )

    base, spread = call(
        functools.partial(base_kernel, range(LATE)),
        "base",
        extra_sum, share, own_sum,
        out_shape=[pltpu.VMEM((rows, LATE * HEAD_FEATURES), f32)] * 2,
        in_specs=[vmem] * 3,
        out_specs=[vmem] * 2,
    )
    late = slice(LATE * HEAD_FEATURES, None)
    late_spread = jnp.repeat(share[:, LATE:HEAD_COUNT], HEAD_FEATURES, axis=1)
    late_base = extra_sum[:, late] + late_spread * own_sum[:, late]
    out = []
    first = 0
    for chunk, vr in zip(CHUNKS, other_vr):
        heads = range(first, first + chunk)
        args = [base, spread, late_base, late_spread, weights_a, weights_b, other_vm, vr]
        out = [
            call(
                functools.partial(finish_kernel, heads),
                "finish",
                *args, *out,
                out_shape=jax.ShapeDtypeStruct((rows, width), bf16),
                in_specs=[vmem] * len(args) + [anywhere] * len(out),
                out_specs=anywhere,
                input_output_aliases={len(args): 0} if out else {},
                scratch_shapes=[pltpu.VMEM((rows, chunk * HEAD_FEATURES), bf16), pltpu.SemaphoreType.DMA((chunk,))],
            )
        ]
        first += chunk
    return out[0]


def solution(mesh):
    placed = (
        P(("outer", "inner"), None),
        P(("outer", "inner"), None),
        P(("outer", "inner"), None),
        P(),
        P(),
    )
    return jax.shard_map(
        on_device,
        mesh=mesh,
        in_specs=placed,
        out_specs=P(("outer", "inner"), None),
        check_vma=False,
    )
```

```python
import functools

import jax
import jax.numpy as jnp
from jax import lax
from jax.experimental import pallas as pl
from jax.experimental.pallas import tpu as pltpu
from jax.sharding import PartitionSpec as P

HEAD_COUNT = 16
HEAD_FEATURES = 128
MIDDLE_DILATION = 4
CHUNKS = (14, 2)
LANES = 128
SUBLANES = 16
EXP2_SCALE = HEAD_FEATURES ** (-0.5) * 1.4426950408889634
MASKED = -1e30


def partner(value, axis, mask):
    pairs = [(source, source ^ mask) for source in range(lax.axis_size(axis))]
    return lax.ppermute(value, axis, pairs)


def partner_elsewhere(value, inner_mask):
    outer = lax.axis_size("outer")
    outer_mask = 2 if outer > 2 else 0
    pairs = []
    for i in range(lax.axis_size("inner")):
        for o in range(outer):
            pairs.append((i * outer + o, (i ^ inner_mask) * outer + (o ^ outer_mask)))
    return lax.ppermute(value, ("inner", "outer"), pairs)


def one_hot(mask):
    return mask.astype(jnp.float32).astype(jnp.bfloat16)


def fill_orders(order_ref):
    rows = order_ref.shape[1]
    members = rows // MIDDLE_DILATION
    group = lax.broadcasted_iota(jnp.int32, (members, rows), 0)
    token = lax.broadcasted_iota(jnp.int32, (members, rows), 1)
    for place in range(MIDDLE_DILATION):
        block = one_hot(token == MIDDLE_DILATION * group + place)
        for shift in range(MIDDLE_DILATION):
            slot = (place - shift) % MIDDLE_DILATION
            order_ref[shift, slot * members : (slot + 1) * members] = block


def dot(a, b):
    return jnp.dot(a, b, preferred_element_type=jnp.float32)


def head_columns(head):
    return slice(head * HEAD_FEATURES, (head + 1) * HEAD_FEATURES)


def prepare_kernel(chunks, middle_ref, coarse_ref, q_hbm, k_hbm, v_hbm, *rest):
    q_ref, k_ref, v_ref, members_ref, vm_ref, *vr_refs, coarse_out_ref, order_ref, semaphores = rest
    pairs = ((k_hbm, k_ref), (v_hbm, v_ref), (q_hbm, q_ref))
    copies = [pltpu.make_async_copy(*pair, semaphores.at[i]) for i, pair in enumerate(pairs)]
    for copy in copies:
        copy.start()
    rows = k_ref.shape[0]
    members = rows // MIDDLE_DILATION
    fill_orders(order_ref)
    token = lax.broadcasted_iota(jnp.int32, (SUBLANES, rows), 1)
    first_row = lax.broadcasted_iota(jnp.int32, (SUBLANES, rows), 0) == 0
    second_row = lax.broadcasted_iota(jnp.int32, (SUBLANES, rows), 0) == 1
    copies[0].wait()
    copies[1].wait()
    head = 0
    for chunk, vr_ref in zip(chunks, vr_refs):
        for place in range(chunk):
            columns = head_columns(head)
            order = order_ref[middle_ref[head]]
            k, v = k_ref[:, columns], v_ref[:, columns]
            v_ordered = dot(order, v).astype(jnp.bfloat16)
            members_ref[:members, columns] = dot(order[:members], k).astype(jnp.bfloat16)
            members_ref[members:, columns] = v_ordered[:members]
            vm_ref[:, columns] = v_ordered[:members]
            vr_ref[:, head_columns(place)] = v_ordered[members:]
            chosen = token == coarse_ref[head]
            picked = dot(one_hot(chosen & first_row), k) + dot(one_hot(chosen & second_row), v)
            coarse_out_ref[:, columns] = picked[:2].astype(jnp.bfloat16)
            head += 1
    copies[2].wait()


def pick_kernel(middle_ref, k_ref, members_ref):
    rows = k_ref.shape[0]
    members = rows // MIDDLE_DILATION
    group = lax.broadcasted_iota(jnp.int32, (members, rows), 0)
    token = lax.broadcasted_iota(jnp.int32, (members, rows), 1)
    offset = token - MIDDLE_DILATION * group
    for head in range(HEAD_COUNT):
        columns = head_columns(head)
        chosen = one_hot(offset == middle_ref[head])
        members_ref[:, columns] = dot(chosen, k_ref[:, columns]).astype(jnp.bfloat16)


def dot_keys(q, keys):
    return lax.dot_general(q, keys, (((1,), (1,)), ((), ())), preferred_element_type=jnp.float32)


def dot_rows(a, b):
    return lax.dot_general(a, b, (((0,), (0,)), ((), ())), preferred_element_type=jnp.float32)


def side_by_side(columns):
    rows = columns[0].shape[0]
    lane = lax.broadcasted_iota(jnp.int32, (rows, LANES), 1)
    result = jnp.zeros((rows, LANES), jnp.float32)
    for place, column in enumerate(columns):
        result = jnp.where(lane == place, column, result)
    return result


def member_rows(rows, shift):
    row = lax.broadcasted_iota(jnp.int32, (rows, 1), 0)
    return (row & (MIDDLE_DILATION - 1)) == shift


def lane_tiles(part):
    return [part[:, i : i + LANES] for i in range(0, part.shape[1], LANES)]


def weights(part, top):
    return jnp.exp2((part - top) * EXP2_SCALE)


def score_kernel(q_ref, k_ref, scores_ref, top_ref):
    for head in range(HEAD_COUNT):
        columns = head_columns(head)
        own = dot_keys(q_ref[:, columns], k_ref[:, columns])
        top = jnp.max(functools.reduce(jnp.maximum, lane_tiles(own)), axis=1, keepdims=True)
        top_ref[head] = jnp.broadcast_to(top, top_ref.shape[1:])
        scores_ref[head] = own


def other_kernel(first, middle_ref, q_ref, own_top_ref, kp_ref, other_ref, top_ref, state_ref, order_ref):
    fill_orders(order_ref)
    rows = q_ref.shape[0]
    members = rows // MIDDLE_DILATION
    column = lax.broadcasted_iota(jnp.int32, (1, LANES), 1)
    tops, totals = [], []
    for place in range(other_ref.shape[0]):
        head = first + place
        columns = head_columns(head)
        shift = middle_ref[head]
        other_keys = dot(order_ref[shift], kp_ref[:, columns]).astype(jnp.bfloat16)
        other = dot_keys(q_ref[:, columns], other_keys)
        top = jnp.max(functools.reduce(jnp.maximum, lane_tiles(other)), axis=1, keepdims=True)
        top = jnp.maximum(top, own_top_ref[head])
        top_ref[place] = top
        tiles = [weights(tile, top) for tile in lane_tiles(other)]
        twice = member_rows(rows, shift) & (column < members)
        tiles[0] = jnp.where(twice, tiles[0] + tiles[0], tiles[0])
        tops.append(top)
        totals.append(jnp.sum(functools.reduce(jnp.add, tiles), axis=1, keepdims=True))
        other_ref[place] = jnp.concatenate(tiles, axis=1).astype(jnp.bfloat16)
    state_ref[...] = side_by_side(tops + totals)


def own_kernel(middle_ref, scores_ref, top_a_ref, top_b_ref, v_ref, sum_ref, total_ref):
    rows = v_ref.shape[0]
    half = HEAD_COUNT // 2
    lane = lax.broadcasted_iota(jnp.int32, (1, LANES), 1)
    totals = []
    for head in range(HEAD_COUNT):
        columns = head_columns(head)
        shift = middle_ref[head]
        top = (top_a_ref, top_b_ref)[head // half][head % half]
        twice = member_rows(rows, shift) & ((lane & (MIDDLE_DILATION - 1)) == shift)
        tiles = [weights(tile, top) for tile in lane_tiles(scores_ref[head])]
        tiles = [jnp.where(twice, tile + tile, tile) for tile in tiles]
        totals.append(jnp.sum(functools.reduce(jnp.add, tiles), axis=1, keepdims=True))
        sum_ref[:, columns] = dot(jnp.concatenate(tiles, axis=1).astype(jnp.bfloat16), v_ref[:, columns])
    total_ref[...] = side_by_side(totals)


def extra_kernel(
    middle_ref, coarse_ref, q_ref, own_total_ref, state_a_ref, state_b_ref, cross_ref, diagonal_k_ref, diagonal_v_ref, mine_ref,
    other_ref, sum_ref, share_ref,
):
    rows = q_ref.shape[0]
    members = rows // MIDDLE_DILATION
    half = HEAD_COUNT // 2
    far_rows, coarse_rows = 2 * members, 2 * mine_ref.shape[0]
    token = lax.broadcasted_iota(jnp.int32, (1, rows), 1)
    is_key = (lax.broadcasted_iota(jnp.int32, (coarse_rows, 1), 0) & 1) == 0
    own_totals = own_total_ref[...].T
    states = [ref[...].T for ref in (state_a_ref, state_b_ref)]
    shares = []
    for head in range(HEAD_COUNT):
        columns = head_columns(head)
        state, place = states[head // half], head % half
        pairs = [mine_ref[:, columns], other_ref[:, columns]]
        keys = jnp.concatenate([cross_ref[:members, columns], diagonal_k_ref[:, columns], *pairs], axis=0)
        values = jnp.concatenate([cross_ref[members:, columns], diagonal_v_ref[:, columns], *pairs], axis=0)
        scores = dot_keys(keys, q_ref[:, columns])
        far = jnp.where((token & (MIDDLE_DILATION - 1)) == middle_ref[head], scores[:far_rows], MASKED)
        coarse = jnp.where(is_key & (token == coarse_ref[head]), scores[far_rows:], MASKED)
        before = state[place : place + 1]
        top = jnp.maximum(before, jnp.max(far, axis=0, keepdims=True))
        top = jnp.maximum(top, jnp.max(coarse, axis=0, keepdims=True))
        far, coarse = weights(far, top), weights(coarse, top)
        kept = weights(before, top)
        total = kept * (state[half + place : half + place + 1] + own_totals[head : head + 1])
        total += jnp.sum(far, axis=0, keepdims=True) + jnp.sum(coarse, axis=0, keepdims=True)
        inverse = 1.0 / total
        shifted = pltpu.roll(coarse, 1, 0)
        mixed = jnp.concatenate([(far * inverse).astype(jnp.bfloat16), (shifted * inverse).astype(jnp.bfloat16)], axis=0)
        sum_ref[:, columns] = dot_rows(mixed, values)
        shares.append(kept * inverse)
    share_ref[:, :HEAD_COUNT] = jnp.concatenate(shares, axis=0).T


def base_kernel(heads, sum_ref, share_ref, own_ref, base_ref, spread_ref):
    shape = (sum_ref.shape[0], HEAD_FEATURES)
    for place, head in enumerate(heads):
        columns, place_columns = head_columns(head), head_columns(place)
        share = jnp.broadcast_to(share_ref[:, head : head + 1], shape)
        base_ref[:, place_columns] = sum_ref[:, columns] + share * own_ref[:, columns]
        spread_ref[:, place_columns] = share


def finish_kernel(heads, base_ref, spread_ref, other_a_ref, other_b_ref, vm_ref, vr_ref, *rest):
    out_ref, ready_ref, semaphores = rest[-3:]
    half = HEAD_COUNT // 2
    copies = []
    for place, head in enumerate(heads):
        columns = head_columns(place)
        other_ref = (other_a_ref, other_b_ref)[head // half]
        values = jnp.concatenate([vm_ref[:, head_columns(head)], vr_ref[:, columns]], axis=0)
        result = base_ref[:, columns] + spread_ref[:, columns] * dot(other_ref[head % half], values)
        ready_ref[:, columns] = result.astype(jnp.bfloat16)
        if (place + 1) % 2 == 0 or place + 1 == len(heads):
            pair = slice(place // 2 * 2 * HEAD_FEATURES, (place + 1) * HEAD_FEATURES)
            target = out_ref.at[:, heads[0] * HEAD_FEATURES + pair.start : heads[0] * HEAD_FEATURES + pair.stop]
            copies.append(pltpu.make_async_copy(ready_ref.at[:, pair], target, semaphores.at[place]))
            copies[-1].start()
    for copy in copies:
        copy.wait()


def in_hbm(array):
    return pltpu.with_memory_space_constraint(array, pltpu.HBM)


def cost():
    return pl.CostEstimate(flops=0, bytes_accessed=0, transcendentals=0)


def stack_kernel(*refs):
    out_ref = refs[-1]
    out_ref[...] = jnp.concatenate([ref[...].astype(jnp.float32) for ref in refs[:-1]], axis=0).astype(out_ref.dtype)


def stack(*pieces):
    vmem = pl.BlockSpec(memory_space=pltpu.VMEM)
    rows = sum(piece.shape[0] for piece in pieces)
    return pl.pallas_call(
        stack_kernel,
        name="stack",
        out_shape=pltpu.VMEM((rows, pieces[0].shape[1]), pieces[0].dtype),
        in_specs=[vmem] * len(pieces),
        out_specs=vmem,
        compiler_params=pltpu.CompilerParams(vmem_limit_bytes=8 * 1024 * 1024),
        cost_estimate=cost(),
    )(*pieces)


def gather_upper(value, axis):
    size = lax.axis_size(axis)
    assert size & (size - 1) == 0
    bits = [2**j for j in range(1, size.bit_length() - 1)]
    for step in [bits[j : j + 2] for j in range(0, len(bits), 2)]:
        masks = step + [sum(step)] if len(step) == 2 else step
        value = stack(value, *[partner(value, axis, mask) for mask in masks])
    return value


def on_device(query, keys, values, middle_head_shift, coarse_head_shift):
    rows, width = query.shape
    members = rows // MIDDLE_DILATION
    half = HEAD_COUNT // 2
    bf16, f32 = jnp.bfloat16, jnp.float32
    smem = pl.BlockSpec(memory_space=pltpu.SMEM)
    vmem = pl.BlockSpec(memory_space=pltpu.VMEM)
    anywhere = pl.BlockSpec(memory_space=pl.ANY)
    params = pltpu.CompilerParams(vmem_limit_bytes=8 * 1024 * 1024)
    orders = pltpu.VMEM((MIDDLE_DILATION, rows, rows), bf16)

    def call(kernel, name, *args, **options):
        return pl.pallas_call(kernel, name=name, compiler_params=params, cost_estimate=cost(), **options)(*args)

    other_keys = partner(keys, "inner", 1)
    q, k, v, own_members, own_vm, *own_vr, coarse = call(
        functools.partial(prepare_kernel, CHUNKS),
        "prepare",
        middle_head_shift, coarse_head_shift, in_hbm(query), in_hbm(keys), in_hbm(values),
        out_shape=[
            *[pltpu.VMEM((rows, width), bf16)] * 3,
            pltpu.VMEM((2 * members, width), bf16),
            pltpu.VMEM((members, width), bf16),
            *[pltpu.VMEM((rows - members, c * HEAD_FEATURES), bf16) for c in CHUNKS],
            pltpu.VMEM((2, width), bf16),
        ],
        in_specs=[smem, smem, anywhere, anywhere, anywhere],
        out_specs=[vmem] * (6 + len(CHUNKS)),
        scratch_shapes=[orders, pltpu.SemaphoreType.DMA((3,))],
    )
    cross = partner(own_members, "inner", 2)
    near = gather_upper(stack(coarse, partner_elsewhere(coarse, 1)), "outer")
    own_scores, own_top = call(
        score_kernel,
        "score",
        q, k,
        out_shape=[pltpu.VMEM((HEAD_COUNT, rows, rows), f32), pltpu.VMEM((HEAD_COUNT, rows, LANES), f32)],
        in_specs=[vmem] * 2,
        out_specs=[vmem] * 2,
    )
    near, own_vm, own_top = lax.optimization_barrier((near, own_vm, own_top))
    other_vm = partner(own_vm, "inner", 1)
    cross, own_vr = lax.optimization_barrier((cross, own_vr))
    other_vr = [partner(piece, "inner", 1) for piece in own_vr]
    other_km = call(
        pick_kernel,
        "pick",
        middle_head_shift, other_keys,
        out_shape=pltpu.VMEM((members, width), bf16),
        in_specs=[smem, vmem],
        out_specs=vmem,
    )
    diagonal_k = partner(other_km, "inner", 2)
    other_keys = lax.optimization_barrier((other_keys, other_km))[0]

    def other_part(first, query):
        return call(
            functools.partial(other_kernel, first),
            "other",
            middle_head_shift, query, own_top, other_keys,
            out_shape=[
                pltpu.VMEM((half, rows, rows), bf16),
                pltpu.VMEM((half, rows, LANES), f32),
                pltpu.VMEM((rows, LANES), f32),
            ],
            in_specs=[smem] + [vmem] * 3,
            out_specs=[vmem] * 3,
            scratch_shapes=[orders],
        )

    weights_a, top_a, state_a = other_part(0, q)
    diagonal_v = partner(lax.optimization_barrier((other_vm, state_a))[0], "inner", 2)
    weights_b, top_b, state_b = other_part(half, lax.optimization_barrier((q, state_a, diagonal_k))[0])
    own_sum, own_total = call(
        own_kernel,
        "own",
        middle_head_shift, own_scores, top_a, top_b, v,
        out_shape=[pltpu.VMEM((rows, width), f32), pltpu.VMEM((rows, LANES), f32)],
        in_specs=[smem] + [vmem] * 4,
        out_specs=[vmem] * 2,
    )
    mine = jnp.concatenate([near, partner_elsewhere(near, 2)], axis=0)
    extra_sum, share = call(
        extra_kernel,
        "extra",
        middle_head_shift, coarse_head_shift, q, own_total, state_a, state_b, cross, diagonal_k, diagonal_v, mine,
        partner(mine, "outer", 1),
        out_shape=[pltpu.VMEM((rows, width), f32), pltpu.VMEM((rows, LANES), f32)],
        in_specs=[smem, smem] + [vmem] * 9,
        out_specs=[vmem] * 2,
    )

    out = []
    first = 0
    for chunk, vr in zip(CHUNKS, other_vr):
        heads = range(first, first + chunk)
        if not out:
            base, spread = call(
                functools.partial(base_kernel, heads),
                "base",
                extra_sum, share, own_sum,
                out_shape=[pltpu.VMEM((rows, chunk * HEAD_FEATURES), f32)] * 2,
                in_specs=[vmem] * 3,
                out_specs=[vmem] * 2,
            )
        else:
            chosen = slice(first * HEAD_FEATURES, None)
            spread = jnp.repeat(share[:, first:HEAD_COUNT], HEAD_FEATURES, axis=1)
            base = extra_sum[:, chosen] + spread * own_sum[:, chosen]
        args = [base, spread, weights_a, weights_b, other_vm, vr]
        out = [
            call(
                functools.partial(finish_kernel, heads),
                "finish",
                *args, *out,
                out_shape=jax.ShapeDtypeStruct((rows, width), bf16),
                in_specs=[vmem] * len(args) + [anywhere] * len(out),
                out_specs=anywhere,
                input_output_aliases={len(args): 0} if out else {},
                scratch_shapes=[pltpu.VMEM((rows, chunk * HEAD_FEATURES), bf16), pltpu.SemaphoreType.DMA((chunk,))],
            )
        ]
        first += chunk
    return out[0]


def solution(mesh):
    placed = (
        P(("outer", "inner"), None),
        P(("outer", "inner"), None),
        P(("outer", "inner"), None),
        P(),
        P(),
    )
    return jax.shard_map(
        on_device,
        mesh=mesh,
        in_specs=placed,
        out_specs=P(("outer", "inner"), None),
        check_vma=False,
    )
```

```python
import functools

import jax
import jax.numpy as jnp
from jax import lax
from jax.experimental import pallas as pl
from jax.experimental.pallas import tpu as pltpu
from jax.sharding import PartitionSpec as P

HEAD_COUNT = 16
HEAD_FEATURES = 128
MIDDLE_DILATION = 4
CHUNKS = (13, 3)
LATE = 14
LANES = 128
SUBLANES = 16
EXP2_SCALE = HEAD_FEATURES ** (-0.5) * 1.4426950408889634
MASKED = -1e30


def partner(value, axis, mask):
    pairs = [(source, source ^ mask) for source in range(lax.axis_size(axis))]
    return lax.ppermute(value, axis, pairs)


def partner_elsewhere(value, inner_mask):
    outer = lax.axis_size("outer")
    outer_mask = 2 if outer > 2 else 0
    pairs = []
    for i in range(lax.axis_size("inner")):
        for o in range(outer):
            pairs.append((i * outer + o, (i ^ inner_mask) * outer + (o ^ outer_mask)))
    return lax.ppermute(value, ("inner", "outer"), pairs)


def one_hot(mask):
    return mask.astype(jnp.float32).astype(jnp.bfloat16)


def fill_orders(order_ref):
    rows = order_ref.shape[1]
    members = rows // MIDDLE_DILATION
    group = lax.broadcasted_iota(jnp.int32, (members, rows), 0)
    token = lax.broadcasted_iota(jnp.int32, (members, rows), 1)
    for place in range(MIDDLE_DILATION):
        block = one_hot(token == MIDDLE_DILATION * group + place)
        for shift in range(MIDDLE_DILATION):
            slot = (place - shift) % MIDDLE_DILATION
            order_ref[shift, slot * members : (slot + 1) * members] = block


def dot(a, b):
    return jnp.dot(a, b, preferred_element_type=jnp.float32)


def head_columns(head):
    return slice(head * HEAD_FEATURES, (head + 1) * HEAD_FEATURES)


def prepare_kernel(chunks, middle_ref, coarse_ref, q_hbm, k_hbm, v_hbm, *rest):
    q_ref, k_ref, v_ref, members_ref, vm_ref, *vr_refs, coarse_out_ref, order_ref, semaphores = rest
    pairs = ((k_hbm, k_ref), (v_hbm, v_ref), (q_hbm, q_ref))
    copies = [pltpu.make_async_copy(*pair, semaphores.at[i]) for i, pair in enumerate(pairs)]
    for copy in copies:
        copy.start()
    rows = k_ref.shape[0]
    members = rows // MIDDLE_DILATION
    fill_orders(order_ref)
    token = lax.broadcasted_iota(jnp.int32, (SUBLANES, rows), 1)
    first_row = lax.broadcasted_iota(jnp.int32, (SUBLANES, rows), 0) == 0
    second_row = lax.broadcasted_iota(jnp.int32, (SUBLANES, rows), 0) == 1
    copies[0].wait()
    copies[1].wait()
    head = 0
    for chunk, vr_ref in zip(chunks, vr_refs):
        for place in range(chunk):
            columns = head_columns(head)
            order = order_ref[middle_ref[head]]
            k, v = k_ref[:, columns], v_ref[:, columns]
            v_ordered = dot(order, v).astype(jnp.bfloat16)
            members_ref[:members, columns] = dot(order[:members], k).astype(jnp.bfloat16)
            members_ref[members:, columns] = v_ordered[:members]
            vm_ref[:, columns] = v_ordered[:members]
            vr_ref[:, head_columns(place)] = v_ordered[members:]
            chosen = token == coarse_ref[head]
            picked = dot(one_hot(chosen & first_row), k) + dot(one_hot(chosen & second_row), v)
            coarse_out_ref[:, columns] = picked[:2].astype(jnp.bfloat16)
            head += 1
    copies[2].wait()


def pick_kernel(middle_ref, k_ref, members_ref):
    rows = k_ref.shape[0]
    members = rows // MIDDLE_DILATION
    group = lax.broadcasted_iota(jnp.int32, (members, rows), 0)
    token = lax.broadcasted_iota(jnp.int32, (members, rows), 1)
    offset = token - MIDDLE_DILATION * group
    for head in range(HEAD_COUNT):
        columns = head_columns(head)
        chosen = one_hot(offset == middle_ref[head])
        members_ref[:, columns] = dot(chosen, k_ref[:, columns]).astype(jnp.bfloat16)


def dot_keys(q, keys):
    return lax.dot_general(q, keys, (((1,), (1,)), ((), ())), preferred_element_type=jnp.float32)


def dot_rows(a, b):
    return lax.dot_general(a, b, (((0,), (0,)), ((), ())), preferred_element_type=jnp.float32)


def side_by_side(columns):
    rows = columns[0].shape[0]
    lane = lax.broadcasted_iota(jnp.int32, (rows, LANES), 1)
    result = jnp.zeros((rows, LANES), jnp.float32)
    for place, column in enumerate(columns):
        result = jnp.where(lane == place, column, result)
    return result


def member_rows(rows, shift):
    row = lax.broadcasted_iota(jnp.int32, (rows, 1), 0)
    return (row & (MIDDLE_DILATION - 1)) == shift


def lane_tiles(part):
    return [part[:, i : i + LANES] for i in range(0, part.shape[1], LANES)]


def weights(part, top):
    return jnp.exp2((part - top) * EXP2_SCALE)


def score_kernel(q_ref, k_ref, scores_ref, top_ref):
    for head in range(HEAD_COUNT):
        columns = head_columns(head)
        own = dot_keys(q_ref[:, columns], k_ref[:, columns])
        top = jnp.max(functools.reduce(jnp.maximum, lane_tiles(own)), axis=1, keepdims=True)
        top_ref[head] = jnp.broadcast_to(top, top_ref.shape[1:])
        scores_ref[head] = own


def other_kernel(first, middle_ref, q_ref, own_top_ref, kp_ref, other_ref, top_ref, state_ref, order_ref):
    fill_orders(order_ref)
    rows = q_ref.shape[0]
    members = rows // MIDDLE_DILATION
    column = lax.broadcasted_iota(jnp.int32, (1, LANES), 1)
    tops, totals = [], []
    for place in range(other_ref.shape[0]):
        head = first + place
        columns = head_columns(head)
        shift = middle_ref[head]
        other_keys = dot(order_ref[shift], kp_ref[:, columns]).astype(jnp.bfloat16)
        other = dot_keys(q_ref[:, columns], other_keys)
        top = jnp.max(functools.reduce(jnp.maximum, lane_tiles(other)), axis=1, keepdims=True)
        top = jnp.maximum(top, own_top_ref[head])
        top_ref[place] = top
        tiles = [weights(tile, top) for tile in lane_tiles(other)]
        twice = member_rows(rows, shift) & (column < members)
        tiles[0] = jnp.where(twice, tiles[0] + tiles[0], tiles[0])
        tops.append(top)
        totals.append(jnp.sum(functools.reduce(jnp.add, tiles), axis=1, keepdims=True))
        other_ref[place] = jnp.concatenate(tiles, axis=1).astype(jnp.bfloat16)
    state_ref[...] = side_by_side(tops + totals)


def own_kernel(middle_ref, scores_ref, top_a_ref, top_b_ref, v_ref, sum_ref, total_ref):
    rows = v_ref.shape[0]
    half = HEAD_COUNT // 2
    lane = lax.broadcasted_iota(jnp.int32, (1, LANES), 1)
    totals = []
    for head in range(HEAD_COUNT):
        columns = head_columns(head)
        shift = middle_ref[head]
        top = (top_a_ref, top_b_ref)[head // half][head % half]
        twice = member_rows(rows, shift) & ((lane & (MIDDLE_DILATION - 1)) == shift)
        tiles = [weights(tile, top) for tile in lane_tiles(scores_ref[head])]
        tiles = [jnp.where(twice, tile + tile, tile) for tile in tiles]
        totals.append(jnp.sum(functools.reduce(jnp.add, tiles), axis=1, keepdims=True))
        sum_ref[:, columns] = dot(jnp.concatenate(tiles, axis=1).astype(jnp.bfloat16), v_ref[:, columns])
    total_ref[...] = side_by_side(totals)


def extra_kernel(
    middle_ref, coarse_ref, q_ref, own_total_ref, state_a_ref, state_b_ref, cross_ref, diagonal_k_ref, diagonal_v_ref, mine_ref,
    other_ref, sum_ref, share_ref,
):
    rows = q_ref.shape[0]
    members = rows // MIDDLE_DILATION
    half = HEAD_COUNT // 2
    far_rows, coarse_rows = 2 * members, 2 * mine_ref.shape[0]
    token = lax.broadcasted_iota(jnp.int32, (1, rows), 1)
    is_key = (lax.broadcasted_iota(jnp.int32, (coarse_rows, 1), 0) & 1) == 0
    own_totals = own_total_ref[...].T
    states = [ref[...].T for ref in (state_a_ref, state_b_ref)]
    shares = []
    for head in range(HEAD_COUNT):
        columns = head_columns(head)
        state, place = states[head // half], head % half
        pairs = [mine_ref[:, columns], other_ref[:, columns]]
        keys = jnp.concatenate([cross_ref[:members, columns], diagonal_k_ref[:, columns], *pairs], axis=0)
        values = jnp.concatenate([cross_ref[members:, columns], diagonal_v_ref[:, columns], *pairs], axis=0)
        scores = dot_keys(keys, q_ref[:, columns])
        far = jnp.where((token & (MIDDLE_DILATION - 1)) == middle_ref[head], scores[:far_rows], MASKED)
        coarse = jnp.where(is_key & (token == coarse_ref[head]), scores[far_rows:], MASKED)
        before = state[place : place + 1]
        top = jnp.maximum(before, jnp.max(far, axis=0, keepdims=True))
        top = jnp.maximum(top, jnp.max(coarse, axis=0, keepdims=True))
        far, coarse = weights(far, top), weights(coarse, top)
        kept = weights(before, top)
        total = kept * (state[half + place : half + place + 1] + own_totals[head : head + 1])
        total += jnp.sum(far, axis=0, keepdims=True) + jnp.sum(coarse, axis=0, keepdims=True)
        inverse = 1.0 / total
        shifted = pltpu.roll(coarse, 1, 0)
        mixed = jnp.concatenate([(far * inverse).astype(jnp.bfloat16), (shifted * inverse).astype(jnp.bfloat16)], axis=0)
        sum_ref[:, columns] = dot_rows(mixed, values)
        shares.append(kept * inverse)
    share_ref[:, :HEAD_COUNT] = jnp.concatenate(shares, axis=0).T


def base_kernel(heads, sum_ref, share_ref, own_ref, base_ref, spread_ref):
    shape = (sum_ref.shape[0], HEAD_FEATURES)
    for place, head in enumerate(heads):
        columns, place_columns = head_columns(head), head_columns(place)
        share = jnp.broadcast_to(share_ref[:, head : head + 1], shape)
        base_ref[:, place_columns] = sum_ref[:, columns] + share * own_ref[:, columns]
        spread_ref[:, place_columns] = share


def finish_kernel(
    heads, base_ref, spread_ref, late_base_ref, late_spread_ref, other_a_ref, other_b_ref, vm_ref, vr_ref, *rest
):
    out_ref, ready_ref, semaphores = rest[-3:]
    half = HEAD_COUNT // 2
    copies = []
    for place, head in enumerate(heads):
        columns = head_columns(place)
        other_ref = (other_a_ref, other_b_ref)[head // half]
        values = jnp.concatenate([vm_ref[:, head_columns(head)], vr_ref[:, columns]], axis=0)
        result = dot(other_ref[head % half], values)
        if head < LATE:
            result = base_ref[:, head_columns(head)] + spread_ref[:, head_columns(head)] * result
        else:
            late = head_columns(head - LATE)
            result = late_base_ref[:, late] + late_spread_ref[:, late] * result
        ready_ref[:, columns] = result.astype(jnp.bfloat16)
        if (place + 1) % 2 == 0 or place + 1 == len(heads):
            pair = slice(place // 2 * 2 * HEAD_FEATURES, (place + 1) * HEAD_FEATURES)
            target = out_ref.at[:, heads[0] * HEAD_FEATURES + pair.start : heads[0] * HEAD_FEATURES + pair.stop]
            copies.append(pltpu.make_async_copy(ready_ref.at[:, pair], target, semaphores.at[place]))
            copies[-1].start()
    for copy in copies:
        copy.wait()


def in_hbm(array):
    return pltpu.with_memory_space_constraint(array, pltpu.HBM)


def cost():
    return pl.CostEstimate(flops=0, bytes_accessed=0, transcendentals=0)


def stack_kernel(*refs):
    out_ref = refs[-1]
    out_ref[...] = jnp.concatenate([ref[...].astype(jnp.float32) for ref in refs[:-1]], axis=0).astype(out_ref.dtype)


def stack(*pieces):
    vmem = pl.BlockSpec(memory_space=pltpu.VMEM)
    rows = sum(piece.shape[0] for piece in pieces)
    return pl.pallas_call(
        stack_kernel,
        name="stack",
        out_shape=pltpu.VMEM((rows, pieces[0].shape[1]), pieces[0].dtype),
        in_specs=[vmem] * len(pieces),
        out_specs=vmem,
        compiler_params=pltpu.CompilerParams(vmem_limit_bytes=8 * 1024 * 1024),
        cost_estimate=cost(),
    )(*pieces)


def gather_upper(value, axis):
    size = lax.axis_size(axis)
    assert size & (size - 1) == 0
    bits = [2**j for j in range(1, size.bit_length() - 1)]
    for step in [bits[j : j + 2] for j in range(0, len(bits), 2)]:
        masks = step + [sum(step)] if len(step) == 2 else step
        value = stack(value, *[partner(value, axis, mask) for mask in masks])
    return value


def on_device(query, keys, values, middle_head_shift, coarse_head_shift):
    rows, width = query.shape
    members = rows // MIDDLE_DILATION
    half = HEAD_COUNT // 2
    bf16, f32 = jnp.bfloat16, jnp.float32
    smem = pl.BlockSpec(memory_space=pltpu.SMEM)
    vmem = pl.BlockSpec(memory_space=pltpu.VMEM)
    anywhere = pl.BlockSpec(memory_space=pl.ANY)
    params = pltpu.CompilerParams(vmem_limit_bytes=8 * 1024 * 1024)
    orders = pltpu.VMEM((MIDDLE_DILATION, rows, rows), bf16)

    def call(kernel, name, *args, **options):
        return pl.pallas_call(kernel, name=name, compiler_params=params, cost_estimate=cost(), **options)(*args)

    other_keys = partner(keys, "inner", 1)
    q, k, v, own_members, own_vm, *own_vr, coarse = call(
        functools.partial(prepare_kernel, CHUNKS),
        "prepare",
        middle_head_shift, coarse_head_shift, in_hbm(query), in_hbm(keys), in_hbm(values),
        out_shape=[
            *[pltpu.VMEM((rows, width), bf16)] * 3,
            pltpu.VMEM((2 * members, width), bf16),
            pltpu.VMEM((members, width), bf16),
            *[pltpu.VMEM((rows - members, c * HEAD_FEATURES), bf16) for c in CHUNKS],
            pltpu.VMEM((2, width), bf16),
        ],
        in_specs=[smem, smem, anywhere, anywhere, anywhere],
        out_specs=[vmem] * (6 + len(CHUNKS)),
        scratch_shapes=[orders, pltpu.SemaphoreType.DMA((3,))],
    )
    cross = partner(own_members, "inner", 2)
    near = gather_upper(stack(coarse, partner_elsewhere(coarse, 1)), "outer")
    own_scores, own_top = call(
        score_kernel,
        "score",
        q, k,
        out_shape=[pltpu.VMEM((HEAD_COUNT, rows, rows), f32), pltpu.VMEM((HEAD_COUNT, rows, LANES), f32)],
        in_specs=[vmem] * 2,
        out_specs=[vmem] * 2,
    )
    near, own_vm, own_top = lax.optimization_barrier((near, own_vm, own_top))
    other_vm = partner(own_vm, "inner", 1)
    cross, own_vr = lax.optimization_barrier((cross, own_vr))
    other_vr = [partner(piece, "inner", 1) for piece in own_vr]
    other_km = call(
        pick_kernel,
        "pick",
        middle_head_shift, other_keys,
        out_shape=pltpu.VMEM((members, width), bf16),
        in_specs=[smem, vmem],
        out_specs=vmem,
    )
    diagonal_k = partner(other_km, "inner", 2)
    other_keys = lax.optimization_barrier((other_keys, other_km))[0]

    def other_part(first, query):
        return call(
            functools.partial(other_kernel, first),
            "other",
            middle_head_shift, query, own_top, other_keys,
            out_shape=[
                pltpu.VMEM((half, rows, rows), bf16),
                pltpu.VMEM((half, rows, LANES), f32),
                pltpu.VMEM((rows, LANES), f32),
            ],
            in_specs=[smem] + [vmem] * 3,
            out_specs=[vmem] * 3,
            scratch_shapes=[orders],
        )

    weights_a, top_a, state_a = other_part(0, q)
    diagonal_v = partner(lax.optimization_barrier((other_vm, state_a))[0], "inner", 2)
    weights_b, top_b, state_b = other_part(half, lax.optimization_barrier((q, state_a, diagonal_k))[0])
    own_sum, own_total = call(
        own_kernel,
        "own",
        middle_head_shift, own_scores, top_a, top_b, v,
        out_shape=[pltpu.VMEM((rows, width), f32), pltpu.VMEM((rows, LANES), f32)],
        in_specs=[smem] + [vmem] * 4,
        out_specs=[vmem] * 2,
    )
    mine = jnp.concatenate([near, partner_elsewhere(near, 2)], axis=0)
    extra_sum, share = call(
        extra_kernel,
        "extra",
        middle_head_shift, coarse_head_shift, q, own_total, state_a, state_b, cross, diagonal_k, diagonal_v, mine,
        partner(mine, "outer", 1),
        out_shape=[pltpu.VMEM((rows, width), f32), pltpu.VMEM((rows, LANES), f32)],
        in_specs=[smem, smem] + [vmem] * 9,
        out_specs=[vmem] * 2,
    )

    base, spread = call(
        functools.partial(base_kernel, range(LATE)),
        "base",
        extra_sum, share, own_sum,
        out_shape=[pltpu.VMEM((rows, LATE * HEAD_FEATURES), f32)] * 2,
        in_specs=[vmem] * 3,
        out_specs=[vmem] * 2,
    )
    late = slice(LATE * HEAD_FEATURES, None)
    late_spread = jnp.repeat(share[:, LATE:HEAD_COUNT], HEAD_FEATURES, axis=1)
    late_base = extra_sum[:, late] + late_spread * own_sum[:, late]
    out = []
    first = 0
    for chunk, vr in zip(CHUNKS, other_vr):
        heads = range(first, first + chunk)
        args = [base, spread, late_base, late_spread, weights_a, weights_b, other_vm, vr]
        out = [
            call(
                functools.partial(finish_kernel, heads),
                "finish",
                *args, *out,
                out_shape=jax.ShapeDtypeStruct((rows, width), bf16),
                in_specs=[vmem] * len(args) + [anywhere] * len(out),
                out_specs=anywhere,
                input_output_aliases={len(args): 0} if out else {},
                scratch_shapes=[pltpu.VMEM((rows, chunk * HEAD_FEATURES), bf16), pltpu.SemaphoreType.DMA((chunk,))],
            )
        ]
        first += chunk
    return out[0]


def solution(mesh):
    placed = (
        P(("outer", "inner"), None),
        P(("outer", "inner"), None),
        P(("outer", "inner"), None),
        P(),
        P(),
    )
    return jax.shard_map(
        on_device,
        mesh=mesh,
        in_specs=placed,
        out_specs=P(("outer", "inner"), None),
        check_vma=False,
    )
```
